32 devices in a mesh: group: 4 (over y, core), mp: 8 (over z, x).
Axes of the slice: x: 2, y: 2, z: 4, core: 2. Of those that a mesh axis runs over, the one named last changes fastest.
Arguments:
- layer_in: float32 [256, 64, 768], P(('group', 'mp')), may hold values from -8 to 8
- cotangent: float32 [256, 64, 768], P(('group', 'mp')), may hold values from -6 to 6
- target: int32 [256], P(('group', 'mp')), may hold values from 0 to 3
- keep_mask: int32 [256], P(('group', 'mp')), may hold values from 0 to 1
- capacity: int32 [4], replicated, may hold values from 1 to 2, as said below
- attention_weights: float32 [4, 4, 768, 768], P('group', None, 'mp')
- feedforward_weights: float32 [4, 2, 768, 3072], P('group', None, 'mp')
- vectors: float32 [4, 12, 768], P('group', None, 'mp')
- row_moments: float32 [4, 6, 768], P('group', None, 'mp'), as said below
- column_moments: float32 [4, 9216], P('group'), as said below
- vector_moments: float32 [4, 12, 768], P('group', None, 'mp'), as said below
Outputs:
- layer_out: float32 [256, 64, 768], P(('group', 'mp'))
- input_grad: float32 [256, 64, 768], P(('group', 'mp'))
- attention_grad: float32 [4, 4, 768, 768], P('group', None, 'mp')
- feedforward_grad: float32 [4, 2, 768, 3072], P('group', None, 'mp')
- vectors_grad: float32 [4, 12, 768], P('group', None, 'mp')
- renewed_rows: float32 [4, 6, 768], P('group', None, 'mp')
- renewed_columns: float32 [4, 9216], P('group')
- renewed_vectors: float32 [4, 12, 768], P('group', None, 'mp')
- attention_updated: float32 [4, 4, 768, 768], P('group', None, 'mp')
- feedforward_updated: float32 [4, 2, 768, 3072], P('group', None, 'mp')
- vectors_updated: float32 [4, 12, 768], P('group', None, 'mp')
- update_scale: float32 [4, 18], P('group')
The draws below stay inside these ranges and needn't reach their ends.
Inputs may be any that keep to these rules, and one draw needn't show every extreme that they name: Some group has capacity 2, and every block of 8 sequences holds 2 or more sequences with keep_mask 1 whose target is a group of capacity 2. `row_moments`: positive. `column_moments`: positive. `vector_moments`: positive.
All inputs are finite; a program needn't handle non-finite values.
Results may differ from the reference program's by a relative error of at most 0.012.
The reference program's roundings to bfloat16 on the way count: a program that leaves them out, or rounds other values in their place, can miss the bound.
Values may be sent and summed in bfloat16 or wider, within the bound.
A program may use at most 192 MiB of HBM per device.

```python
import math
import jax
import jax.numpy as jnp
from jax import lax

D = 768
HEADS = 12
HEAD = 64
FF = 3072
SEQ = 64
SEQ_DEV = 8
SLOTS = 2
STEP = 10
GROUPS = 4
SEQS = 256
TOK_GROUP = 4096


def rising(start, finish, length):
    return jnp.exp(jnp.linspace(math.log(start), math.log(finish), length)).astype(jnp.float32)


def routing(key):
    devices = SEQS // SEQ_DEV
    pick_key, aim_key, order_key, flag_key, limit_key = jax.random.split(key, 5)
    hottest = jax.random.randint(pick_key, (), 0, GROUPS)
    aimed = jax.random.randint(aim_key, (devices, SEQ_DEV), 0, GROUPS)
    ranking = jax.random.randint(order_key, (devices, SEQ_DEV), 0, 1 << 20) * SEQ_DEV + jnp.arange(SEQ_DEV, dtype=jnp.int32)[None, :]
    placing = jnp.argsort(jnp.argsort(ranking, axis=1), axis=1)
    forced = placing < SLOTS
    aimed = jnp.where(forced, hottest, aimed)
    chance = (jax.random.randint(flag_key, (devices, SEQ_DEV), 0, 5) > 0).astype(jnp.int32)
    flagged = jnp.where(forced, 1, chance)
    limits = jax.random.randint(limit_key, (GROUPS,), 1, SLOTS + 1)
    limits = jnp.where(jnp.arange(GROUPS) == hottest, SLOTS, limits)
    return (aimed.reshape(-1).astype(jnp.int32), flagged.reshape(-1).astype(jnp.int32), limits.astype(jnp.int32))


def draw_target(key, part):
    aimed, flagged, limits = routing(key)
    return aimed


def draw_keep_mask(key, part):
    aimed, flagged, limits = routing(key)
    return flagged


def draw_capacity(key, part):
    aimed, flagged, limits = routing(key)
    return limits


def draw_layer_in(key, part):
    key = jax.random.fold_in(key, 1)
    sample = jax.random.normal(key, (SEQS, SEQ, D), jnp.float32) * rising(0.6, 1.8, D)
    return jnp.clip(sample, -8.0, 8.0)


def draw_attention_weights(key, part):
    key = jax.random.fold_in(key, 2)
    sample = jax.random.normal(key, (GROUPS, 4, D, D), jnp.float32) * D ** (-0.5)
    ones = jnp.ones((D,), jnp.float32)
    column_scale = jnp.stack([ones, ones, rising(0.6, 1.8, D), 3.0 * ones])
    return sample * column_scale[None, :, None, :]


def draw_feedforward_weights(key, part):
    key = jax.random.fold_in(key, 3)
    sample = jax.random.normal(key, (GROUPS, 2, D, FF), jnp.float32)
    matrix_scale = jnp.array([D ** (-0.5), FF ** (-0.5)], jnp.float32)
    return sample * matrix_scale[None, :, None, None]


def draw_vectors(key, part):
    key = jax.random.fold_in(key, 4)
    bias_key, gain_key = jax.random.split(key)
    biases = jax.random.normal(bias_key, (GROUPS, 12, D), jnp.float32) * 0.1
    gains = rising(0.6, 1.8, D)[None, None, :] * jax.random.uniform(gain_key, (GROUPS, 12, D), jnp.float32, 0.9, 1.1)
    row_ids = jnp.arange(12)
    is_gain = (row_ids == 3) | (row_ids == 6)
    return jnp.where(is_gain[None, :, None], gains, biases)


def draw_row_moments(key, part):
    key = jax.random.fold_in(key, 5)
    factor = jnp.exp(jax.random.uniform(key, (GROUPS, 6, D), jnp.float32, math.log(0.006), math.log(0.024)))
    profile = rising(200.0, 0.05, D)
    return TOK_GROUP * factor * profile[None, None, :] * rising(0.6, 1.8, D)[None, None, :] ** 2


def draw_column_moments(key, part):
    key = jax.random.fold_in(key, 6)
    factor = jnp.exp(jax.random.uniform(key, (GROUPS, 4 * D + 2 * FF), jnp.float32, math.log(0.003), math.log(0.03)))
    return TOK_GROUP * factor


def draw_vector_moments(key, part):
    key = jax.random.fold_in(key, 7)
    factor = jnp.exp(jax.random.uniform(key, (GROUPS, 12, D), jnp.float32, math.log(0.01), math.log(0.1)))
    return TOK_GROUP * factor


def block_scale(key, shape, cuts, smallest, high):
    gain, own = 1.0, jax.random.fold_in(key, 6)
    for dim, blocks in cuts:
        steps = jnp.exp(jax.random.uniform(jax.random.fold_in(own, dim), (blocks,), jnp.float32, smallest / len(cuts), high / len(cuts)))
        gain = gain * jnp.repeat(steps, shape[dim] // blocks).reshape([-1 if axis == dim else 1 for axis in range(len(shape))])
    return gain


def normal_values(key, extent, scale, most, pieces=(), kind=jnp.bfloat16):
    gain = block_scale(key, extent, pieces, -0.22, 0.18) if pieces else 1.0
    values = jax.random.normal(key, extent, jnp.float32) * scale * gain
    return jnp.minimum(jnp.maximum(values, -most), most).astype(kind)


def setup_inputs(seed: int = 0) -> dict:
    keys = jax.random.split(jax.random.key(seed), 12)
    layer_in = draw_layer_in(jax.random.fold_in(keys[11], 71), 0)
    cotangent = normal_values(keys[1], (SEQS, SEQ, D), 1.0, 6.0, ((0, 32),), jnp.float32)
    target = draw_target(jax.random.fold_in(keys[11], 71), 0)
    keep_mask = draw_keep_mask(jax.random.fold_in(keys[11], 71), 0)
    capacity = draw_capacity(jax.random.fold_in(keys[11], 71), 0)
    attention_weights = draw_attention_weights(jax.random.fold_in(keys[11], 71), 0)
    feedforward_weights = draw_feedforward_weights(jax.random.fold_in(keys[11], 71), 0)
    vectors = draw_vectors(jax.random.fold_in(keys[11], 71), 0)
    row_moments = draw_row_moments(jax.random.fold_in(keys[11], 71), 0)
    column_moments = draw_column_moments(jax.random.fold_in(keys[11], 71), 0)
    vector_moments = draw_vector_moments(jax.random.fold_in(keys[11], 71), 0)
    return dict(layer_in=layer_in, cotangent=cotangent, target=target, keep_mask=keep_mask, capacity=capacity, attention_weights=attention_weights, feedforward_weights=feedforward_weights, vectors=vectors, row_moments=row_moments, column_moments=column_moments, vector_moments=vector_moments)


@jax.custom_vjp
def low(v):
    return lax.optimization_barrier(v.astype(jnp.bfloat16)).astype(jnp.float32)

@jax.custom_vjp
def low_back(v):
    return v

def low_keep(v):
    return (low(v), None)

def low_pass(kept, grad):
    return (grad,)

def back_keep(v):
    return (v, None)

def back_low(kept, grad):
    return (low(grad),)
low.defvjp(low_keep, low_pass)
low_back.defvjp(back_keep, back_low)
epsilon = 1e-05
tiny_square = 1e-30
clip_level = 1.0
matrix_rate = 0.01
vector_rate = 0.1
highest = lax.Precision.HIGHEST

def rounded(tensor):
    return low(low_back(tensor))

def normalize(stream, gains, shifts):
    center = stream - lax.optimization_barrier(jnp.mean(stream, axis=-1, keepdims=True))
    spread = lax.optimization_barrier(jnp.mean(center * center, axis=-1, keepdims=True))
    return center * lax.rsqrt(spread + epsilon) * gains + shifts

def encoder(sequence, attention, feedforward, vector_rows):
    model_width = sequence.shape[-1]
    bias_query = vector_rows[0]
    bias_value = vector_rows[1]
    bias_output = vector_rows[2]
    gain_first = vector_rows[3]
    shift_first = vector_rows[4]
    bias_down = vector_rows[5]
    gain_second = vector_rows[6]
    shift_second = vector_rows[7]
    bias_up = vector_rows[8:12].reshape(-1)
    sequence_low = low(sequence)
    queries = rounded(jnp.dot(sequence_low, attention[0], precision=highest) + bias_query).reshape(SEQ, HEADS, HEAD)
    key_rows = rounded(jnp.dot(sequence_low, attention[1], precision=highest)).reshape(SEQ, HEADS, HEAD)
    values = rounded(jnp.dot(sequence_low, attention[2], precision=highest) + bias_value).reshape(SEQ, HEADS, HEAD)
    scores = low_back(jnp.einsum('she,the->hst', queries, key_rows, precision=highest) * HEAD ** (-0.5))
    largest = lax.optimization_barrier(jnp.max(scores, axis=-1, keepdims=True))
    shifted = jnp.exp(scores - largest)
    weights_low = low(shifted / lax.optimization_barrier(jnp.sum(shifted, axis=-1, keepdims=True)))
    attended = rounded(jnp.einsum('hst,the->she', weights_low, values, precision=highest).reshape(SEQ, model_width))
    branch = low_back(jnp.dot(attended, attention[3], precision=highest) + bias_output)
    first_norm = normalize(sequence + branch, gain_first, shift_first)
    before_act = low_back(jnp.dot(low(first_norm), feedforward[0], precision=highest) + bias_up)
    activated = low(jax.nn.gelu(before_act, approximate=False))
    down_branch = low_back(jnp.dot(activated, feedforward[1].T, precision=highest) + bias_down)
    return normalize(first_norm + down_branch, gain_second, shift_second)

def reference(layer_in, cotangent, target, keep_mask, capacity, attention_weights, feedforward_weights, vectors, row_moments, column_moments, vector_moments):
    device_count = target.shape[0] // SEQ_DEV
    block_rows = target.reshape(device_count, SEQ_DEV)
    flag_rows = keep_mask.reshape(device_count, SEQ_DEV)
    group_ids = jnp.arange(GROUPS, dtype=jnp.int32)
    aimed_at = (block_rows[:, :, None] == group_ids[None, None, :]).astype(jnp.int32)
    wanted = aimed_at * flag_rows[:, :, None]
    earlier = jnp.cumsum(wanted, axis=1) - wanted
    position = lax.optimization_barrier(jnp.sum(earlier * aimed_at, axis=-1))
    allowed = lax.optimization_barrier(jnp.sum(aimed_at * capacity[None, None, :], axis=-1))
    admitted = ((flag_rows == 1) & (position < allowed)).reshape(-1)

    def forward(inputs, attention, feedforward, vector_all):
        attention_low = low(attention)
        feedforward_low = low(feedforward)
        vectors_low = low(vector_all)

        def one_sequence(carried, element):
            sequence, owner_id, is_taken = element
            result = encoder(sequence, attention_low[owner_id], feedforward_low[owner_id], vectors_low[owner_id])
            return (carried, jnp.where(is_taken, result, sequence))
        unused, outputs = lax.scan(jax.checkpoint(one_sequence), jnp.zeros((), jnp.float32), (inputs, target, admitted))
        return outputs
    layer_out, pullback = jax.vjp(forward, layer_in, attention_weights, feedforward_weights, vectors)
    input_grad, attention_grad, feedforward_grad, vectors_grad = pullback(cotangent)
    decay_rate = 1.0 - STEP ** (-0.8)
    keep_rate = 1.0 - decay_rate
    square_attention = attention_grad * attention_grad + tiny_square
    square_feedforward = feedforward_grad * feedforward_grad + tiny_square
    square_vectors = vectors_grad * vectors_grad + tiny_square
    rows_attention = decay_rate * row_moments[:, :4] + keep_rate * lax.optimization_barrier(jnp.mean(square_attention, axis=-1))
    rows_feedforward = decay_rate * row_moments[:, 4:] + keep_rate * lax.optimization_barrier(jnp.mean(square_feedforward, axis=-1))
    old_attention = column_moments[:, :4 * D].reshape(GROUPS, 4, D)
    old_feedforward = column_moments[:, 4 * D:].reshape(GROUPS, 2, FF)
    columns_attention = decay_rate * old_attention + keep_rate * lax.optimization_barrier(jnp.mean(square_attention, axis=-2))
    columns_feedforward = decay_rate * old_feedforward + keep_rate * lax.optimization_barrier(jnp.mean(square_feedforward, axis=-2))
    step_attention = attention_grad / jnp.sqrt(rows_attention[..., :, None] * columns_attention[..., None, :] / lax.optimization_barrier(jnp.mean(rows_attention, axis=-1))[..., None, None])
    step_feedforward = feedforward_grad / jnp.sqrt(rows_feedforward[..., :, None] * columns_feedforward[..., None, :] / lax.optimization_barrier(jnp.mean(rows_feedforward, axis=-1))[..., None, None])
    scale_attention = jnp.sqrt(lax.optimization_barrier(jnp.mean(step_attention * step_attention, axis=(-2, -1))))
    scale_feedforward = jnp.sqrt(lax.optimization_barrier(jnp.mean(step_feedforward * step_feedforward, axis=(-2, -1))))
    attention_updated = attention_weights - matrix_rate * step_attention / jnp.maximum(1.0, scale_attention / clip_level)[..., None, None]
    feedforward_updated = feedforward_weights - matrix_rate * step_feedforward / jnp.maximum(1.0, scale_feedforward / clip_level)[..., None, None]
    renewed_vectors = decay_rate * vector_moments + keep_rate * square_vectors
    step_vectors = vectors_grad / jnp.sqrt(renewed_vectors)
    scale_vectors = jnp.sqrt(lax.optimization_barrier(jnp.mean(step_vectors * step_vectors, axis=-1)))
    vectors_updated = vectors - vector_rate * step_vectors / jnp.maximum(1.0, scale_vectors / clip_level)[..., None]
    renewed_rows = jnp.concatenate([rows_attention, rows_feedforward], axis=1)
    renewed_columns = jnp.concatenate([columns_attention.reshape(GROUPS, 4 * D), columns_feedforward.reshape(GROUPS, 2 * FF)], axis=1)
    update_scale = jnp.concatenate([scale_attention, scale_feedforward, scale_vectors], axis=1)
    return (layer_out, input_grad, attention_grad, feedforward_grad, vectors_grad, renewed_rows, renewed_columns, renewed_vectors, attention_updated, feedforward_updated, vectors_updated, update_scale)
```

```python
import functools
import types

import jax
import jax.numpy as jnp
from jax import lax
from jax.experimental import pallas as pl
from jax.experimental.pallas import tpu as pltpu
from jax.sharding import PartitionSpec as P

HEADS = 12
SLOTS = 2
STEP = 10


epsilon = 1e-05
tiny_square = 1e-30
clip_level = 1.0
matrix_rate = 0.01
vector_rate = 0.1


def normalize(stream, gains, shifts):
    center = stream - jnp.mean(stream, axis=-1, keepdims=True)
    inverse = lax.rsqrt(jnp.mean(center * center, axis=-1, keepdims=True) + epsilon)
    normed = center * inverse
    return (normed * gains + shifts, normed, inverse)


def normalize_back(upstream, gains, normed, inverse):
    scaled = upstream * gains
    return inverse * (
        scaled
        - jnp.mean(scaled, axis=-1, keepdims=True)
        - normed * jnp.mean(scaled * normed, axis=-1, keepdims=True)
    )


def gelu_exact(tensor):
    return jax.nn.gelu(tensor, approximate=False)


def generic_body(
    layer_in,
    cotangent,
    target,
    keep_mask,
    capacity,
    attention_weights,
    feedforward_weights,
    vectors,
    row_moments,
    column_moments,
    vector_moments,
):
    group_count = lax.axis_size("group")
    local_count = layer_in.shape[0]
    seq_len = layer_in.shape[1]
    model_width = layer_in.shape[2]
    head_dim = model_width // HEADS
    hidden = feedforward_weights.shape[3]
    slot_count = SLOTS
    buffered = group_count * slot_count
    row_total = buffered * seq_len
    score_scale = head_dim ** (-0.5)
    group_ids = jnp.arange(group_count, dtype=jnp.int32)
    aimed_at = (target[:, None] == group_ids[None, :]).astype(jnp.int32)
    wanted = aimed_at * keep_mask[:, None]
    earlier = jnp.cumsum(wanted, axis=0) - wanted
    position = jnp.sum(earlier * aimed_at, axis=1)
    allowed = jnp.sum(aimed_at * capacity[None, :], axis=1)
    admitted = (keep_mask == 1) & (position < allowed)
    placed = target * slot_count + position
    cell_ids = jnp.arange(buffered, dtype=jnp.int32)
    matched = admitted[:, None] & (placed[:, None] == cell_ids[None, :])
    local_ids = jnp.arange(local_count, dtype=jnp.int32)
    source = jnp.sum(jnp.where(matched, local_ids[:, None], 0), axis=0) + jnp.where(
        jnp.any(matched, axis=0), 0, local_count
    )
    blank_row = jnp.zeros((1, seq_len, model_width), jnp.float32)
    send_inputs = jnp.take(jnp.concatenate([layer_in, blank_row], axis=0), source, axis=0).reshape(
        group_count, slot_count, seq_len, model_width
    )
    send_grads = jnp.take(jnp.concatenate([cotangent, blank_row], axis=0), source, axis=0).reshape(
        group_count, slot_count, seq_len, model_width
    )
    got_inputs, got_grads = (
        lax.all_to_all(send_inputs, "group", split_axis=0, concat_axis=0, tiled=True),
        lax.all_to_all(send_grads, "group", split_axis=0, concat_axis=0, tiled=True),
    )
    attention_full, feedforward_full, vectors_full = (
        lax.all_gather(attention_weights[0].astype(jnp.bfloat16), "mp", axis=1, tiled=True),
        lax.all_gather(feedforward_weights[0].astype(jnp.bfloat16), "mp", axis=1, tiled=True),
        lax.all_gather(vectors[0].astype(jnp.bfloat16), "mp", axis=1, tiled=True),
    )
    vector_rows = vectors_full.astype(jnp.float32)
    bias_query = vector_rows[0]
    bias_value = vector_rows[1]
    bias_output = vector_rows[2]
    gain_first = vector_rows[3]
    shift_first = vector_rows[4]
    bias_down = vector_rows[5]
    gain_second = vector_rows[6]
    shift_second = vector_rows[7]
    bias_up = vector_rows[8:12].reshape(-1)
    inputs = got_inputs.reshape(row_total, model_width)
    inputs_low = inputs.astype(jnp.bfloat16)
    projected = jnp.einsum(
        "rd,cde->cre", inputs_low, attention_full[:3], preferred_element_type=jnp.float32
    )
    projection_bias = jnp.stack([bias_query, jnp.zeros_like(bias_query), bias_value])
    projected_low = (projected + projection_bias[:, None, :]).astype(jnp.bfloat16)
    queries = projected_low[0].reshape(buffered, seq_len, HEADS, head_dim)
    key_rows = projected_low[1].reshape(buffered, seq_len, HEADS, head_dim)
    values = projected_low[2].reshape(buffered, seq_len, HEADS, head_dim)
    scores = (
        jnp.einsum("nshe,nthe->nhst", queries, key_rows, preferred_element_type=jnp.float32)
        * score_scale
    )
    largest = jnp.max(scores, axis=-1, keepdims=True)
    shifted = jnp.exp(scores - largest)
    totals = jnp.sum(shifted, axis=-1, keepdims=True)
    log_totals = largest + jnp.log(totals)
    weights_low = (shifted / totals).astype(jnp.bfloat16)
    attended = jnp.einsum(
        "nhst,nthe->nshe", weights_low, values, preferred_element_type=jnp.float32
    )
    attended_low = attended.reshape(row_total, model_width).astype(jnp.bfloat16)
    branch = (
        jnp.dot(attended_low, attention_full[3], preferred_element_type=jnp.float32) + bias_output
    )
    first_norm, normed_first, inverse_first = normalize(inputs + branch, gain_first, shift_first)
    first_low = first_norm.astype(jnp.bfloat16)
    before_act = (
        jnp.dot(first_low, feedforward_full[0], preferred_element_type=jnp.float32) + bias_up
    )
    activated = gelu_exact(before_act).astype(jnp.bfloat16)
    down_branch = (
        jnp.einsum("rf,df->rd", activated, feedforward_full[1], preferred_element_type=jnp.float32)
        + bias_down
    )
    output_rows, normed_second, inverse_second = normalize(
        first_norm + down_branch, gain_second, shift_second
    )
    returned = lax.all_to_all(
        output_rows.reshape(group_count, slot_count, seq_len, model_width),
        "group",
        split_axis=0,
        concat_axis=0,
        tiled=True,
    )
    upstream = got_grads.reshape(row_total, model_width)
    grad_gain_second = jnp.sum(upstream * normed_second, axis=0)
    grad_shift_second = jnp.sum(upstream, axis=0)
    grad_second = normalize_back(upstream, gain_second, normed_second, inverse_second)
    grad_down = grad_second.astype(jnp.bfloat16)
    grad_bias_down = jnp.sum(grad_down.astype(jnp.float32), axis=0)
    grad_w_down = jnp.einsum("rd,rf->df", grad_down, activated, preferred_element_type=jnp.float32)
    grad_activated = jnp.dot(grad_down, feedforward_full[1], preferred_element_type=jnp.float32)
    gelu_pull = jax.vjp(gelu_exact, before_act)[1]
    grad_before = gelu_pull(grad_activated)[0].astype(jnp.bfloat16)
    grad_bias_up = jnp.sum(grad_before.astype(jnp.float32), axis=0)
    grad_w_up = jnp.einsum("rd,rf->df", first_low, grad_before, preferred_element_type=jnp.float32)
    grad_first = grad_second + jnp.einsum(
        "rf,df->rd", grad_before, feedforward_full[0], preferred_element_type=jnp.float32
    )
    feedforward_grads = jnp.stack([grad_w_up, grad_w_down])
    grad_gain_first = jnp.sum(grad_first * normed_first, axis=0)
    grad_shift_first = jnp.sum(grad_first, axis=0)
    grad_residual = normalize_back(grad_first, gain_first, normed_first, inverse_first)
    grad_branch = grad_residual.astype(jnp.bfloat16)
    grad_bias_output = jnp.sum(grad_branch.astype(jnp.float32), axis=0)
    grad_w_output = jnp.einsum(
        "rd,re->de", attended_low, grad_branch, preferred_element_type=jnp.float32
    )
    grad_attended = jnp.einsum(
        "re,de->rd", grad_branch, attention_full[3], preferred_element_type=jnp.float32
    )
    grad_heads = grad_attended.astype(jnp.bfloat16).reshape(buffered, seq_len, HEADS, head_dim)
    again = (
        jnp.einsum("nshe,nthe->nhst", queries, key_rows, preferred_element_type=jnp.float32)
        * score_scale
    )
    exact = jnp.exp(again - log_totals)
    grad_values = jnp.einsum(
        "nhst,nshe->nthe",
        exact.astype(jnp.bfloat16),
        grad_heads,
        preferred_element_type=jnp.float32,
    ).astype(jnp.bfloat16)
    grad_weights = jnp.einsum(
        "nshe,nthe->nhst", grad_heads, values, preferred_element_type=jnp.float32
    )
    grad_scores = (
        exact * (grad_weights - jnp.sum(grad_weights * exact, axis=-1, keepdims=True))
    ).astype(jnp.bfloat16)
    grad_queries = (
        jnp.einsum("nhst,nthe->nshe", grad_scores, key_rows, preferred_element_type=jnp.float32)
        * score_scale
    ).astype(jnp.bfloat16)
    grad_keys = (
        jnp.einsum("nhst,nshe->nthe", grad_scores, queries, preferred_element_type=jnp.float32)
        * score_scale
    ).astype(jnp.bfloat16)
    grad_projected = jnp.stack(
        [
            grad_queries.reshape(row_total, model_width),
            grad_keys.reshape(row_total, model_width),
            grad_values.reshape(row_total, model_width),
        ]
    )
    grad_w_projected = jnp.einsum(
        "rd,cre->cde", inputs_low, grad_projected, preferred_element_type=jnp.float32
    )
    grad_inputs = grad_residual + jnp.einsum(
        "cre,cde->rd", grad_projected, attention_full[:3], preferred_element_type=jnp.float32
    )
    grad_bias_projected = jnp.sum(grad_projected.astype(jnp.float32), axis=1)
    grads_back = lax.all_to_all(
        grad_inputs.reshape(group_count, slot_count, seq_len, model_width),
        "group",
        split_axis=0,
        concat_axis=0,
        tiled=True,
    )
    attention_grads = jnp.concatenate([grad_w_projected, grad_w_output[None]], axis=0)
    vector_grads = jnp.concatenate(
        [
            jnp.stack(
                [
                    grad_bias_projected[0],
                    grad_bias_projected[2],
                    grad_bias_output,
                    grad_gain_first,
                    grad_shift_first,
                    grad_bias_down,
                    grad_gain_second,
                    grad_shift_second,
                ]
            ),
            grad_bias_up.reshape(4, model_width),
        ],
        axis=0,
    )
    attention_part, feedforward_part, vectors_part = (
        lax.psum_scatter(attention_grads, "mp", scatter_dimension=1, tiled=True),
        lax.psum_scatter(feedforward_grads, "mp", scatter_dimension=1, tiled=True),
        lax.psum_scatter(vector_grads, "mp", scatter_dimension=1, tiled=True),
    )
    slot_index = jnp.where(admitted, placed, 0)
    layer_out = jnp.where(
        admitted[:, None, None],
        jnp.take(returned.reshape(buffered, seq_len, model_width), slot_index, axis=0),
        layer_in,
    )
    input_grad = jnp.where(
        admitted[:, None, None],
        jnp.take(grads_back.reshape(buffered, seq_len, model_width), slot_index, axis=0),
        cotangent,
    )
    decay_rate = 1.0 - STEP ** (-0.8)
    keep_rate = 1.0 - decay_rate
    square_attention = attention_part * attention_part + tiny_square
    square_feedforward = feedforward_part * feedforward_part + tiny_square
    square_vectors = vectors_part * vectors_part + tiny_square
    rows_attention = decay_rate * row_moments[0, :4] + keep_rate * jnp.mean(
        square_attention, axis=-1
    )
    rows_feedforward = decay_rate * row_moments[0, 4:] + keep_rate * jnp.mean(
        square_feedforward, axis=-1
    )
    renewed_vectors = decay_rate * vector_moments[0] + keep_rate * square_vectors
    step_vectors = vectors_part / jnp.sqrt(renewed_vectors)
    vector_squares = jnp.sum(step_vectors * step_vectors, axis=-1)
    attention_columns = jnp.sum(square_attention, axis=1)
    feedforward_columns = jnp.sum(square_feedforward, axis=1)
    row_sums = jnp.concatenate(
        [jnp.sum(rows_attention, axis=-1), jnp.sum(rows_feedforward, axis=-1)]
    )
    old_attention = column_moments[0, : 4 * model_width].reshape(4, model_width)
    old_feedforward = column_moments[0, 4 * model_width :].reshape(2, hidden)
    attention_sums, feedforward_sums, rows_summed, vector_total = lax.psum(
        (attention_columns, feedforward_columns, row_sums, vector_squares), "mp"
    )
    columns_attention = decay_rate * old_attention + keep_rate * attention_sums / model_width
    columns_feedforward = decay_rate * old_feedforward + keep_rate * feedforward_sums / model_width
    mean_rows = rows_summed / model_width
    step_attention = attention_part / jnp.sqrt(
        rows_attention[:, :, None] * columns_attention[:, None, :] / mean_rows[:4, None, None]
    )
    step_feedforward = feedforward_part / jnp.sqrt(
        rows_feedforward[:, :, None] * columns_feedforward[:, None, :] / mean_rows[4:, None, None]
    )
    attention_total, feedforward_total = lax.psum(
        (
            jnp.sum(step_attention * step_attention, axis=(1, 2)),
            jnp.sum(step_feedforward * step_feedforward, axis=(1, 2)),
        ),
        "mp",
    )
    scale_attention = jnp.sqrt(attention_total / (model_width * model_width))
    scale_feedforward = jnp.sqrt(feedforward_total / (model_width * hidden))
    scale_vectors = jnp.sqrt(vector_total / model_width)
    attention_updated = (
        attention_weights[0]
        - matrix_rate
        * step_attention
        / jnp.maximum(1.0, scale_attention / clip_level)[:, None, None]
    )
    feedforward_updated = (
        feedforward_weights[0]
        - matrix_rate
        * step_feedforward
        / jnp.maximum(1.0, scale_feedforward / clip_level)[:, None, None]
    )
    vectors_updated = (
        vectors[0]
        - vector_rate * step_vectors / jnp.maximum(1.0, scale_vectors / clip_level)[:, None]
    )
    renewed_rows = jnp.concatenate([rows_attention, rows_feedforward], axis=0)
    renewed_columns = jnp.concatenate(
        [columns_attention.reshape(-1), columns_feedforward.reshape(-1)]
    )
    update_scale = jnp.concatenate([scale_attention, scale_feedforward, scale_vectors])
    return (
        layer_out,
        input_grad,
        attention_part[None],
        feedforward_part[None],
        vectors_part[None],
        renewed_rows[None],
        renewed_columns[None],
        renewed_vectors[None],
        attention_updated[None],
        feedforward_updated[None],
        vectors_updated[None],
        update_scale[None],
    )


MESH = pl.DeviceIdType.MESH
ANY = pl.BlockSpec(memory_space=pl.ANY)
VMEM = pl.BlockSpec(memory_space=pltpu.VMEM)
SMEM = pl.BlockSpec(memory_space=pltpu.SMEM)
LANES = 128
PEERS = 8
LIMIT = 63 * 1024 * 1024
D = 768
FF = 3072
QKV = 3 * D
VEC = QKV + D
WIDE = VEC + LANES
SEQ = 64
TOKENS = 512
HEAD = D // HEADS
DECAY = 1.0 - STEP ** (-0.8)
KEEP = 1.0 - DECAY


class Spot:
    def __init__(self):
        g = lax.axis_index("group")
        m = lax.axis_index("mp")
        y, c = lax.div(g, 2), lax.rem(g, 2)
        z, x = lax.div(m, 2), lax.rem(m, 2)
        h, zl = lax.div(z, 2), lax.rem(z, 2)
        self.g, self.m, self.y, self.c, self.x, self.h, self.zl = g, m, y, c, x, h, zl
        self.home = c == h
        self.k = y * 2 + h
        self.r = c * 4 + zl * 2 + x
        self.across_x = (g, m + 1 - 2 * x)
        self.across_z = (g, m + 2 - 4 * zl)
        self.across_core = (g + 1 - 2 * c, m)
        self.partner = (y * 2 + 1 - c, ((1 - h) * 2 + zl) * 2 + x)

    def shard(self, dc=0, dz=0, dx=0):
        c = 1 - self.c if dc else self.c
        zl = 1 - self.zl if dz else self.zl
        x = 1 - self.x if dx else self.x
        return c * 4 + zl * 2 + x

    def router(self, n):
        y = 1 - self.y if n % 2 else self.y
        h = 1 - self.h if n // 2 else self.h
        return (y * 2 + self.c, (h * 2 + self.zl) * 2 + self.x), y * 2 + h

    def peer(self, step):
        m = lax.rem(self.m + step, PEERS)
        return (self.g, m), m


def rows(index, count):
    if isinstance(index, int):
        return pl.ds(index * count, count)
    return pl.ds(pl.multiple_of(index * count, count), count)


def remote(src, dst, send, recv, device):
    return pltpu.make_async_remote_copy(
        src_ref=src,
        dst_ref=dst,
        send_sem=send,
        recv_sem=recv,
        device_id=device,
        device_id_type=MESH,
    )


def greet(devices):
    barrier = pltpu.get_barrier_semaphore()
    for device in devices:
        pl.semaphore_signal(barrier, inc=1, device_id=device, device_id_type=MESH)
    pl.semaphore_wait(barrier, len(devices))


def dot(a, b):
    return jnp.dot(a, b, preferred_element_type=jnp.float32)


def dot_t(a, b):
    return lax.dot_general(a, b, (((1,), (1,)), ((), ())), preferred_element_type=jnp.float32)


def t_dot(a, b):
    return lax.dot_general(a, b, (((0,), (0,)), ((), ())), preferred_element_type=jnp.float32)


def loop(count, step, unroll=1):
    def turn(i, carry):
        for n in range(unroll):
            step(i * unroll + n)
        return carry

    if count == unroll:
        turn(0, 0)
    else:
        lax.fori_loop(0, count // unroll, turn, 0)


def mean_of(value):
    return jnp.sum(value, axis=-1, keepdims=True) * (1.0 / D)


def sum_rows(value):
    return jnp.sum(value, axis=0, keepdims=True)


def placing(target, keep_mask, capacity):
    count, groups = target.shape[0], capacity.shape[0]
    aims = [target[s] for s in range(count)]
    flags = [keep_mask[s] for s in range(count)]
    limits = [capacity[k] for k in range(groups)]
    placed = []
    for s in range(count):
        rank = jnp.int32(0)
        for before in range(s):
            rank = rank + flags[before] * (aims[before] == aims[s]).astype(jnp.int32)
        placed.append(
            [
                (
                    flags[s]
                    * (aims[s] == k).astype(jnp.int32)
                    * (rank == n).astype(jnp.int32)
                    * (rank < limits[k]).astype(jnp.int32)
                ).astype(jnp.float32)
                for k in range(groups)
                for n in range(SLOTS)
            ]
        )
    return placed


class Heads:
    def __init__(self):
        row = lax.broadcasted_iota(jnp.int32, (2 * LANES, LANES), 0)
        col = lax.broadcasted_iota(jnp.int32, (2 * LANES, LANES), 1)
        self.same = lax.rem(lax.div(row, SEQ), 2) == lax.div(col, SEQ)
        self.first = col[:LANES] < HEAD
        lane = lax.broadcasted_iota(jnp.int32, (1, LANES), 1)
        self.masks = [
            (lane < HEAD).astype(jnp.float32).astype(jnp.bfloat16),
            (lane >= HEAD).astype(jnp.float32).astype(jnp.bfloat16),
        ]

    def stack(self, pair):
        return jnp.concatenate([pair * mask for mask in self.masks], axis=0)

    def join(self, both):
        return jnp.where(self.first, both[:LANES], both[LANES:]).astype(jnp.bfloat16)

    def weigh(self, q, k):
        scores = jnp.where(self.same, dot_t(q, k) * HEAD ** (-0.5), -3.0e38)
        largest = jnp.max(scores, axis=-1, keepdims=True)
        shifted = jnp.exp(scores - largest)
        return shifted / jnp.sum(shifted, axis=-1, keepdims=True)


CHUNK = 512
CHUNKS = FF // CHUNK
PAIR = 2 * CHUNK
BASE = CHUNKS * PAIR
SPANS = tuple((i * PAIR, PAIR) for i in range(CHUNKS)) + (
    (BASE, D),
    (BASE + D, D),
    (BASE + 2 * D, D),
    (BASE + 3 * D, D + LANES),
)
OUT_PIECE, QUERY_PIECE, KEY_PIECE, VALUE_PIECE = range(CHUNKS, CHUNKS + 4)
PIECES = CHUNKS + 4
Z_FIRST = (0,)
RING = 2
HALF = 384
SHARD_AT = 2 * LANES
STAT_F = 4 * FF + 2 * LANES
STAT_A = 8 * D + 2 * LANES
ATTENTION_AT = (BASE + D, BASE + 2 * D, BASE + 3 * D, BASE)


def forward_phase(spot, r):
    low, full = jnp.bfloat16, jnp.float32
    count = r.diag.shape[0]
    group_count = r.capacity.shape[0]
    target, keep_mask, capacity, vectors = r.target, r.keep_mask, r.capacity, r.vectors
    fa, f1, f2, xt, ot, ht, dft, qkv, g, gp = r.fa, r.f1, r.f2, r.xt, r.ot, r.ht, r.dft, r.qkv, r.g, r.gp
    n1, inv, dr, df, vt, vg, x, dy, o, h1, hb = r.n1, r.inv, r.dr, r.df, r.vt, r.vg, r.x, r.dy, r.o, r.h1, r.hb
    qb, bu, square, acc, total = r.qb, r.bu, r.square, r.acc, r.total
    swap_s, swap_r, x_s, x_r, z_s, z_r, d_s, d_r = r.swap_s, r.swap_r, r.x_s, r.x_r, r.z_s, r.z_r, r.d_s, r.d_r
    c_s, c_r, t_s, t_r, own_sem, keep_sem, load_sem = r.c_s, r.c_r, r.t_s, r.t_r, r.own_sem, r.keep_sem, r.load_sem

    def raw(block):
        return (n1, dr, h1)[block // 5].at[pl.ds(block % 5 * count, count)]

    def load_weights(block):
        src = r.wa.at[block] if block < 4 else r.wf.at[block // 4 - 1, :, pl.ds(block % 4 * D, D)]
        return pltpu.make_async_copy(src, raw(block), load_sem.at[block])

    def load_tokens(src, s):
        return pltpu.make_async_copy(
            src.at[pl.ds(s * SEQ, SEQ)], total.at[pl.ds(0, SEQ), pl.ds(s * D, D)], load_sem.at[12 + s]
        )

    for block in range(4):
        load_weights(block).start()
    for s in range(target.shape[0]):
        load_tokens(r.layer_in, s).start()
    for block in range(4, 12):
        load_weights(block).start()
    square[...] = jnp.zeros(square.shape, full)
    for row in range(12):
        square[row : row + 1, pl.ds(0, count)] = vectors[row]
    acc[pl.ds(SHARD_AT, count), pl.ds(VEC, LANES)] = square[...].T[:count].astype(low)
    placed = placing(target, keep_mask, capacity)
    r.greet()
    firsts, widths, fulls = (0, WIDE, WIDE + FF), (WIDE, FF, FF), (fa, f1, f2)
    shards = [acc.at[pl.ds(SHARD_AT, count), pl.ds(*span)] for span in zip(firsts, widths)]
    pieces = range(3)
    away = jnp.logical_not(spot.home)

    def swap(p):
        return remote(
            shards[p], fulls[p].at[rows(spot.m, count)], swap_s.at[p], swap_r.at[p], spot.partner
        )

    def keep(p):
        return pltpu.make_async_copy(shards[p], fulls[p].at[rows(spot.r, count)], own_sem.at[p])

    def hop(p, shard, send, recv, device):
        view = fulls[p].at[rows(shard, count)]
        return remote(view, view, send, recv, device)

    def over_x(p, shard):
        return hop(p, shard, x_s.at[p], x_r.at[p], spot.across_x)

    def over_z(p, shard):
        return hop(p, shard, z_s.at[p], z_r.at[p], spot.across_z)

    def diagonal(p, shard):
        return hop(p, shard, d_s.at[p], d_r.at[p], spot.across_x)

    def over_core(p, n, shard):
        return hop(p, shard, c_s.at[p, n], c_r.at[p, n], spot.across_core)

    routed = (x, dy)

    def token(a, n):
        device, k = spot.router(n)
        return remote(
            acc.at[pl.ds(a * LANES, LANES), rows(k, D)],
            routed[a].at[pl.ds(n * LANES, LANES)],
            t_s.at[a, n],
            t_r.at[a, n],
            device,
        )

    def token_keep(a):
        return pltpu.make_async_copy(
            acc.at[pl.ds(a * LANES, LANES), rows(spot.k, D)],
            routed[a].at[pl.ds(0, LANES)],
            keep_sem.at[a],
        )

    mine = spot.r
    by_x, by_z, by_both = spot.shard(dx=1), spot.shard(dz=1), spot.shard(dz=1, dx=1)

    def lead(p):
        over_x(p, mine).start()
        over_z(p, mine).start()
        over_core(p, 0, mine).start()

    def lead_home(p):
        keep(p).wait()
        lead(p)

    def lead_away(p):
        hop(p, mine, swap_s.at[p], swap_r.at[p], spot.partner).wait_recv()
        lead(p)

    def relay(p):
        over_z(p, by_z).wait_recv()
        diagonal(p, by_z).start()
        over_core(p, 2, by_z).start()
        over_x(p, by_x).wait_recv()
        over_core(p, 1, by_x).start()

    def finish(p):
        diagonal(p, by_both).wait_recv()
        over_core(p, 3, by_both).start()

    def collect_first(p):
        over_core(p, 0, spot.shard(dc=1)).wait_recv()

    def collect_rest(p):
        over_core(p, 1, spot.shard(dc=1, dx=1)).wait_recv()
        over_core(p, 2, spot.shard(dc=1, dz=1)).wait_recv()
        over_core(p, 3, spot.shard(dc=1, dz=1, dx=1)).wait_recv()

    def cast(p, block):
        load_weights(block).wait()
        at = firsts[p] + block % 4 * D
        acc[pl.ds(SHARD_AT, count), pl.ds(at, D)] = raw(block)[...].astype(low)

    for block in range(4):
        cast(0, block)

    @pl.when(away)
    def _():
        swap(0).start()

    @pl.when(spot.home)
    def _():
        keep(0).start()

    for p in (1, 2):
        for j in range(4):
            cast(p, p * 4 + j)

        @pl.when(spot.home)
        def _():
            lead_home(p - 1)
            keep(p).start()

    @pl.when(spot.home)
    def _():
        lead_home(2)

    def choose(a):
        def part(n):
            parts = [total[rows(n, 16), pl.ds(s * D, D)] for s in range(len(placed))]
            for slot in range(2 * group_count):
                value = sum(places[slot] * one for places, one in zip(placed, parts))
                at = pl.multiple_of(a * LANES + slot % 2 * SEQ + n * 16, 16)
                acc[pl.ds(at, 16), pl.ds(slot // 2 * D, D)] = value.astype(low)

        loop(SEQ // 16, part)

    for s in range(target.shape[0]):
        load_tokens(r.layer_in, s).wait()
    choose(0)
    for s in range(target.shape[0]):
        load_tokens(r.cotangent, s).start()
    token_keep(0).start()
    token(0, 1).start()

    @pl.when(away)
    def _():
        lead_away(0)
        swap(1).start()

    @pl.when(spot.home)
    def _():
        relay(0)
        finish(0)

    collect_first(0)
    token(0, 2).start()
    token(0, 3).start()
    for s in range(target.shape[0]):
        load_tokens(r.cotangent, s).wait()
    choose(1)
    square[...] = jnp.zeros(square.shape, full)
    for n, part in enumerate((vectors, r.vector_moments, r.row_moments)):
        for row in range(part.shape[0]):
            square[row : row + 1, pl.ds(0, count)] = part[row]
        r.small[n] = square[...].T[:count]

    @pl.when(away)
    def _():
        relay(0)
        finish(0)

    @pl.when(spot.home)
    def _():
        relay(1)
        finish(1)

    def turn(src, dst, i):
        block = rows(i, LANES)
        turned = src[block, :].T
        dst[rows(1 - spot.c, HALF), block] = turned[:HALF]
        dst[rows(spot.c, HALF), block] = turned[HALF:]

    token_keep(0).wait()
    token(0, 1).wait_recv()
    turn(x, xt, 0)
    turn(x, xt, 1)
    collect_rest(0)
    vt[...] = fa[:, pl.ds(VEC, LANES)].astype(full).T[:16]
    qb[:, pl.ds(0, D)] = vt[0:1]
    qb[:, pl.ds(D, D)] = jnp.zeros((1, D), full)
    qb[:, pl.ds(2 * D, D)] = vt[1:2]
    for i in range(4):
        bu[:, pl.ds(i * D, D)] = vt[8 + i : 9 + i]

    def project(first, j):
        cols = rows(j, 256)
        at = pl.ds(first, 256)
        qkv[at, cols] = (dot(x[at, :], fa[:, cols]) + qb[:, cols]).astype(low)

    heads = Heads()

    def attend(block, j):
        at = pl.ds(block * LANES, LANES)
        q = qkv[at, rows(j, LANES)]
        k = qkv[at, rows(j + 6, LANES)]
        v = qkv[at, rows(j + 12, LANES)]
        weights = heads.weigh(heads.stack(q), k).astype(low)
        o[at, rows(j, LANES)] = heads.join(dot(weights, v))

    def attend_block(block):
        def part(n):
            for j in range(3):
                attend(block, n * 3 + j)

        loop(2, part)

    loop(QKV // 256, functools.partial(project, 0), 3)

    @pl.when(spot.home)
    def _():
        relay(2)

    attend_block(0)
    attend_block(1)

    @pl.when(spot.home)
    def _():
        finish(2)

    token(0, 2).wait_recv()
    token(0, 3).wait_recv()
    loop(QKV // 256, functools.partial(project, 256), 3)

    @pl.when(away)
    def _():
        lead_away(1)
        swap(2).start()

    attend_block(2)
    attend_block(3)

    @pl.when(away)
    def _():
        relay(1)

    def attention_out(j):
        h1[:, rows(j, 256)] = dot(o[...], fa[:, pl.ds(QKV + j * 256, 256)])

    loop(D // 256, attention_out, 3)

    def first_norm(i):
        for n in range(2):
            at = pl.ds(pl.multiple_of(i * 64 + n * 32, 32), 32)
            stream = x[at, :].astype(full) + (h1[at, :] + vt[2:3])
            center = stream - mean_of(stream)
            inverse = lax.rsqrt(mean_of(center * center) + epsilon)
            normed = center * inverse
            n1[at, :] = normed
            inv[at, :] = jnp.broadcast_to(inverse, (32, LANES))
            value = normed * vt[3:4] + vt[4:5]
            h1[at, :] = value
            hb[at, :] = value.astype(low)

    loop(TOKENS // 64, first_norm)

    @pl.when(away)
    def _():
        lead_away(2)
        finish(1)

    collect_first(2)
    token_keep(1).start()
    for n in (1, 2, 3):
        token(1, n).start()

    collect_first(1)
    collect_rest(1)

    def rise(j, dst):
        dr[:, pl.ds(dst * 256, 256)] = dot(hb[...], f1[:, rows(j, 256)])

    def bend(j, src):
        cols = rows(j, 256)
        for i in range(TOKENS // 32):
            at = pl.ds(i * 32, 32)
            u = dr[at, pl.ds(src * 256, 256)] + bu[:, cols]
            below = 0.5 + 0.5 * lax.erf(u * (0.5**0.5))
            slope = below + u * (jnp.exp(-0.5 * u * u) * 0.3989422804014327)
            g[at, cols] = (u * below).astype(low)
            gp[at, cols] = slope.astype(low)

    rise(0, 0)

    def up(t):
        rise(2 * t + 1, 1)
        bend(2 * t, 0)
        rise(lax.rem(2 * t + 2, FF // 256), 0)
        bend(2 * t + 1, 1)

    def up_some(first):
        loop(2, lambda t: up(t + first))

    up_some(0)

    @pl.when(away)
    def _():
        relay(2)

    up_some(2)

    @pl.when(away)
    def _():
        finish(2)

    up_some(4)
    for i in range(4):
        if i >= 2:
            turn(x, xt, i)
        turn(hb, ht, i)
        turn(o, ot, i)
    def down(half):
        at = rows(half, D // 2)
        dr[:, at] = dot_t(g[:, pl.ds(0, D)], f2[at, pl.ds(0, D)])

        def more(n):
            part = rows(n + 1, D)
            dr[:, at] += dot_t(g[:, part], f2[at, part])

        loop(FF // D - 1, more, 3)

    @pl.when(away)
    def _():
        collect_rest(2)

    down(spot.h)

    @pl.when(spot.home)
    def _():
        collect_rest(2)

    down(1 - spot.h)
    token_keep(1).wait()
    for n in (1, 2, 3):
        token(1, n).wait_recv()
    vg[...] = jnp.zeros(vg.shape, full)

    def second_norm(i):
        sums = []
        for n in range(4):
            at = pl.ds(pl.multiple_of(i * LANES + n * 32, 32), 32)
            stream = h1[at, :] + (dr[at, :] + vt[5:6])
            center = stream - mean_of(stream)
            inverse = lax.rsqrt(mean_of(center * center) + epsilon)
            normed = center * inverse
            result = (normed * vt[6:7] + vt[7:8]).astype(low)
            upstream = dy[at, :].astype(full)
            dy[at, :] = result
            scaled = upstream * vt[6:7]
            back = inverse * (scaled - mean_of(scaled) - normed * mean_of(scaled * normed))
            dr[at, :] = back
            rounded = back.astype(low)
            df[at, :] = rounded
            sums.append((sum_rows(rounded.astype(full)), sum_rows(upstream * normed), sum_rows(upstream)))
        for row, parts in enumerate(zip(*sums)):
            vg[5 + row : 6 + row] += sum(parts)
        turn(df, dft, i)

    loop(TOKENS // LANES, second_norm)
    for a in (0, 1):
        for n in (1, 2, 3):
            token(a, n).wait_send()

    @pl.when(away)
    def _():
        for p in pieces:
            swap(p).wait_send()

    def settle():
        for p in pieces:
            over_x(p, mine).wait_send()
            over_z(p, mine).wait_send()
            diagonal(p, by_z).wait_send()
            for n, shard in enumerate((mine, by_x, by_z, by_both)):
                over_core(p, n, shard).wait_send()

    return settle


def backward_phase(spot, r, settle):
    low, full = jnp.bfloat16, jnp.float32
    count = r.diag.shape[0]
    away = jnp.logical_not(spot.home)
    columns, got_outs, got_grads, sums, by_row, by_column = r.columns, r.got_outs, r.got_grads, r.sums, r.by_row, r.by_column
    vectors_grad, rows_new, columns_new = r.vectors_grad, r.rows_new, r.columns_new
    moments_new, vectors_new, scale_new = r.moments_new, r.vectors_new, r.scale_new
    fa, f1, f2, xt, ot, ht, dft, qkv, g, gp = r.fa, r.f1, r.f2, r.xt, r.ot, r.ht, r.dft, r.qkv, r.g, r.gp
    n1, inv, dr, df, vt, vg, dbu, vt_low, square = r.n1, r.inv, r.dr, r.df, r.vt, r.vg, r.dbu, r.vt_low, r.square
    da, do, dx, du = r.x, r.dy, r.o, r.hb
    acc, other, stage_f, stage_v, total = r.acc, r.other, r.stage_f, r.stage_v, r.total
    diag, from_x, from_z, swapped = r.diag, r.from_x, r.from_z, r.swapped
    stf, sta, srf, sra, small, small_new, spread_row = r.stf, r.sta, r.srf, r.sra, r.small, r.small_new, r.square.at[pl.ds(0, count)]
    out_sem, core_s, core_r, x_s, x_r, z_s, z_r = r.out_sem, r.core_s, r.core_r, r.bx_s, r.bx_r, r.bz_s, r.bz_r
    d_s, d_r, swap_s, swap_r, st_s, st_r, st_keep = r.bd_s, r.bd_r, r.bswap_s, r.bswap_r, r.st_s, r.st_r, r.st_keep
    t_s, t_r, keep_sem = r.bt_s, r.bt_r, r.bkeep_sem
    routed = ((do, got_outs), (dx, got_grads))

    def token(a, n):
        device, k = spot.router(n)
        src, dst = routed[a]
        return remote(
            src.at[pl.ds(n * LANES, LANES)],
            dst.at[rows(spot.k, LANES)],
            t_s.at[a, n],
            t_r.at[a, n],
            device,
        )

    def token_from(a, n):
        device, k = spot.router(n)
        src, dst = routed[a]
        return remote(
            src.at[pl.ds(n * LANES, LANES)],
            dst.at[rows(k, LANES)],
            t_s.at[a, n],
            t_r.at[a, n],
            device,
        )

    def token_keep(a):
        src, dst = routed[a]
        return pltpu.make_async_copy(
            src.at[pl.ds(0, LANES)], dst.at[rows(spot.k, LANES)], keep_sem.at[a]
        )

    def send_tokens(a, which=(1, 2, 3)):
        for n in which:
            token(a, n).start()

    here = spot.zl * 2 + spot.x
    at_x = spot.zl * 2 + 1 - spot.x
    at_z = (1 - spot.zl) * 2 + spot.x
    at_both = (1 - spot.zl) * 2 + 1 - spot.x

    def cols(p):
        if isinstance(p, int):
            return pl.ds(*SPANS[p])
        return rows(p, PAIR)

    def trade(p):
        if isinstance(p, int) and p >= CHUNKS:
            first, width = SPANS[p][0], D
            src = f1.at[pl.ds(0, HALF), pl.ds(first - BASE, width)]
            dst = other.at[:, pl.ds(first, width)]
        else:
            src, dst = stage_f.at[lax.rem(p, RING)], other.at[:, cols(p)]
        return remote(src, dst, core_s.at[p], core_r.at[p], spot.across_core)

    def trade_vectors():
        return remote(
            stage_v,
            other.at[:, pl.ds(BASE + VEC, LANES)],
            core_s.at[PIECES],
            core_r.at[PIECES],
            spot.across_core,
        )

    def over_x(p):
        return remote(
            acc.at[rows(at_x, count), cols(p)],
            from_x.at[:, cols(p)],
            x_s.at[p],
            x_r.at[p],
            spot.across_x,
        )

    def over_z(p):
        return remote(
            acc.at[rows(at_z, count), cols(p)],
            from_z.at[:, cols(p)],
            z_s.at[p],
            z_r.at[p],
            spot.across_z,
        )

    def diagonal(p, z_first):
        return remote(
            acc.at[rows(at_both, count), cols(p)],
            diag.at[:, cols(p)],
            d_s.at[p],
            d_r.at[p],
            spot.across_z if z_first else spot.across_x,
        )

    def swap(p):
        return remote(
            acc.at[rows(here, count), cols(p)],
            swapped.at[:, cols(p)],
            swap_s.at[p],
            swap_r.at[p],
            spot.partner,
        )

    stats, gathered = (stf, sta), (srf, sra)

    def share(n, step):
        device, _ = spot.peer(step)
        return remote(stats[n], gathered[n].at[spot.m], st_s.at[n, step], st_r.at[n, step], device)

    def share_from(n, step):
        device, m = spot.peer((PEERS - step) % PEERS)
        return remote(stats[n], gathered[n].at[m], st_s.at[n, step], st_r.at[n, step], device)

    def share_keep(n):
        return pltpu.make_async_copy(stats[n], gathered[n].at[spot.m], st_keep.at[n])

    def meet(p):
        trade(p).wait_recv()
        if isinstance(p, int) and p == VALUE_PIECE:
            trade_vectors().wait_recv()

        def add(i):
            view = (rows(i, 32), cols(p))
            acc[view] = acc[view] + other[view]

        loop(HALF // 32, add, 3)

        def forward(z_first):
            diagonal(p, z_first).start()
            if z_first:
                over_z(p).start()
            else:
                over_x(p).start()

        forward(isinstance(p, int) and p in Z_FIRST)

    def relay(p):
        z_first = p in Z_FIRST
        diagonal(p, z_first).wait_recv()
        base = at_x if z_first else at_z

        def add(i):
            view = (pl.ds(pl.multiple_of(base * count + i * 32, 32), 32), cols(p))
            acc[view] = acc[view] + diag[rows(i, 32), cols(p)]

        loop(count // 32, add, 3)
        if z_first:
            over_x(p).start()
        else:
            over_z(p).start()

    def close(p):
        over_x(p).wait_recv()
        over_z(p).wait_recv()

        def add(i):
            view = (pl.ds(pl.multiple_of(here * count + i * 16, 16), 16), cols(p))
            part = (rows(i, 16), cols(p))
            done = acc[view].astype(full) + from_x[part].astype(full) + from_z[part].astype(full)
            total[part] = done
            acc[view] = done.astype(low)

        loop(count // 16, add, 3)

        @pl.when(away)
        def _():
            swap(p).start()

    token_keep(0).start()
    send_tokens(0)

    def chunk(c):
        third = lax.rem(c, RING)
        mine = rows(c, CHUNK)

        @pl.when(c >= RING)
        def _():
            trade(c - RING).wait_send()

        first = pl.multiple_of(c * PAIR, PAIR)

        def give(left, right, shift, at):
            def part(n):
                n = n * 256
                whole = dot(left[...], right[:, pl.ds(pl.multiple_of(shift + n, 256), 256)]).astype(low)
                stage_f[third, :, pl.ds(pl.multiple_of(at + n, 256), 256)] = whole[:HALF]
                acc[:, pl.ds(pl.multiple_of(first + at + n, 256), 256)] = whole[HALF:]

            loop(CHUNK // 256, part, 2)

        def bend_back(i):
            at, here_c = rows(i, 256), rows(c * 2 + i, 256)
            value = dot(df[...], f2[:, here_c]) * gp[:, here_c].astype(full)
            rounded = value.astype(low)
            du[:, at] = rounded
            dbu[:, here_c] = sum_rows(rounded.astype(full))

        loop(CHUNK // 256, bend_back, 2)
        give(dft, g, c * CHUNK, CHUNK)

        @pl.when(c >= 2)
        def _():
            meet(c - 1)

        give(ht, du, 0, 0)
        trade(c).start()
        def lift(i):
            at = rows(i, 256)
            dr[:, at] += dot_t(du[:, pl.ds(0, CHUNK)], f1[at, mine])

        loop(D // 256, lift, 3)

        @pl.when(c == 0)
        def _():
            meet(0)

        @pl.when(c == 3)
        def _():
            relay(0)

        @pl.when(c == 5)
        def _():
            relay(1)
            close(0)

    loop(CHUNKS, chunk)
    meet(CHUNKS - 1)
    for row in range(4):
        vg[8 + row : 9 + row] = dbu[:, pl.ds(row * D, D)]
    settle()

    def first_norm_back(i):
        sums = []
        for n in range(2):
            at = pl.ds(pl.multiple_of(i * 64 + n * 32, 32), 32)
            normed = n1[at, :]
            upstream = dr[at, :]
            scaled = upstream * vt[3:4]
            back = inv[at, :1] * (scaled - mean_of(scaled) - normed * mean_of(scaled * normed))
            dr[at, :] = back
            rounded = back.astype(low)
            da[at, :] = rounded
            sums.append((sum_rows(rounded.astype(full)), sum_rows(upstream * normed), sum_rows(upstream)))
        for row, (one, two) in enumerate(zip(*sums)):
            vg[2 + row : 3 + row] += one + two

    loop(TOKENS // 64, first_norm_back)
    def outer(src, right, first, j):
        def part(n):
            at = n * 256
            whole = dot(src[...], right[:, pl.ds(j * D + at, 256)]).astype(low)
            f1[pl.ds(0, HALF), pl.ds(first - BASE + at, 256)] = whole[:HALF]
            acc[:, pl.ds(first + at, 256)] = whole[HALF:]

        loop(D // 256, part, 3)

    outer(ot, da, BASE, 0)
    trade(OUT_PIECE).start()

    token_keep(0).wait()
    for n in (1, 2, 3):
        token(0, n).wait_send()

    def out_back(j):
        do[:, rows(j, 256)] = dot_t(da[...], fa[rows(j, 256), pl.ds(QKV, D)]).astype(low)

    loop(D // 256, out_back, 3)
    relay(2)
    close(1)
    heads = Heads()

    def attend_back(block, j):
        at = rows(block, LANES)
        q_cols, k_cols, v_cols = rows(j, LANES), rows(j + 6, LANES), rows(j + 12, LANES)
        q, k, v = heads.stack(qkv[at, q_cols]), qkv[at, k_cols], qkv[at, v_cols]
        upstream = heads.stack(do[at, q_cols])
        weights = heads.weigh(q, k)
        grad_w = dot_t(upstream, v)
        centered = grad_w - jnp.sum(grad_w * weights, axis=-1, keepdims=True)
        grad_s = (weights * centered).astype(low)
        qkv[at, q_cols] = heads.join(dot(grad_s, k) * HEAD ** (-0.5))
        qkv[at, k_cols] = (t_dot(grad_s, q) * HEAD ** (-0.5)).astype(low)
        qkv[at, v_cols] = t_dot(weights.astype(low), upstream).astype(low)

    def attend_back_block(block):
        def part(n):
            for j in range(3):
                attend_back(block, n * 3 + j)

        loop(2, part)

    attend_back_block(0)
    meet(OUT_PIECE)
    relay(3)
    attend_back_block(1)
    close(2)
    attend_back_block(2)
    relay(4)
    close(3)
    attend_back_block(3)
    outer(xt, qkv, BASE + D, 0)
    trade(QUERY_PIECE).start()
    outer(xt, qkv, BASE + 2 * D, 1)
    trade(KEY_PIECE).start()

    def bias_sums(i):
        at = rows(i, LANES)
        vg[0:1] += sum_rows(qkv[at, pl.ds(0, D)].astype(full))
        vg[1:2] += sum_rows(qkv[at, pl.ds(2 * D, D)].astype(full))

    loop(4, bias_sums)
    vt_low[...] = vg[...].T.astype(low)
    stage_v[...] = vt_low[rows(1 - spot.c, HALF), :]
    trade_vectors().start()
    acc[:, pl.ds(BASE + VEC, LANES)] = vt_low[rows(spot.c, HALF), :]
    outer(xt, qkv, BASE + 3 * D, 2)
    trade(VALUE_PIECE).start()
    meet(QUERY_PIECE)
    relay(5)
    close(4)
    meet(KEY_PIECE)

    def input_back(j):
        at = rows(j, 256)

        value = dr[:, at]
        for n in range(3):
            value = value + dot_t(qkv[:, rows(n, D)], fa[at, rows(n, D)])
        dx[:, at] = value.astype(low)

    loop(D // 256, input_back)
    token_keep(1).start()
    send_tokens(1)
    meet(VALUE_PIECE)
    lane = lax.broadcasted_iota(jnp.int32, (1, LANES), 1)
    row_new = {}

    def arrive(p):
        @pl.when(away)
        def _():
            swap(p).wait_recv()
            total[:, cols(p)] = swapped[:, cols(p)].astype(full)

        put(p).start()

    def put(p):
        return pltpu.make_async_copy(total.at[:, cols(p)], sums.at[:, cols(p)], out_sem.at[p])

    def tally_feedforward():
        for c in range(CHUNKS):
            arrive(c)
        for w in range(2):
            spread_row[...] = jnp.zeros(spread_row.shape, full)

            def add_squares(c):
                at = pl.ds(pl.multiple_of(c * PAIR + w * CHUNK, CHUNK), CHUNK)
                m = total[:, at]
                held = m * m + tiny_square
                spread_row[:, :1] += jnp.sum(held, axis=1, keepdims=True)
                stf[:, at] = sum_rows(held)

            loop(CHUNKS, add_squares)
            r = DECAY * small[2, :, 4 + w : 5 + w] + KEEP * (spread_row[:, :1] / FF)
            row_new[4 + w] = r
            inverse = 1.0 / r

            def weigh_squares(c):
                first = pl.multiple_of(c * PAIR + w * CHUNK, CHUNK)
                m = total[:, pl.ds(first, CHUNK)]
                stf[:, pl.ds(pl.multiple_of(2 * FF + first, CHUNK), CHUNK)] = sum_rows(m * m * inverse)

            loop(CHUNKS, weigh_squares)
            stf[:, pl.ds(4 * FF + w * LANES, LANES)] = jnp.broadcast_to(sum_rows(r), (1, LANES))
        spread(0)

    def spread(n):
        share_keep(n).start()
        for step in range(1, PEERS):
            share(n, step).start()

    row_sums = [jnp.zeros((1, LANES), full)]

    def tally_matrix(j):
        m = total[:, pl.ds(ATTENTION_AT[j], D)]
        squared = m * m
        held = squared + tiny_square
        mean = jnp.sum(held, axis=1, keepdims=True) / D
        r = DECAY * small[2, :, j : j + 1] + KEEP * mean
        row_new[j] = r
        sta[:, pl.ds(j * D, D)] = sum_rows(held)
        sta[:, pl.ds((4 + j) * D, D)] = sum_rows(squared * (1.0 / r))
        row_sums[0] = jnp.where(lane == j, sum_rows(r), row_sums[0])

    def tally_vectors():
        sta[:, pl.ds(8 * D, LANES)] = row_sums[0]
        m = total[:, pl.ds(BASE + VEC, LANES)]
        renewed = DECAY * small[1] + KEEP * (m * m + tiny_square)
        move = m * lax.rsqrt(renewed)
        small_new[0] = m
        small_new[1] = renewed
        small_new[2] = move
        sta[:, pl.ds(8 * D + LANES, LANES)] = sum_rows(move * move)
        spread(1)

    scale = [jnp.zeros((1, LANES), full)]

    def gathered_sum(n, first, width):
        value = gathered[n][0, :, pl.ds(first, width)]
        for peer in range(1, PEERS):
            value = value + gathered[n][peer, :, pl.ds(first, width)]
        return value

    def take(n):
        share_keep(n).wait()
        for step in range(1, PEERS):
            share_from(n, step).wait_recv()

    def renew(n, index, mean, tiles, column_at, entries):
        weighted = jnp.zeros((1, 1), full)
        for at_stat, at_column, width in tiles:
            here_c = (slice(None), pl.ds(at_column, width))
            c = DECAY * columns[here_c] + KEEP * (gathered_sum(n, at_stat, width) / D)
            columns_new[here_c] = c
            sums = gathered_sum(n, column_at + at_stat, width)
            weighted = weighted + jnp.sum(sums * mean / c, axis=1, keepdims=True)
        size = jnp.sqrt(weighted / entries)
        scale[0] = jnp.where(lane == index, size, scale[0])
        factor = jnp.sqrt(mean) * (matrix_rate / jnp.maximum(1.0, size / clip_level))
        for _, at_column, width in tiles:
            here_c = (slice(None), pl.ds(at_column, width))
            by_column[here_c] = lax.rsqrt(columns_new[here_c]) * factor

    close(5)
    relay(OUT_PIECE)
    relay(QUERY_PIECE)
    close(OUT_PIECE)
    relay(KEY_PIECE)
    tally_feedforward()
    close(QUERY_PIECE)
    relay(VALUE_PIECE)
    arrive(OUT_PIECE)
    tally_matrix(3)
    close(KEY_PIECE)
    arrive(QUERY_PIECE)
    tally_matrix(0)
    close(VALUE_PIECE)
    arrive(KEY_PIECE)
    tally_matrix(1)
    take(0)
    for w in range(2):
        mean = gathered_sum(0, 4 * FF + w * LANES, LANES)[:, :1] / D
        tiles = [
            (c * PAIR + w * CHUNK, 4 * D + w * FF + c * CHUNK, CHUNK) for c in range(CHUNKS)
        ]
        renew(0, 4 + w, mean, tiles, 2 * FF, D * FF)
    arrive(VALUE_PIECE)
    tally_matrix(2)
    tally_vectors()
    take(1)
    extra = gathered_sum(1, 8 * D, LANES)
    for j in range(4):
        renew(1, j, extra[:, j : j + 1] / D, [(j * D, j * D, D)], 4 * D, D * D)
    size = jnp.sqrt(gathered_sum(1, 8 * D + LANES, LANES) / D)
    small_new[3] = small[0] - small_new[2] * (vector_rate / jnp.maximum(1.0, size / clip_level))
    scale_new[...] = jnp.where(lane < 6, scale[0], pltpu.roll(size, 6, 1))[:, : scale_new.shape[1]]
    row_all = jnp.zeros((count, LANES), full)
    lanes = lax.broadcasted_iota(jnp.int32, (count, LANES), 1)
    for j in range(6):
        row_all = jnp.where(lanes == j, row_new[j], row_all)
    small_new[2] = row_all
    by_row[...] = lax.rsqrt(jnp.where(lanes < 6, row_all, 1.0))
    for n, dst in enumerate((vectors_grad, moments_new, rows_new, vectors_new)):
        square[pl.ds(0, count), :] = small_new[n]
        turned = square[...].T
        for row in range(dst.shape[0]):
            dst[row] = turned[row : row + 1, :count]

    for p in range(PIECES):
        if p >= CHUNKS - RING:
            trade(p).wait_send()
        diagonal(p, p in Z_FIRST).wait_send()
        over_x(p).wait_send()
        over_z(p).wait_send()
    for n in range(2):
        for step in range(1, PEERS):
            share(n, step).wait_send()

    @pl.when(away)
    def _():
        for p in range(PIECES):
            swap(p).wait_send()

    trade_vectors().wait_send()
    token_keep(1).wait()
    for n in (1, 2, 3):
        token_from(0, n).wait_recv()
        token_from(1, n).wait_recv()
        token(1, n).wait_send()
    for p in range(PIECES):
        put(p).wait()


LAYER_IN = (
    "wa", "wf", "layer_in", "cotangent", "vectors", "row_moments", "vector_moments", "columns", "target", "keep_mask",
    "capacity",
)
LAYER_OUT = (
    "got_outs", "got_grads", "sums", "by_row", "by_column", "vectors_grad", "rows_new", "columns_new", "moments_new",
    "vectors_new", "scale_new",
)


def layer_scratch(count):
    low, full = jnp.bfloat16, jnp.float32
    wide = BASE + WIDE
    dma = pltpu.SemaphoreType.DMA
    buffers = dict(
        fa=((D, WIDE), low),
        f1=((D, FF), low),
        f2=((D, FF), low),
        xt=((D, TOKENS), low),
        ot=((D, TOKENS), low),
        ht=((D, TOKENS), low),
        dft=((D, TOKENS), low),
        qkv=((TOKENS, QKV), low),
        g=((TOKENS, FF), low),
        gp=((TOKENS, FF), low),
        n1=((TOKENS, D), full),
        inv=((TOKENS, LANES), full),
        dr=((TOKENS, D), full),
        df=((TOKENS, D), low),
        vt=((16, D), full),
        vg=((LANES, D), full),
        x=((TOKENS, D), low),
        dy=((TOKENS, D), low),
        o=((TOKENS, D), low),
        h1=((TOKENS, D), full),
        hb=((TOKENS, D), low),
        qb=((1, QKV), full),
        bu=((1, FF), full),
        square=((LANES, LANES), full),
        dbu=((1, FF), full),
        vt_low=((D, LANES), low),
        acc=((HALF, wide), low),
        other=((HALF, wide), low),
        stage_f=((RING, HALF, PAIR), low),
        stage_v=((HALF, LANES), low),
        diag=((count, wide), low),
        from_x=((count, wide), low),
        from_z=((count, wide), low),
        swapped=((count, wide), low),
        total=((count, wide), full),
        stf=((1, STAT_F), full),
        sta=((1, STAT_A), full),
        srf=((PEERS, 1, STAT_F), full),
        sra=((PEERS, 1, STAT_A), full),
        small=((3, count, LANES), full),
        small_new=((4, count, LANES), full),
    )
    scratch = {name: pltpu.VMEM(*one) for name, one in buffers.items()}
    for name in ("swap", "x", "z", "d"):
        for end in ("s", "r"):
            scratch[f"{name}_{end}"] = dma((3,))
            scratch[f"b{name}_{end}"] = dma((PIECES,))
    for end in ("s", "r"):
        scratch[f"c_{end}"] = dma((3, 4))
        scratch[f"t_{end}"] = dma((2, 4))
        scratch[f"bt_{end}"] = dma((2, 4))
        scratch[f"core_{end}"] = dma((PIECES + 1,))
        scratch[f"st_{end}"] = dma((2, PEERS))
    scratch.update(
        own_sem=dma((3,)), keep_sem=dma((2,)), bkeep_sem=dma((2,)), load_sem=dma((20,)),
        out_sem=dma((PIECES,)), st_keep=dma((2,)),
    )
    return scratch


def layer_kernel(names, *refs):
    r = types.SimpleNamespace(**dict(zip(names, refs)))
    spot = Spot()
    r.greet = lambda: greet(
        [spot.across_core, spot.partner]
        + [spot.router(n)[0] for n in (1, 2, 3)]
        + [spot.peer(step)[0] for step in range(1, PEERS)]
    )
    settle = forward_phase(spot, r)
    backward_phase(spot, r, settle)


def layer(wa, wf, layer_in, cotangent, vectors, row_moments, vector_moments, columns, *routing):
    low, full = jnp.bfloat16, jnp.float32
    count = wa.shape[1]
    sds = jax.ShapeDtypeStruct
    scratch = layer_scratch(count)
    return pl.pallas_call(
        functools.partial(layer_kernel, LAYER_IN + LAYER_OUT + tuple(scratch)),
        out_shape=(
            sds((TOKENS, D), low),
            sds((TOKENS, D), low),
            sds((count, BASE + WIDE), full),
            sds((count, LANES), full),
            sds(columns.shape, full),
            sds(vectors.shape, full),
            sds(row_moments.shape, full),
            sds(columns.shape, full),
            sds(vectors.shape, full),
            sds(vectors.shape, full),
            sds((1, 18), full),
        ),
        in_specs=[ANY] * 4 + [VMEM] * 4 + [SMEM] * 3,
        out_specs=(ANY,) * 3 + (VMEM,) * 8,
        scratch_shapes=list(scratch.values()),
        compiler_params=pltpu.CompilerParams(
            collective_id=0, has_side_effects=True, vmem_limit_bytes=LIMIT
        ),
        name="layer",
    )(wa, wf, layer_in, cotangent, vectors, row_moments, vector_moments, columns, *routing)


WIDTH = 1024


def finish_kernel(
    target, keep_mask, capacity, outs, grads, layer_in, cotangent, sums_f, sums_a, wa, wf, by_row, by_f1, by_f2, by_a,
    vectors_grad_i, rows_i, columns_i, moments_i, vectors_i, scale_i,
    layer_out, input_grad, ga, gf, ua, uf, vectors_grad, rows_new, columns_new, moments_new, vectors_new, scale,
):
    step = pl.program_id(0)
    for n in range(2):
        at = step * 2 + n
        aim = target[at]
        rank = jnp.int32(0)
        for s in range(target.shape[0]):
            same = (target[s] == aim) & (keep_mask[s] == 1) & (s < at)
            rank = rank + same.astype(jnp.int32)
        taken = (keep_mask[at] == 1) & (rank < capacity[aim])
        slot = jnp.where(taken, aim * SLOTS + rank, 0)
        here = pl.ds(n * SEQ, SEQ)
        for src, own, dst in ((outs, layer_in, layer_out), (grads, cotangent, input_grad)):
            back = src[rows(slot, SEQ), :].astype(jnp.float32)
            dst[here, :] = jnp.where(taken, back, own[here, :])

    @pl.when(step < FF // WIDTH)
    def _():
        for w, by_column in enumerate((by_f1, by_f2)):
            for n in range(WIDTH // CHUNK):
                at = pl.ds(n * CHUNK, CHUNK)
                m = sums_f[:, pl.ds((2 * n + w) * CHUNK, CHUNK)]
                gf[w, :, at] = m
                uf[w, :, at] = wf[w, :, at] - m * by_row[:, 4 + w : 5 + w] * by_column[:, at]

    for j in range(4):

        @pl.when(step == j)
        def _():
            m = sums_a[...]
            ga[0] = m
            ua[0] = wa[0] - m * by_row[:, j : j + 1] * by_a[...]

    @pl.when(step == 0)
    def _():
        for src, dst in (
            (vectors_grad_i, vectors_grad),
            (rows_i, rows_new),
            (columns_i, columns_new),
            (moments_i, moments_new),
            (vectors_i, vectors_new),
            (scale_i, scale),
        ):
            dst[...] = src[...]


def finish(routing, layer_in, cotangent, wa, wf, results):
    got_outs, got_grads, sums, by_row, by_column, *small = results
    count = wa.shape[1]
    full = jnp.float32

    def whole(value):
        return pl.BlockSpec(value.shape, lambda i: (0,) * len(value.shape))

    def tokens():
        return pl.BlockSpec((2 * SEQ, D), lambda i: (i, 0))

    def matrix():
        return pl.BlockSpec((1, count, D), lambda i: (jnp.minimum(i, 3), 0, 0))

    def chunk():
        return pl.BlockSpec((2, count, WIDTH), lambda i: (0, 0, third(i)))

    def third(i):
        return jnp.minimum(i, FF // WIDTH - 1)

    def column_block(shape, first):
        return pl.BlockSpec(shape, lambda i: (0, first // WIDTH + third(i)))

    return pl.pallas_call(
        finish_kernel,
        grid=(TOKENS // SEQ // 2,),
        out_shape=(
            jax.ShapeDtypeStruct((TOKENS, D), full),
            jax.ShapeDtypeStruct((TOKENS, D), full),
            jax.ShapeDtypeStruct(wa.shape, full),
            jax.ShapeDtypeStruct(wf.shape, full),
            jax.ShapeDtypeStruct(wa.shape, full),
            jax.ShapeDtypeStruct(wf.shape, full),
        )
        + tuple(jax.ShapeDtypeStruct(one.shape, full) for one in small),
        in_specs=[SMEM] * 3
        + [
            whole(got_outs),
            whole(got_grads),
            tokens(),
            tokens(),
            pl.BlockSpec((count, 2 * WIDTH), lambda i: (0, third(i))),
            pl.BlockSpec((count, D), lambda i: (0, BASE // D + lax.rem(jnp.minimum(i, 3) + 1, 4))),
            matrix(),
            chunk(),
            whole(by_row),
            column_block((1, WIDTH), 4 * D),
            column_block((1, WIDTH), 4 * D + FF),
            pl.BlockSpec((1, D), lambda i: (0, jnp.minimum(i, 3))),
        ]
        + [whole(one) for one in small],
        out_specs=(tokens(), tokens(), matrix(), chunk(), matrix(), chunk())
        + tuple(whole(one) for one in small),
        compiler_params=pltpu.CompilerParams(vmem_limit_bytes=LIMIT),
        name="finish",
    )(
        *routing, got_outs, got_grads, layer_in, cotangent, sums, sums, wa, wf, by_row, by_column,
        by_column, by_column, *small,
    )

def fast_body(
    layer_in,
    cotangent,
    target,
    keep_mask,
    capacity,
    attention_weights,
    feedforward_weights,
    vectors,
    row_moments,
    column_moments,
    vector_moments,
):
    inputs, upstream = layer_in.reshape(TOKENS, D), cotangent.reshape(TOKENS, D)
    routing = (target, keep_mask, capacity)
    vectors, row_moments, vector_moments = (
        value.transpose(1, 0, 2) for value in (vectors, row_moments, vector_moments)
    )
    results = layer(
        attention_weights[0],
        feedforward_weights[0],
        inputs,
        upstream,
        vectors,
        row_moments,
        vector_moments,
        column_moments,
        *routing,
    )
    layer_out, input_grad, ga, gf, ua, uf, vectors_grad, rows_new, columns_new, moments_new, vectors_new, scale = finish(
        routing, inputs, upstream, attention_weights[0], feedforward_weights[0], results
    )
    layer_out, input_grad = (value.reshape(layer_in.shape) for value in (layer_out, input_grad))
    return (
        layer_out,
        input_grad,
        ga[None],
        gf[None],
        vectors_grad.transpose(1, 0, 2),
        rows_new.transpose(1, 0, 2),
        columns_new,
        moments_new.transpose(1, 0, 2),
        ua[None],
        uf[None],
        vectors_new.transpose(1, 0, 2),
        scale,
    )


def solution(mesh):
    in_specs = (
        P(("group", "mp"), None, None),
        P(("group", "mp"), None, None),
        P(("group", "mp")),
        P(("group", "mp")),
        P(),
        P("group", None, "mp", None),
        P("group", None, "mp", None),
        P("group", None, "mp"),
        P("group", None, "mp"),
        P("group", None),
        P("group", None, "mp"),
    )
    out_specs = (
        P(("group", "mp"), None, None),
        P(("group", "mp"), None, None),
        P("group", None, "mp", None),
        P("group", None, "mp", None),
        P("group", None, "mp"),
        P("group", None, "mp"),
        P("group", None),
        P("group", None, "mp"),
        P("group", None, "mp", None),
        P("group", None, "mp", None),
        P("group", None, "mp"),
        P("group", None),
    )
    suited = mesh.shape["group"] == 4 and mesh.shape["mp"] == PEERS
    body = fast_body if suited else generic_body
    return jax.shard_map(body, mesh=mesh, in_specs=in_specs, out_specs=out_specs, check_vma=False)
```

```python
import functools
import types

import jax
import jax.numpy as jnp
from jax import lax
from jax.experimental import pallas as pl
from jax.experimental.pallas import tpu as pltpu
from jax.sharding import PartitionSpec as P

HEADS = 12
SLOTS = 2
STEP = 10


epsilon = 1e-05
tiny_square = 1e-30
clip_level = 1.0
matrix_rate = 0.01
vector_rate = 0.1


def normalize(stream, gains, shifts):
    center = stream - jnp.mean(stream, axis=-1, keepdims=True)
    inverse = lax.rsqrt(jnp.mean(center * center, axis=-1, keepdims=True) + epsilon)
    normed = center * inverse
    return (normed * gains + shifts, normed, inverse)


def normalize_back(upstream, gains, normed, inverse):
    scaled = upstream * gains
    return inverse * (
        scaled
        - jnp.mean(scaled, axis=-1, keepdims=True)
        - normed * jnp.mean(scaled * normed, axis=-1, keepdims=True)
    )


def gelu_exact(tensor):
    return jax.nn.gelu(tensor, approximate=False)


def generic_body(
    layer_in,
    cotangent,
    target,
    keep_mask,
    capacity,
    attention_weights,
    feedforward_weights,
    vectors,
    row_moments,
    column_moments,
    vector_moments,
):
    group_count = lax.axis_size("group")
    local_count = layer_in.shape[0]
    seq_len = layer_in.shape[1]
    model_width = layer_in.shape[2]
    head_dim = model_width // HEADS
    hidden = feedforward_weights.shape[3]
    slot_count = SLOTS
    buffered = group_count * slot_count
    row_total = buffered * seq_len
    score_scale = head_dim ** (-0.5)
    group_ids = jnp.arange(group_count, dtype=jnp.int32)
    aimed_at = (target[:, None] == group_ids[None, :]).astype(jnp.int32)
    wanted = aimed_at * keep_mask[:, None]
    earlier = jnp.cumsum(wanted, axis=0) - wanted
    position = jnp.sum(earlier * aimed_at, axis=1)
    allowed = jnp.sum(aimed_at * capacity[None, :], axis=1)
    admitted = (keep_mask == 1) & (position < allowed)
    placed = target * slot_count + position
    cell_ids = jnp.arange(buffered, dtype=jnp.int32)
    matched = admitted[:, None] & (placed[:, None] == cell_ids[None, :])
    local_ids = jnp.arange(local_count, dtype=jnp.int32)
    source = jnp.sum(jnp.where(matched, local_ids[:, None], 0), axis=0) + jnp.where(
        jnp.any(matched, axis=0), 0, local_count
    )
    blank_row = jnp.zeros((1, seq_len, model_width), jnp.float32)
    send_inputs = jnp.take(jnp.concatenate([layer_in, blank_row], axis=0), source, axis=0).reshape(
        group_count, slot_count, seq_len, model_width
    )
    send_grads = jnp.take(jnp.concatenate([cotangent, blank_row], axis=0), source, axis=0).reshape(
        group_count, slot_count, seq_len, model_width
    )
    got_inputs, got_grads = (
        lax.all_to_all(send_inputs, "group", split_axis=0, concat_axis=0, tiled=True),
        lax.all_to_all(send_grads, "group", split_axis=0, concat_axis=0, tiled=True),
    )
    attention_full, feedforward_full, vectors_full = (
        lax.all_gather(attention_weights[0].astype(jnp.bfloat16), "mp", axis=1, tiled=True),
        lax.all_gather(feedforward_weights[0].astype(jnp.bfloat16), "mp", axis=1, tiled=True),
        lax.all_gather(vectors[0].astype(jnp.bfloat16), "mp", axis=1, tiled=True),
    )
    vector_rows = vectors_full.astype(jnp.float32)
    bias_query = vector_rows[0]
    bias_value = vector_rows[1]
    bias_output = vector_rows[2]
    gain_first = vector_rows[3]
    shift_first = vector_rows[4]
    bias_down = vector_rows[5]
    gain_second = vector_rows[6]
    shift_second = vector_rows[7]
    bias_up = vector_rows[8:12].reshape(-1)
    inputs = got_inputs.reshape(row_total, model_width)
    inputs_low = inputs.astype(jnp.bfloat16)
    projected = jnp.einsum(
        "rd,cde->cre", inputs_low, attention_full[:3], preferred_element_type=jnp.float32
    )
    projection_bias = jnp.stack([bias_query, jnp.zeros_like(bias_query), bias_value])
    projected_low = (projected + projection_bias[:, None, :]).astype(jnp.bfloat16)
    queries = projected_low[0].reshape(buffered, seq_len, HEADS, head_dim)
    key_rows = projected_low[1].reshape(buffered, seq_len, HEADS, head_dim)
    values = projected_low[2].reshape(buffered, seq_len, HEADS, head_dim)
    scores = (
        jnp.einsum("nshe,nthe->nhst", queries, key_rows, preferred_element_type=jnp.float32)
        * score_scale
    )
    largest = jnp.max(scores, axis=-1, keepdims=True)
    shifted = jnp.exp(scores - largest)
    totals = jnp.sum(shifted, axis=-1, keepdims=True)
    log_totals = largest + jnp.log(totals)
    weights_low = (shifted / totals).astype(jnp.bfloat16)
    attended = jnp.einsum(
        "nhst,nthe->nshe", weights_low, values, preferred_element_type=jnp.float32
    )
    attended_low = attended.reshape(row_total, model_width).astype(jnp.bfloat16)
    branch = (
        jnp.dot(attended_low, attention_full[3], preferred_element_type=jnp.float32) + bias_output
    )
    first_norm, normed_first, inverse_first = normalize(inputs + branch, gain_first, shift_first)
    first_low = first_norm.astype(jnp.bfloat16)
    before_act = (
        jnp.dot(first_low, feedforward_full[0], preferred_element_type=jnp.float32) + bias_up
    )
    activated = gelu_exact(before_act).astype(jnp.bfloat16)
    down_branch = (
        jnp.einsum("rf,df->rd", activated, feedforward_full[1], preferred_element_type=jnp.float32)
        + bias_down
    )
    output_rows, normed_second, inverse_second = normalize(
        first_norm + down_branch, gain_second, shift_second
    )
    returned = lax.all_to_all(
        output_rows.reshape(group_count, slot_count, seq_len, model_width),
        "group",
        split_axis=0,
        concat_axis=0,
        tiled=True,
    )
    upstream = got_grads.reshape(row_total, model_width)
    grad_gain_second = jnp.sum(upstream * normed_second, axis=0)
    grad_shift_second = jnp.sum(upstream, axis=0)
    grad_second = normalize_back(upstream, gain_second, normed_second, inverse_second)
    grad_down = grad_second.astype(jnp.bfloat16)
    grad_bias_down = jnp.sum(grad_down.astype(jnp.float32), axis=0)
    grad_w_down = jnp.einsum("rd,rf->df", grad_down, activated, preferred_element_type=jnp.float32)
    grad_activated = jnp.dot(grad_down, feedforward_full[1], preferred_element_type=jnp.float32)
    gelu_pull = jax.vjp(gelu_exact, before_act)[1]
    grad_before = gelu_pull(grad_activated)[0].astype(jnp.bfloat16)
    grad_bias_up = jnp.sum(grad_before.astype(jnp.float32), axis=0)
    grad_w_up = jnp.einsum("rd,rf->df", first_low, grad_before, preferred_element_type=jnp.float32)
    grad_first = grad_second + jnp.einsum(
        "rf,df->rd", grad_before, feedforward_full[0], preferred_element_type=jnp.float32
    )
    feedforward_grads = jnp.stack([grad_w_up, grad_w_down])
    grad_gain_first = jnp.sum(grad_first * normed_first, axis=0)
    grad_shift_first = jnp.sum(grad_first, axis=0)
    grad_residual = normalize_back(grad_first, gain_first, normed_first, inverse_first)
    grad_branch = grad_residual.astype(jnp.bfloat16)
    grad_bias_output = jnp.sum(grad_branch.astype(jnp.float32), axis=0)
    grad_w_output = jnp.einsum(
        "rd,re->de", attended_low, grad_branch, preferred_element_type=jnp.float32
    )
    grad_attended = jnp.einsum(
        "re,de->rd", grad_branch, attention_full[3], preferred_element_type=jnp.float32
    )
    grad_heads = grad_attended.astype(jnp.bfloat16).reshape(buffered, seq_len, HEADS, head_dim)
    again = (
        jnp.einsum("nshe,nthe->nhst", queries, key_rows, preferred_element_type=jnp.float32)
        * score_scale
    )
    exact = jnp.exp(again - log_totals)
    grad_values = jnp.einsum(
        "nhst,nshe->nthe",
        exact.astype(jnp.bfloat16),
        grad_heads,
        preferred_element_type=jnp.float32,
    ).astype(jnp.bfloat16)
    grad_weights = jnp.einsum(
        "nshe,nthe->nhst", grad_heads, values, preferred_element_type=jnp.float32
    )
    grad_scores = (
        exact * (grad_weights - jnp.sum(grad_weights * exact, axis=-1, keepdims=True))
    ).astype(jnp.bfloat16)
    grad_queries = (
        jnp.einsum("nhst,nthe->nshe", grad_scores, key_rows, preferred_element_type=jnp.float32)
        * score_scale
    ).astype(jnp.bfloat16)
    grad_keys = (
        jnp.einsum("nhst,nshe->nthe", grad_scores, queries, preferred_element_type=jnp.float32)
        * score_scale
    ).astype(jnp.bfloat16)
    grad_projected = jnp.stack(
        [
            grad_queries.reshape(row_total, model_width),
            grad_keys.reshape(row_total, model_width),
            grad_values.reshape(row_total, model_width),
        ]
    )
    grad_w_projected = jnp.einsum(
        "rd,cre->cde", inputs_low, grad_projected, preferred_element_type=jnp.float32
    )
    grad_inputs = grad_residual + jnp.einsum(
        "cre,cde->rd", grad_projected, attention_full[:3], preferred_element_type=jnp.float32
    )
    grad_bias_projected = jnp.sum(grad_projected.astype(jnp.float32), axis=1)
    grads_back = lax.all_to_all(
        grad_inputs.reshape(group_count, slot_count, seq_len, model_width),
        "group",
        split_axis=0,
        concat_axis=0,
        tiled=True,
    )
    attention_grads = jnp.concatenate([grad_w_projected, grad_w_output[None]], axis=0)
    vector_grads = jnp.concatenate(
        [
            jnp.stack(
                [
                    grad_bias_projected[0],
                    grad_bias_projected[2],
                    grad_bias_output,
                    grad_gain_first,
                    grad_shift_first,
                    grad_bias_down,
                    grad_gain_second,
                    grad_shift_second,
                ]
            ),
            grad_bias_up.reshape(4, model_width),
        ],
        axis=0,
    )
    attention_part, feedforward_part, vectors_part = (
        lax.psum_scatter(attention_grads, "mp", scatter_dimension=1, tiled=True),
        lax.psum_scatter(feedforward_grads, "mp", scatter_dimension=1, tiled=True),
        lax.psum_scatter(vector_grads, "mp", scatter_dimension=1, tiled=True),
    )
    slot_index = jnp.where(admitted, placed, 0)
    layer_out = jnp.where(
        admitted[:, None, None],
        jnp.take(returned.reshape(buffered, seq_len, model_width), slot_index, axis=0),
        layer_in,
    )
    input_grad = jnp.where(
        admitted[:, None, None],
        jnp.take(grads_back.reshape(buffered, seq_len, model_width), slot_index, axis=0),
        cotangent,
    )
    decay_rate = 1.0 - STEP ** (-0.8)
    keep_rate = 1.0 - decay_rate
    square_attention = attention_part * attention_part + tiny_square
    square_feedforward = feedforward_part * feedforward_part + tiny_square
    square_vectors = vectors_part * vectors_part + tiny_square
    rows_attention = decay_rate * row_moments[0, :4] + keep_rate * jnp.mean(
        square_attention, axis=-1
    )
    rows_feedforward = decay_rate * row_moments[0, 4:] + keep_rate * jnp.mean(
        square_feedforward, axis=-1
    )
    renewed_vectors = decay_rate * vector_moments[0] + keep_rate * square_vectors
    step_vectors = vectors_part / jnp.sqrt(renewed_vectors)
    vector_squares = jnp.sum(step_vectors * step_vectors, axis=-1)
    attention_columns = jnp.sum(square_attention, axis=1)
    feedforward_columns = jnp.sum(square_feedforward, axis=1)
    row_sums = jnp.concatenate(
        [jnp.sum(rows_attention, axis=-1), jnp.sum(rows_feedforward, axis=-1)]
    )
    old_attention = column_moments[0, : 4 * model_width].reshape(4, model_width)
    old_feedforward = column_moments[0, 4 * model_width :].reshape(2, hidden)
    attention_sums, feedforward_sums, rows_summed, vector_total = lax.psum(
        (attention_columns, feedforward_columns, row_sums, vector_squares), "mp"
    )
    columns_attention = decay_rate * old_attention + keep_rate * attention_sums / model_width
    columns_feedforward = decay_rate * old_feedforward + keep_rate * feedforward_sums / model_width
    mean_rows = rows_summed / model_width
    step_attention = attention_part / jnp.sqrt(
        rows_attention[:, :, None] * columns_attention[:, None, :] / mean_rows[:4, None, None]
    )
    step_feedforward = feedforward_part / jnp.sqrt(
        rows_feedforward[:, :, None] * columns_feedforward[:, None, :] / mean_rows[4:, None, None]
    )
    attention_total, feedforward_total = lax.psum(
        (
            jnp.sum(step_attention * step_attention, axis=(1, 2)),
            jnp.sum(step_feedforward * step_feedforward, axis=(1, 2)),
        ),
        "mp",
    )
    scale_attention = jnp.sqrt(attention_total / (model_width * model_width))
    scale_feedforward = jnp.sqrt(feedforward_total / (model_width * hidden))
    scale_vectors = jnp.sqrt(vector_total / model_width)
    attention_updated = (
        attention_weights[0]
        - matrix_rate
        * step_attention
        / jnp.maximum(1.0, scale_attention / clip_level)[:, None, None]
    )
    feedforward_updated = (
        feedforward_weights[0]
        - matrix_rate
        * step_feedforward
        / jnp.maximum(1.0, scale_feedforward / clip_level)[:, None, None]
    )
    vectors_updated = (
        vectors[0]
        - vector_rate * step_vectors / jnp.maximum(1.0, scale_vectors / clip_level)[:, None]
    )
    renewed_rows = jnp.concatenate([rows_attention, rows_feedforward], axis=0)
    renewed_columns = jnp.concatenate(
        [columns_attention.reshape(-1), columns_feedforward.reshape(-1)]
    )
    update_scale = jnp.concatenate([scale_attention, scale_feedforward, scale_vectors])
    return (
        layer_out,
        input_grad,
        attention_part[None],
        feedforward_part[None],
        vectors_part[None],
        renewed_rows[None],
        renewed_columns[None],
        renewed_vectors[None],
        attention_updated[None],
        feedforward_updated[None],
        vectors_updated[None],
        update_scale[None],
    )


MESH = pl.DeviceIdType.MESH
ANY = pl.BlockSpec(memory_space=pl.ANY)
VMEM = pl.BlockSpec(memory_space=pltpu.VMEM)
SMEM = pl.BlockSpec(memory_space=pltpu.SMEM)
LANES = 128
PEERS = 8
LIMIT = 63 * 1024 * 1024
D = 768
FF = 3072
QKV = 3 * D
VEC = QKV + D
WIDE = VEC + LANES
SEQ = 64
TOKENS = 512
HEAD = D // HEADS
DECAY = 1.0 - STEP ** (-0.8)
KEEP = 1.0 - DECAY


class Spot:
    def __init__(self):
        g = lax.axis_index("group")
        m = lax.axis_index("mp")
        y, c = lax.div(g, 2), lax.rem(g, 2)
        z, x = lax.div(m, 2), lax.rem(m, 2)
        h, zl = lax.div(z, 2), lax.rem(z, 2)
        self.g, self.m, self.y, self.c, self.x, self.h, self.zl = g, m, y, c, x, h, zl
        self.home = c == h
        self.k = y * 2 + h
        self.r = c * 4 + zl * 2 + x
        self.across_x = (g, m + 1 - 2 * x)
        self.across_z = (g, m + 2 - 4 * zl)
        self.across_core = (g + 1 - 2 * c, m)
        self.partner = (y * 2 + 1 - c, ((1 - h) * 2 + zl) * 2 + x)

    def shard(self, dc=0, dz=0, dx=0):
        c = 1 - self.c if dc else self.c
        zl = 1 - self.zl if dz else self.zl
        x = 1 - self.x if dx else self.x
        return c * 4 + zl * 2 + x

    def router(self, n):
        y = 1 - self.y if n % 2 else self.y
        h = 1 - self.h if n // 2 else self.h
        return (y * 2 + self.c, (h * 2 + self.zl) * 2 + self.x), y * 2 + h

    def peer(self, step):
        m = lax.rem(self.m + step, PEERS)
        return (self.g, m), m


def rows(index, count):
    if isinstance(index, int):
        return pl.ds(index * count, count)
    return pl.ds(pl.multiple_of(index * count, count), count)


def remote(src, dst, send, recv, device):
    return pltpu.make_async_remote_copy(
        src_ref=src,
        dst_ref=dst,
        send_sem=send,
        recv_sem=recv,
        device_id=device,
        device_id_type=MESH,
    )


def greet(devices):
    barrier = pltpu.get_barrier_semaphore()
    for device in devices:
        pl.semaphore_signal(barrier, inc=1, device_id=device, device_id_type=MESH)
    pl.semaphore_wait(barrier, len(devices))


def dot(a, b):
    return jnp.dot(a, b, preferred_element_type=jnp.float32)


def dot_t(a, b):
    return lax.dot_general(a, b, (((1,), (1,)), ((), ())), preferred_element_type=jnp.float32)


def t_dot(a, b):
    return lax.dot_general(a, b, (((0,), (0,)), ((), ())), preferred_element_type=jnp.float32)


def loop(count, step, unroll=1):
    def turn(i, carry):
        for n in range(unroll):
            step(i * unroll + n)
        return carry

    if count == unroll:
        turn(0, 0)
    else:
        lax.fori_loop(0, count // unroll, turn, 0)


def mean_of(value):
    return jnp.sum(value, axis=-1, keepdims=True) * (1.0 / D)


def sum_rows(value):
    return jnp.sum(value, axis=0, keepdims=True)


def placing(target, keep_mask, capacity):
    count, groups = target.shape[0], capacity.shape[0]
    aims = [target[s] for s in range(count)]
    flags = [keep_mask[s] for s in range(count)]
    limits = [capacity[k] for k in range(groups)]
    placed = []
    for s in range(count):
        rank = jnp.int32(0)
        for before in range(s):
            rank = rank + flags[before] * (aims[before] == aims[s]).astype(jnp.int32)
        placed.append(
            [
                (
                    flags[s]
                    * (aims[s] == k).astype(jnp.int32)
                    * (rank == n).astype(jnp.int32)
                    * (rank < limits[k]).astype(jnp.int32)
                ).astype(jnp.float32)
                for k in range(groups)
                for n in range(SLOTS)
            ]
        )
    return placed


class Heads:
    def __init__(self):
        row = lax.broadcasted_iota(jnp.int32, (2 * LANES, LANES), 0)
        col = lax.broadcasted_iota(jnp.int32, (2 * LANES, LANES), 1)
        self.same = lax.rem(lax.div(row, SEQ), 2) == lax.div(col, SEQ)
        self.first = col[:LANES] < HEAD
        lane = lax.broadcasted_iota(jnp.int32, (1, LANES), 1)
        self.masks = [
            (lane < HEAD).astype(jnp.float32).astype(jnp.bfloat16),
            (lane >= HEAD).astype(jnp.float32).astype(jnp.bfloat16),
        ]

    def stack(self, pair):
        return jnp.concatenate([pair * mask for mask in self.masks], axis=0)

    def join(self, both):
        return jnp.where(self.first, both[:LANES], both[LANES:]).astype(jnp.bfloat16)

    def weigh(self, q, k):
        scores = jnp.where(self.same, dot_t(q, k) * HEAD ** (-0.5), -3.0e38)
        largest = jnp.max(scores, axis=-1, keepdims=True)
        shifted = jnp.exp(scores - largest)
        return shifted / jnp.sum(shifted, axis=-1, keepdims=True)


CHUNK = 512
CHUNKS = FF // CHUNK
PAIR = 2 * CHUNK
BASE = CHUNKS * PAIR
SPANS = ((CHUNK, CHUNK),) + tuple((i * PAIR, PAIR) for i in range(1, CHUNKS)) + (
    (BASE, D),
    (BASE + D, D),
    (BASE + 2 * D, D),
    (BASE + 3 * D, D + LANES),
    (0, CHUNK),
)
OUT_PIECE, QUERY_PIECE, KEY_PIECE, VALUE_PIECE = range(CHUNKS, CHUNKS + 4)
UP_PIECE = CHUNKS + 4
PIECES = CHUNKS + 5
Z_FIRST = (UP_PIECE,)
RING = 2
HALF = 384
SHARD_AT = 2 * LANES
STAT_F = 4 * FF + 2 * LANES
STAT_A = 8 * D + 2 * LANES
ATTENTION_AT = (BASE + D, BASE + 2 * D, BASE + 3 * D, BASE)


def forward_phase(spot, r):
    low, full = jnp.bfloat16, jnp.float32
    count = r.diag.shape[0]
    group_count = r.capacity.shape[0]
    target, keep_mask, capacity, vectors = r.target, r.keep_mask, r.capacity, r.vectors
    fa, f1, f2, xt, ot, ht, dft, qkv, g, gp = r.fa, r.f1, r.f2, r.xt, r.ot, r.ht, r.dft, r.qkv, r.g, r.gp
    n1, inv, dr, df, vt, vg, x, dy, o, h1, hb = r.n1, r.inv, r.dr, r.df, r.vt, r.vg, r.x, r.dy, r.o, r.h1, r.hb
    qb, bu, square, acc, total = r.qb, r.bu, r.square, r.acc, r.total
    swap_s, swap_r, x_s, x_r, z_s, z_r, d_s, d_r = r.swap_s, r.swap_r, r.x_s, r.x_r, r.z_s, r.z_r, r.d_s, r.d_r
    c_s, c_r, t_s, t_r, own_sem, keep_sem, load_sem = r.c_s, r.c_r, r.t_s, r.t_r, r.own_sem, r.keep_sem, r.load_sem

    def raw(block):
        return (n1, dr, h1)[block // 5].at[pl.ds(block % 5 * count, count)]

    def load_weights(block):
        src = r.wa.at[block] if block < 4 else r.wf.at[block // 4 - 1, :, pl.ds(block % 4 * D, D)]
        return pltpu.make_async_copy(src, raw(block), load_sem.at[block])

    def load_tokens(src, s):
        return pltpu.make_async_copy(
            src.at[pl.ds(s * SEQ, SEQ)], total.at[pl.ds(0, SEQ), pl.ds(s * D, D)], load_sem.at[12 + s]
        )

    for block in range(4):
        load_weights(block).start()
    for s in range(target.shape[0]):
        load_tokens(r.layer_in, s).start()
    for block in range(4, 12):
        load_weights(block).start()
    square[...] = jnp.zeros(square.shape, full)
    for row in range(12):
        square[row : row + 1, pl.ds(0, count)] = vectors[row]
    acc[pl.ds(SHARD_AT, count), pl.ds(VEC, LANES)] = square[...].T[:count].astype(low)
    placed = placing(target, keep_mask, capacity)
    r.greet()
    firsts, widths, fulls = (0, WIDE, WIDE + FF), (WIDE, FF, FF), (fa, f1, f2)
    shards = [acc.at[pl.ds(SHARD_AT, count), pl.ds(*span)] for span in zip(firsts, widths)]
    pieces = range(3)
    away = jnp.logical_not(spot.home)

    def swap(p):
        return remote(
            shards[p], fulls[p].at[rows(spot.m, count)], swap_s.at[p], swap_r.at[p], spot.partner
        )

    def keep(p):
        return pltpu.make_async_copy(shards[p], fulls[p].at[rows(spot.r, count)], own_sem.at[p])

    def hop(p, shard, send, recv, device):
        view = fulls[p].at[rows(shard, count)]
        return remote(view, view, send, recv, device)

    def over_x(p, shard):
        return hop(p, shard, x_s.at[p], x_r.at[p], spot.across_x)

    def over_z(p, shard):
        return hop(p, shard, z_s.at[p], z_r.at[p], spot.across_z)

    def diagonal(p, shard):
        return hop(p, shard, d_s.at[p], d_r.at[p], spot.across_x)

    def over_core(p, n, shard):
        return hop(p, shard, c_s.at[p, n], c_r.at[p, n], spot.across_core)

    routed = (x, dy)

    def token(a, n):
        device, k = spot.router(n)
        return remote(
            acc.at[pl.ds(a * LANES, LANES), rows(k, D)],
            routed[a].at[pl.ds(n * LANES, LANES)],
            t_s.at[a, n],
            t_r.at[a, n],
            device,
        )

    def token_keep(a):
        return pltpu.make_async_copy(
            acc.at[pl.ds(a * LANES, LANES), rows(spot.k, D)],
            routed[a].at[pl.ds(0, LANES)],
            keep_sem.at[a],
        )

    mine = spot.r
    by_x, by_z, by_both = spot.shard(dx=1), spot.shard(dz=1), spot.shard(dz=1, dx=1)

    def lead(p):
        over_x(p, mine).start()
        over_z(p, mine).start()
        over_core(p, 0, mine).start()

    def lead_home(p):
        keep(p).wait()
        lead(p)

    def lead_away(p):
        hop(p, mine, swap_s.at[p], swap_r.at[p], spot.partner).wait_recv()
        lead(p)

    def relay(p):
        over_z(p, by_z).wait_recv()
        diagonal(p, by_z).start()
        over_core(p, 2, by_z).start()
        over_x(p, by_x).wait_recv()
        over_core(p, 1, by_x).start()

    def finish(p):
        diagonal(p, by_both).wait_recv()
        over_core(p, 3, by_both).start()

    def collect_first(p):
        over_core(p, 0, spot.shard(dc=1)).wait_recv()

    def collect_rest(p):
        over_core(p, 1, spot.shard(dc=1, dx=1)).wait_recv()
        over_core(p, 2, spot.shard(dc=1, dz=1)).wait_recv()
        over_core(p, 3, spot.shard(dc=1, dz=1, dx=1)).wait_recv()

    def cast(p, block):
        load_weights(block).wait()
        at = firsts[p] + block % 4 * D
        acc[pl.ds(SHARD_AT, count), pl.ds(at, D)] = raw(block)[...].astype(low)

    for block in range(4):
        cast(0, block)

    @pl.when(away)
    def _():
        swap(0).start()

    @pl.when(spot.home)
    def _():
        keep(0).start()

    for p in (1, 2):
        for j in range(4):
            cast(p, p * 4 + j)

        @pl.when(spot.home)
        def _():
            lead_home(p - 1)
            keep(p).start()

    @pl.when(spot.home)
    def _():
        lead_home(2)

    def choose(a):
        def part(n):
            parts = [total[rows(n, 16), pl.ds(s * D, D)] for s in range(len(placed))]
            for slot in range(2 * group_count):
                value = sum(places[slot] * one for places, one in zip(placed, parts))
                at = pl.multiple_of(a * LANES + slot % 2 * SEQ + n * 16, 16)
                acc[pl.ds(at, 16), pl.ds(slot // 2 * D, D)] = value.astype(low)

        loop(SEQ // 16, part)

    for s in range(target.shape[0]):
        load_tokens(r.layer_in, s).wait()
    choose(0)
    for s in range(target.shape[0]):
        load_tokens(r.cotangent, s).start()
    token_keep(0).start()
    token(0, 1).start()

    @pl.when(away)
    def _():
        lead_away(0)
        swap(1).start()

    @pl.when(spot.home)
    def _():
        relay(0)
        finish(0)

    collect_first(0)
    token(0, 2).start()
    token(0, 3).start()
    for s in range(target.shape[0]):
        load_tokens(r.cotangent, s).wait()
    choose(1)
    square[...] = jnp.zeros(square.shape, full)
    for n, part in enumerate((vectors, r.vector_moments, r.row_moments)):
        for row in range(part.shape[0]):
            square[row : row + 1, pl.ds(0, count)] = part[row]
        r.small[n] = square[...].T[:count]

    @pl.when(away)
    def _():
        relay(0)
        finish(0)

    @pl.when(spot.home)
    def _():
        relay(1)
        finish(1)

    def turn(src, dst, i):
        block = rows(i, LANES)
        turned = src[block, :].T
        dst[rows(1 - spot.c, HALF), block] = turned[:HALF]
        dst[rows(spot.c, HALF), block] = turned[HALF:]

    token_keep(0).wait()
    token(0, 1).wait_recv()
    turn(x, xt, 0)
    turn(x, xt, 1)
    collect_rest(0)
    vt[...] = fa[:, pl.ds(VEC, LANES)].astype(full).T[:16]
    qb[:, pl.ds(0, D)] = vt[0:1]
    qb[:, pl.ds(D, D)] = jnp.zeros((1, D), full)
    qb[:, pl.ds(2 * D, D)] = vt[1:2]
    for i in range(4):
        bu[:, pl.ds(i * D, D)] = vt[8 + i : 9 + i]

    def project(first, j):
        cols = rows(j, 256)
        at = pl.ds(first, 256)
        qkv[at, cols] = (dot(x[at, :], fa[:, cols]) + qb[:, cols]).astype(low)

    heads = Heads()

    def attend(block, j):
        at = pl.ds(block * LANES, LANES)
        q = qkv[at, rows(j, LANES)]
        k = qkv[at, rows(j + 6, LANES)]
        v = qkv[at, rows(j + 12, LANES)]
        weights = heads.weigh(heads.stack(q), k).astype(low)
        o[at, rows(j, LANES)] = heads.join(dot(weights, v))

    def attend_block(block):
        def part(n):
            for j in range(3):
                attend(block, n * 3 + j)

        loop(2, part)

    loop(QKV // 256, functools.partial(project, 0), 3)

    @pl.when(spot.home)
    def _():
        relay(2)

    attend_block(0)
    attend_block(1)

    @pl.when(spot.home)
    def _():
        finish(2)

    token(0, 2).wait_recv()
    token(0, 3).wait_recv()
    loop(QKV // 256, functools.partial(project, 256), 3)

    @pl.when(away)
    def _():
        lead_away(1)
        swap(2).start()

    attend_block(2)
    attend_block(3)

    @pl.when(away)
    def _():
        relay(1)

    def attention_out(j):
        h1[:, rows(j, 256)] = dot(o[...], fa[:, pl.ds(QKV + j * 256, 256)])

    loop(D // 256, attention_out, 3)

    def first_norm(i):
        for n in range(2):
            at = pl.ds(pl.multiple_of(i * 64 + n * 32, 32), 32)
            stream = x[at, :].astype(full) + (h1[at, :] + vt[2:3])
            center = stream - mean_of(stream)
            inverse = lax.rsqrt(mean_of(center * center) + epsilon)
            normed = center * inverse
            n1[at, :] = normed
            inv[at, :] = jnp.broadcast_to(inverse, (32, LANES))
            value = normed * vt[3:4] + vt[4:5]
            h1[at, :] = value
            hb[at, :] = value.astype(low)

    loop(TOKENS // 64, first_norm)

    @pl.when(away)
    def _():
        lead_away(2)
        finish(1)

    collect_first(2)
    token_keep(1).start()
    token(1, 1).start()
    collect_first(1)
    collect_rest(1)

    def rise(j, dst):
        dr[:, pl.ds(dst * 256, 256)] = dot(hb[...], f1[:, rows(j, 256)])

    def bend(j, src):
        cols = rows(j, 256)
        for i in range(TOKENS // 32):
            at = pl.ds(i * 32, 32)
            u = dr[at, pl.ds(src * 256, 256)] + bu[:, cols]
            below = 0.5 + 0.5 * lax.erf(u * (0.5**0.5))
            slope = below + u * (jnp.exp(-0.5 * u * u) * 0.3989422804014327)
            g[at, cols] = (u * below).astype(low)
            gp[at, cols] = slope.astype(low)

    rise(0, 0)

    def up(t):
        rise(2 * t + 1, 1)
        bend(2 * t, 0)
        rise(lax.rem(2 * t + 2, FF // 256), 0)
        bend(2 * t + 1, 1)

    def up_some(first):
        loop(2, lambda t: up(t + first))

    up_some(0)

    @pl.when(away)
    def _():
        relay(2)

    token(1, 2).start()
    token(1, 3).start()
    up_some(2)

    @pl.when(away)
    def _():
        finish(2)

    up_some(4)
    for i in range(4):
        if i >= 2:
            turn(x, xt, i)
        turn(hb, ht, i)
        turn(o, ot, i)
    def down(half):
        at = rows(half, D // 2)
        dr[:, at] = dot_t(g[:, pl.ds(0, D)], f2[at, pl.ds(0, D)])

        def more(n):
            part = rows(n + 1, D)
            dr[:, at] += dot_t(g[:, part], f2[at, part])

        loop(FF // D - 1, more, 3)

    @pl.when(away)
    def _():
        collect_rest(2)

    down(spot.h)

    @pl.when(spot.home)
    def _():
        collect_rest(2)

    down(1 - spot.h)
    token_keep(1).wait()
    token(1, 1).wait_recv()
    vg[...] = jnp.zeros(vg.shape, full)

    def second_norm(i):
        sums = []
        for n in range(4):
            at = pl.ds(pl.multiple_of(i * LANES + n * 32, 32), 32)
            stream = h1[at, :] + (dr[at, :] + vt[5:6])
            center = stream - mean_of(stream)
            inverse = lax.rsqrt(mean_of(center * center) + epsilon)
            normed = center * inverse
            result = (normed * vt[6:7] + vt[7:8]).astype(low)
            upstream = dy[at, :].astype(full)
            dy[at, :] = result
            scaled = upstream * vt[6:7]
            back = inverse * (scaled - mean_of(scaled) - normed * mean_of(scaled * normed))
            dr[at, :] = back
            rounded = back.astype(low)
            df[at, :] = rounded
            sums.append((sum_rows(rounded.astype(full)), sum_rows(upstream * normed), sum_rows(upstream)))
        for row, parts in enumerate(zip(*sums)):
            vg[5 + row : 6 + row] += sum(parts)
        turn(df, dft, i)

    loop(2, second_norm)
    token(1, 2).wait_recv()
    token(1, 3).wait_recv()
    loop(2, lambda i: second_norm(i + 2))
    for a in (0, 1):
        for n in (1, 2, 3):
            token(a, n).wait_send()

    @pl.when(away)
    def _():
        for p in pieces:
            swap(p).wait_send()

    def settle():
        for p in pieces:
            over_x(p, mine).wait_send()
            over_z(p, mine).wait_send()
            diagonal(p, by_z).wait_send()
            for n, shard in enumerate((mine, by_x, by_z, by_both)):
                over_core(p, n, shard).wait_send()

    return settle


def backward_phase(spot, r, settle):
    low, full = jnp.bfloat16, jnp.float32
    count = r.diag.shape[0]
    away = jnp.logical_not(spot.home)
    columns, got_outs, got_grads, sums, by_row, by_column = r.columns, r.got_outs, r.got_grads, r.sums, r.by_row, r.by_column
    vectors_grad, rows_new, columns_new = r.vectors_grad, r.rows_new, r.columns_new
    moments_new, vectors_new, scale_new = r.moments_new, r.vectors_new, r.scale_new
    fa, f1, f2, xt, ot, ht, dft, qkv, g, gp = r.fa, r.f1, r.f2, r.xt, r.ot, r.ht, r.dft, r.qkv, r.g, r.gp
    n1, inv, dr, df, vt, vg, dbu, vt_low, square = r.n1, r.inv, r.dr, r.df, r.vt, r.vg, r.dbu, r.vt_low, r.square
    da, do, dx, du = r.x, r.dy, r.o, r.hb
    acc, other, stage_f, stage_v, total = r.acc, r.other, r.stage_f, r.stage_v, r.total
    diag, from_x, from_z, swapped = r.diag, r.from_x, r.from_z, r.swapped
    stf, sta, srf, sra, small, small_new, spread_row = r.stf, r.sta, r.srf, r.sra, r.small, r.small_new, r.square.at[pl.ds(0, count)]
    out_sem, core_s, core_r, x_s, x_r, z_s, z_r = r.out_sem, r.core_s, r.core_r, r.bx_s, r.bx_r, r.bz_s, r.bz_r
    d_s, d_r, swap_s, swap_r, st_s, st_r, st_keep = r.bd_s, r.bd_r, r.bswap_s, r.bswap_r, r.st_s, r.st_r, r.st_keep
    t_s, t_r, keep_sem = r.bt_s, r.bt_r, r.bkeep_sem
    routed = ((do, got_outs), (dx, got_grads))

    def token(a, n):
        device, k = spot.router(n)
        src, dst = routed[a]
        return remote(
            src.at[pl.ds(n * LANES, LANES)],
            dst.at[rows(spot.k, LANES)],
            t_s.at[a, n],
            t_r.at[a, n],
            device,
        )

    def token_from(a, n):
        device, k = spot.router(n)
        src, dst = routed[a]
        return remote(
            src.at[pl.ds(n * LANES, LANES)],
            dst.at[rows(k, LANES)],
            t_s.at[a, n],
            t_r.at[a, n],
            device,
        )

    def token_keep(a):
        src, dst = routed[a]
        return pltpu.make_async_copy(
            src.at[pl.ds(0, LANES)], dst.at[rows(spot.k, LANES)], keep_sem.at[a]
        )

    def send_tokens(a, which=(1, 2, 3)):
        for n in which:
            token(a, n).start()

    here = spot.zl * 2 + spot.x
    at_x = spot.zl * 2 + 1 - spot.x
    at_z = (1 - spot.zl) * 2 + spot.x
    at_both = (1 - spot.zl) * 2 + 1 - spot.x

    def cols(p):
        if isinstance(p, int):
            return pl.ds(*SPANS[p])
        return rows(p, PAIR)

    def trade(p):
        if isinstance(p, int) and p in (0, UP_PIECE):
            src, dst = stage_f.at[0, :, pl.ds(*SPANS[p])], other.at[:, cols(p)]
        elif isinstance(p, int) and p >= CHUNKS:
            first, width = SPANS[p][0], D
            src = f1.at[pl.ds(0, HALF), pl.ds(first - BASE, width)]
            dst = other.at[:, pl.ds(first, width)]
        else:
            src, dst = stage_f.at[lax.rem(p, RING)], other.at[:, cols(p)]
        return remote(src, dst, core_s.at[p], core_r.at[p], spot.across_core)

    def trade_vectors():
        return remote(
            stage_v,
            other.at[:, pl.ds(BASE + VEC, LANES)],
            core_s.at[PIECES],
            core_r.at[PIECES],
            spot.across_core,
        )

    def over_x(p):
        return remote(
            acc.at[rows(at_x, count), cols(p)],
            from_x.at[:, cols(p)],
            x_s.at[p],
            x_r.at[p],
            spot.across_x,
        )

    def over_z(p):
        return remote(
            acc.at[rows(at_z, count), cols(p)],
            from_z.at[:, cols(p)],
            z_s.at[p],
            z_r.at[p],
            spot.across_z,
        )

    def diagonal(p, z_first):
        return remote(
            acc.at[rows(at_both, count), cols(p)],
            diag.at[:, cols(p)],
            d_s.at[p],
            d_r.at[p],
            spot.across_z if z_first else spot.across_x,
        )

    def swap(p):
        return remote(
            acc.at[rows(here, count), cols(p)],
            swapped.at[:, cols(p)],
            swap_s.at[p],
            swap_r.at[p],
            spot.partner,
        )

    stats, gathered = (stf, sta), (srf, sra)

    def share(n, step):
        device, _ = spot.peer(step)
        return remote(stats[n], gathered[n].at[spot.m], st_s.at[n, step], st_r.at[n, step], device)

    def share_from(n, step):
        device, m = spot.peer((PEERS - step) % PEERS)
        return remote(stats[n], gathered[n].at[m], st_s.at[n, step], st_r.at[n, step], device)

    def share_keep(n):
        return pltpu.make_async_copy(stats[n], gathered[n].at[spot.m], st_keep.at[n])

    def meet(p):
        trade(p).wait_recv()
        if isinstance(p, int) and p == VALUE_PIECE:
            trade_vectors().wait_recv()

        def add(i):
            view = (rows(i, 32), cols(p))
            acc[view] = acc[view] + other[view]

        loop(HALF // 32, add, 3)

        def forward(z_first):
            diagonal(p, z_first).start()
            if z_first:
                over_z(p).start()
            else:
                over_x(p).start()

        forward(isinstance(p, int) and p in Z_FIRST)

    def relay(p):
        z_first = p in Z_FIRST
        diagonal(p, z_first).wait_recv()
        base = at_x if z_first else at_z

        def add(i):
            view = (pl.ds(pl.multiple_of(base * count + i * 32, 32), 32), cols(p))
            acc[view] = acc[view] + diag[rows(i, 32), cols(p)]

        loop(count // 32, add, 3)
        if z_first:
            over_x(p).start()
        else:
            over_z(p).start()

    def close(p):
        over_x(p).wait_recv()
        over_z(p).wait_recv()

        def add(i):
            view = (pl.ds(pl.multiple_of(here * count + i * 16, 16), 16), cols(p))
            part = (rows(i, 16), cols(p))
            done = acc[view].astype(full) + from_x[part].astype(full) + from_z[part].astype(full)
            total[part] = done
            acc[view] = done.astype(low)

        loop(count // 16, add, 3)

        @pl.when(away)
        def _():
            swap(p).start()

    token_keep(0).start()
    send_tokens(0)

    def chunk(c):
        third = lax.rem(c, RING)
        mine = rows(c, CHUNK)

        @pl.when(c == RING)
        def _():
            trade(0).wait_send()
            trade(UP_PIECE).wait_send()

        @pl.when(c > RING)
        def _():
            trade(c - RING).wait_send()

        first = pl.multiple_of(c * PAIR, PAIR)

        def give(left, right, shift, at):
            def part(n):
                n = n * 256
                whole = dot(left[...], right[:, pl.ds(pl.multiple_of(shift + n, 256), 256)]).astype(low)
                stage_f[third, :, pl.ds(pl.multiple_of(at + n, 256), 256)] = whole[:HALF]
                acc[:, pl.ds(pl.multiple_of(first + at + n, 256), 256)] = whole[HALF:]

            loop(CHUNK // 256, part, 2)

        def bend_back(i):
            at, here_c = rows(i, 256), rows(c * 2 + i, 256)
            value = dot(df[...], f2[:, here_c]) * gp[:, here_c].astype(full)
            rounded = value.astype(low)
            du[:, at] = rounded
            dbu[:, here_c] = sum_rows(rounded.astype(full))

        give(dft, g, c * CHUNK, CHUNK)

        @pl.when(c == 0)
        def _():
            trade(0).start()

        loop(CHUNK // 256, bend_back, 2)

        @pl.when(c == 0)
        def _():
            meet(0)

        @pl.when(c >= 2)
        def _():
            meet(c - 1)

        give(ht, du, 0, 0)

        @pl.when(c == 0)
        def _():
            trade(UP_PIECE).start()

        @pl.when(c > 0)
        def _():
            trade(c).start()
        def lift(i):
            at = rows(i, 256)
            dr[:, at] += dot_t(du[:, pl.ds(0, CHUNK)], f1[at, mine])

        loop(D // 256, lift, 3)

        @pl.when(c == 0)
        def _():
            meet(UP_PIECE)

        @pl.when(c == 2)
        def _():
            relay(0)

        @pl.when(c == 3)
        def _():
            relay(UP_PIECE)

        @pl.when(c == 5)
        def _():
            relay(1)
            close(0)
            close(UP_PIECE)

    loop(CHUNKS, chunk)
    meet(CHUNKS - 1)
    for row in range(4):
        vg[8 + row : 9 + row] = dbu[:, pl.ds(row * D, D)]
    settle()

    def first_norm_back(i):
        sums = []
        for n in range(2):
            at = pl.ds(pl.multiple_of(i * 64 + n * 32, 32), 32)
            normed = n1[at, :]
            upstream = dr[at, :]
            scaled = upstream * vt[3:4]
            back = inv[at, :1] * (scaled - mean_of(scaled) - normed * mean_of(scaled * normed))
            dr[at, :] = back
            rounded = back.astype(low)
            da[at, :] = rounded
            sums.append((sum_rows(rounded.astype(full)), sum_rows(upstream * normed), sum_rows(upstream)))
        for row, (one, two) in enumerate(zip(*sums)):
            vg[2 + row : 3 + row] += one + two

    loop(TOKENS // 64, first_norm_back)
    def outer(src, right, first, j):
        def part(n):
            at = n * 256
            whole = dot(src[...], right[:, pl.ds(j * D + at, 256)]).astype(low)
            f1[pl.ds(0, HALF), pl.ds(first - BASE + at, 256)] = whole[:HALF]
            acc[:, pl.ds(first + at, 256)] = whole[HALF:]

        loop(D // 256, part, 3)

    outer(ot, da, BASE, 0)
    trade(OUT_PIECE).start()

    token_keep(0).wait()
    for n in (1, 2, 3):
        token(0, n).wait_send()

    def out_back(j):
        do[:, rows(j, 256)] = dot_t(da[...], fa[rows(j, 256), pl.ds(QKV, D)]).astype(low)

    loop(D // 256, out_back, 3)
    relay(2)
    close(1)
    heads = Heads()

    def attend_back(block, j):
        at = rows(block, LANES)
        q_cols, k_cols, v_cols = rows(j, LANES), rows(j + 6, LANES), rows(j + 12, LANES)
        q, k, v = heads.stack(qkv[at, q_cols]), qkv[at, k_cols], qkv[at, v_cols]
        upstream = heads.stack(do[at, q_cols])
        weights = heads.weigh(q, k)
        grad_w = dot_t(upstream, v)
        centered = grad_w - jnp.sum(grad_w * weights, axis=-1, keepdims=True)
        grad_s = (weights * centered).astype(low)
        qkv[at, q_cols] = heads.join(dot(grad_s, k) * HEAD ** (-0.5))
        qkv[at, k_cols] = (t_dot(grad_s, q) * HEAD ** (-0.5)).astype(low)
        qkv[at, v_cols] = t_dot(weights.astype(low), upstream).astype(low)

    def attend_back_block(block):
        def part(n):
            for j in range(3):
                attend_back(block, n * 3 + j)

        loop(2, part)

    attend_back_block(0)
    meet(OUT_PIECE)
    relay(3)
    attend_back_block(1)
    close(2)
    attend_back_block(2)
    relay(4)
    close(3)
    attend_back_block(3)
    outer(xt, qkv, BASE + D, 0)
    trade(QUERY_PIECE).start()
    outer(xt, qkv, BASE + 2 * D, 1)
    trade(KEY_PIECE).start()

    def bias_sums(i):
        at = rows(i, LANES)
        vg[0:1] += sum_rows(qkv[at, pl.ds(0, D)].astype(full))
        vg[1:2] += sum_rows(qkv[at, pl.ds(2 * D, D)].astype(full))

    loop(4, bias_sums)
    vt_low[...] = vg[...].T.astype(low)
    stage_v[...] = vt_low[rows(1 - spot.c, HALF), :]
    trade_vectors().start()
    acc[:, pl.ds(BASE + VEC, LANES)] = vt_low[rows(spot.c, HALF), :]
    outer(xt, qkv, BASE + 3 * D, 2)
    trade(VALUE_PIECE).start()
    meet(QUERY_PIECE)
    relay(5)
    close(4)
    meet(KEY_PIECE)

    def input_back(j):
        at = rows(j, 256)

        value = dr[:, at]
        for n in range(3):
            value = value + dot_t(qkv[:, rows(n, D)], fa[at, rows(n, D)])
        dx[:, at] = value.astype(low)

    loop(D // 256, input_back)
    token_keep(1).start()
    send_tokens(1)
    meet(VALUE_PIECE)
    lane = lax.broadcasted_iota(jnp.int32, (1, LANES), 1)
    row_new = {}

    def arrive(p):
        @pl.when(away)
        def _():
            swap(p).wait_recv()
            total[:, cols(p)] = swapped[:, cols(p)].astype(full)

        put(p).start()

    def put(p):
        return pltpu.make_async_copy(total.at[:, cols(p)], sums.at[:, cols(p)], out_sem.at[p])

    def tally_feedforward():
        arrive(UP_PIECE)
        for c in range(CHUNKS):
            arrive(c)
        for w in range(2):
            spread_row[...] = jnp.zeros(spread_row.shape, full)

            def add_squares(c):
                at = pl.ds(pl.multiple_of(c * PAIR + w * CHUNK, CHUNK), CHUNK)
                m = total[:, at]
                held = m * m + tiny_square
                spread_row[:, :1] += jnp.sum(held, axis=1, keepdims=True)
                stf[:, at] = sum_rows(held)

            loop(CHUNKS, add_squares)
            r = DECAY * small[2, :, 4 + w : 5 + w] + KEEP * (spread_row[:, :1] / FF)
            row_new[4 + w] = r
            inverse = 1.0 / r

            def weigh_squares(c):
                first = pl.multiple_of(c * PAIR + w * CHUNK, CHUNK)
                m = total[:, pl.ds(first, CHUNK)]
                stf[:, pl.ds(pl.multiple_of(2 * FF + first, CHUNK), CHUNK)] = sum_rows(m * m * inverse)

            loop(CHUNKS, weigh_squares)
            stf[:, pl.ds(4 * FF + w * LANES, LANES)] = jnp.broadcast_to(sum_rows(r), (1, LANES))
        spread(0)

    def spread(n):
        share_keep(n).start()
        for step in range(1, PEERS):
            share(n, step).start()

    row_sums = [jnp.zeros((1, LANES), full)]

    def tally_matrix(j):
        m = total[:, pl.ds(ATTENTION_AT[j], D)]
        squared = m * m
        held = squared + tiny_square
        mean = jnp.sum(held, axis=1, keepdims=True) / D
        r = DECAY * small[2, :, j : j + 1] + KEEP * mean
        row_new[j] = r
        sta[:, pl.ds(j * D, D)] = sum_rows(held)
        sta[:, pl.ds((4 + j) * D, D)] = sum_rows(squared * (1.0 / r))
        row_sums[0] = jnp.where(lane == j, sum_rows(r), row_sums[0])

    def tally_vectors():
        sta[:, pl.ds(8 * D, LANES)] = row_sums[0]
        m = total[:, pl.ds(BASE + VEC, LANES)]
        renewed = DECAY * small[1] + KEEP * (m * m + tiny_square)
        move = m * lax.rsqrt(renewed)
        small_new[0] = m
        small_new[1] = renewed
        small_new[2] = move
        sta[:, pl.ds(8 * D + LANES, LANES)] = sum_rows(move * move)
        spread(1)

    scale = [jnp.zeros((1, LANES), full)]

    def gathered_sum(n, first, width):
        value = gathered[n][0, :, pl.ds(first, width)]
        for peer in range(1, PEERS):
            value = value + gathered[n][peer, :, pl.ds(first, width)]
        return value

    def take(n):
        share_keep(n).wait()
        for step in range(1, PEERS):
            share_from(n, step).wait_recv()

    def renew(n, index, mean, tiles, column_at, entries):
        weighted = jnp.zeros((1, 1), full)
        for at_stat, at_column, width in tiles:
            here_c = (slice(None), pl.ds(at_column, width))
            c = DECAY * columns[here_c] + KEEP * (gathered_sum(n, at_stat, width) / D)
            columns_new[here_c] = c
            sums = gathered_sum(n, column_at + at_stat, width)
            weighted = weighted + jnp.sum(sums * mean / c, axis=1, keepdims=True)
        size = jnp.sqrt(weighted / entries)
        scale[0] = jnp.where(lane == index, size, scale[0])
        factor = jnp.sqrt(mean) * (matrix_rate / jnp.maximum(1.0, size / clip_level))
        for _, at_column, width in tiles:
            here_c = (slice(None), pl.ds(at_column, width))
            by_column[here_c] = lax.rsqrt(columns_new[here_c]) * factor

    close(5)
    relay(OUT_PIECE)
    relay(QUERY_PIECE)
    close(OUT_PIECE)
    relay(KEY_PIECE)
    tally_feedforward()
    close(QUERY_PIECE)
    relay(VALUE_PIECE)
    arrive(OUT_PIECE)
    tally_matrix(3)
    close(KEY_PIECE)
    arrive(QUERY_PIECE)
    tally_matrix(0)
    close(VALUE_PIECE)
    arrive(KEY_PIECE)
    tally_matrix(1)
    take(0)
    for w in range(2):
        mean = gathered_sum(0, 4 * FF + w * LANES, LANES)[:, :1] / D
        tiles = [
            (c * PAIR + w * CHUNK, 4 * D + w * FF + c * CHUNK, CHUNK) for c in range(CHUNKS)
        ]
        renew(0, 4 + w, mean, tiles, 2 * FF, D * FF)
    arrive(VALUE_PIECE)
    tally_matrix(2)
    tally_vectors()
    take(1)
    extra = gathered_sum(1, 8 * D, LANES)
    for j in range(4):
        renew(1, j, extra[:, j : j + 1] / D, [(j * D, j * D, D)], 4 * D, D * D)
    size = jnp.sqrt(gathered_sum(1, 8 * D + LANES, LANES) / D)
    small_new[3] = small[0] - small_new[2] * (vector_rate / jnp.maximum(1.0, size / clip_level))
    scale_new[...] = jnp.where(lane < 6, scale[0], pltpu.roll(size, 6, 1))[:, : scale_new.shape[1]]
    row_all = jnp.zeros((count, LANES), full)
    lanes = lax.broadcasted_iota(jnp.int32, (count, LANES), 1)
    for j in range(6):
        row_all = jnp.where(lanes == j, row_new[j], row_all)
    small_new[2] = row_all
    by_row[...] = lax.rsqrt(jnp.where(lanes < 6, row_all, 1.0))
    for n, dst in enumerate((vectors_grad, moments_new, rows_new, vectors_new)):
        square[pl.ds(0, count), :] = small_new[n]
        turned = square[...].T
        for row in range(dst.shape[0]):
            dst[row] = turned[row : row + 1, :count]

    for p in range(PIECES):
        if CHUNKS - RING <= p < UP_PIECE:
            trade(p).wait_send()
        diagonal(p, p in Z_FIRST).wait_send()
        over_x(p).wait_send()
        over_z(p).wait_send()
    for n in range(2):
        for step in range(1, PEERS):
            share(n, step).wait_send()

    @pl.when(away)
    def _():
        for p in range(PIECES):
            swap(p).wait_send()

    trade_vectors().wait_send()
    token_keep(1).wait()
    for n in (1, 2, 3):
        token_from(0, n).wait_recv()
        token_from(1, n).wait_recv()
        token(1, n).wait_send()
    for p in range(PIECES):
        put(p).wait()


LAYER_IN = (
    "wa", "wf", "layer_in", "cotangent", "vectors", "row_moments", "vector_moments", "columns", "target", "keep_mask",
    "capacity",
)
LAYER_OUT = (
    "got_outs", "got_grads", "sums", "by_row", "by_column", "vectors_grad", "rows_new", "columns_new", "moments_new",
    "vectors_new", "scale_new",
)


def layer_scratch(count):
    low, full = jnp.bfloat16, jnp.float32
    wide = BASE + WIDE
    dma = pltpu.SemaphoreType.DMA
    buffers = dict(
        fa=((D, WIDE), low),
        f1=((D, FF), low),
        f2=((D, FF), low),
        xt=((D, TOKENS), low),
        ot=((D, TOKENS), low),
        ht=((D, TOKENS), low),
        dft=((D, TOKENS), low),
        qkv=((TOKENS, QKV), low),
        g=((TOKENS, FF), low),
        gp=((TOKENS, FF), low),
        n1=((TOKENS, D), full),
        inv=((TOKENS, LANES), full),
        dr=((TOKENS, D), full),
        df=((TOKENS, D), low),
        vt=((16, D), full),
        vg=((LANES, D), full),
        x=((TOKENS, D), low),
        dy=((TOKENS, D), low),
        o=((TOKENS, D), low),
        h1=((TOKENS, D), full),
        hb=((TOKENS, D), low),
        qb=((1, QKV), full),
        bu=((1, FF), full),
        square=((LANES, LANES), full),
        dbu=((1, FF), full),
        vt_low=((D, LANES), low),
        acc=((HALF, wide), low),
        other=((HALF, wide), low),
        stage_f=((RING, HALF, PAIR), low),
        stage_v=((HALF, LANES), low),
        diag=((count, wide), low),
        from_x=((count, wide), low),
        from_z=((count, wide), low),
        swapped=((count, wide), low),
        total=((count, wide), full),
        stf=((1, STAT_F), full),
        sta=((1, STAT_A), full),
        srf=((PEERS, 1, STAT_F), full),
        sra=((PEERS, 1, STAT_A), full),
        small=((3, count, LANES), full),
        small_new=((4, count, LANES), full),
    )
    scratch = {name: pltpu.VMEM(*one) for name, one in buffers.items()}
    for name in ("swap", "x", "z", "d"):
        for end in ("s", "r"):
            scratch[f"{name}_{end}"] = dma((3,))
            scratch[f"b{name}_{end}"] = dma((PIECES,))
    for end in ("s", "r"):
        scratch[f"c_{end}"] = dma((3, 4))
        scratch[f"t_{end}"] = dma((2, 4))
        scratch[f"bt_{end}"] = dma((2, 4))
        scratch[f"core_{end}"] = dma((PIECES + 1,))
        scratch[f"st_{end}"] = dma((2, PEERS))
    scratch.update(
        own_sem=dma((3,)), keep_sem=dma((2,)), bkeep_sem=dma((2,)), load_sem=dma((20,)),
        out_sem=dma((PIECES,)), st_keep=dma((2,)),
    )
    return scratch


def layer_kernel(names, *refs):
    r = types.SimpleNamespace(**dict(zip(names, refs)))
    spot = Spot()
    r.greet = lambda: greet(
        [spot.across_core, spot.partner]
        + [spot.router(n)[0] for n in (1, 2, 3)]
        + [spot.peer(step)[0] for step in range(1, PEERS)]
    )
    settle = forward_phase(spot, r)
    backward_phase(spot, r, settle)


def layer(wa, wf, layer_in, cotangent, vectors, row_moments, vector_moments, columns, *routing):
    low, full = jnp.bfloat16, jnp.float32
    count = wa.shape[1]
    sds = jax.ShapeDtypeStruct
    scratch = layer_scratch(count)
    return pl.pallas_call(
        functools.partial(layer_kernel, LAYER_IN + LAYER_OUT + tuple(scratch)),
        out_shape=(
            sds((TOKENS, D), low),
            sds((TOKENS, D), low),
            sds((count, BASE + WIDE), full),
            sds((count, LANES), full),
            sds(columns.shape, full),
            sds(vectors.shape, full),
            sds(row_moments.shape, full),
            sds(columns.shape, full),
            sds(vectors.shape, full),
            sds(vectors.shape, full),
            sds((1, 18), full),
        ),
        in_specs=[ANY] * 4 + [VMEM] * 4 + [SMEM] * 3,
        out_specs=(ANY,) * 3 + (VMEM,) * 8,
        scratch_shapes=list(scratch.values()),
        compiler_params=pltpu.CompilerParams(
            collective_id=0, has_side_effects=True, vmem_limit_bytes=LIMIT
        ),
        name="layer",
    )(wa, wf, layer_in, cotangent, vectors, row_moments, vector_moments, columns, *routing)


WIDTH = 1024


def finish_kernel(
    target, keep_mask, capacity, outs, grads, layer_in, cotangent, sums_f, sums_a, wa, wf, by_row, by_f1, by_f2, by_a,
    vectors_grad_i, rows_i, columns_i, moments_i, vectors_i, scale_i,
    layer_out, input_grad, ga, gf, ua, uf, vectors_grad, rows_new, columns_new, moments_new, vectors_new, scale,
):
    step = pl.program_id(0)
    for n in range(2):
        at = step * 2 + n
        aim = target[at]
        rank = jnp.int32(0)
        for s in range(target.shape[0]):
            same = (target[s] == aim) & (keep_mask[s] == 1) & (s < at)
            rank = rank + same.astype(jnp.int32)
        taken = (keep_mask[at] == 1) & (rank < capacity[aim])
        slot = jnp.where(taken, aim * SLOTS + rank, 0)
        here = pl.ds(n * SEQ, SEQ)
        for src, own, dst in ((outs, layer_in, layer_out), (grads, cotangent, input_grad)):
            back = src[rows(slot, SEQ), :].astype(jnp.float32)
            dst[here, :] = jnp.where(taken, back, own[here, :])

    @pl.when(step < FF // WIDTH)
    def _():
        for w, by_column in enumerate((by_f1, by_f2)):
            for n in range(WIDTH // CHUNK):
                at = pl.ds(n * CHUNK, CHUNK)
                m = sums_f[:, pl.ds((2 * n + w) * CHUNK, CHUNK)]
                gf[w, :, at] = m
                uf[w, :, at] = wf[w, :, at] - m * by_row[:, 4 + w : 5 + w] * by_column[:, at]

    for j in range(4):

        @pl.when(step == j)
        def _():
            m = sums_a[...]
            ga[0] = m
            ua[0] = wa[0] - m * by_row[:, j : j + 1] * by_a[...]

    @pl.when(step == 0)
    def _():
        for src, dst in (
            (vectors_grad_i, vectors_grad),
            (rows_i, rows_new),
            (columns_i, columns_new),
            (moments_i, moments_new),
            (vectors_i, vectors_new),
            (scale_i, scale),
        ):
            dst[...] = src[...]


def finish(routing, layer_in, cotangent, wa, wf, results):
    got_outs, got_grads, sums, by_row, by_column, *small = results
    count = wa.shape[1]
    full = jnp.float32

    def whole(value):
        return pl.BlockSpec(value.shape, lambda i: (0,) * len(value.shape))

    def tokens():
        return pl.BlockSpec((2 * SEQ, D), lambda i: (i, 0))

    def matrix():
        return pl.BlockSpec((1, count, D), lambda i: (jnp.minimum(i, 3), 0, 0))

    def chunk():
        return pl.BlockSpec((2, count, WIDTH), lambda i: (0, 0, third(i)))

    def third(i):
        return jnp.minimum(i, FF // WIDTH - 1)

    def column_block(shape, first):
        return pl.BlockSpec(shape, lambda i: (0, first // WIDTH + third(i)))

    return pl.pallas_call(
        finish_kernel,
        grid=(TOKENS // SEQ // 2,),
        out_shape=(
            jax.ShapeDtypeStruct((TOKENS, D), full),
            jax.ShapeDtypeStruct((TOKENS, D), full),
            jax.ShapeDtypeStruct(wa.shape, full),
            jax.ShapeDtypeStruct(wf.shape, full),
            jax.ShapeDtypeStruct(wa.shape, full),
            jax.ShapeDtypeStruct(wf.shape, full),
        )
        + tuple(jax.ShapeDtypeStruct(one.shape, full) for one in small),
        in_specs=[SMEM] * 3
        + [
            whole(got_outs),
            whole(got_grads),
            tokens(),
            tokens(),
            pl.BlockSpec((count, 2 * WIDTH), lambda i: (0, third(i))),
            pl.BlockSpec((count, D), lambda i: (0, BASE // D + lax.rem(jnp.minimum(i, 3) + 1, 4))),
            matrix(),
            chunk(),
            whole(by_row),
            column_block((1, WIDTH), 4 * D),
            column_block((1, WIDTH), 4 * D + FF),
            pl.BlockSpec((1, D), lambda i: (0, jnp.minimum(i, 3))),
        ]
        + [whole(one) for one in small],
        out_specs=(tokens(), tokens(), matrix(), chunk(), matrix(), chunk())
        + tuple(whole(one) for one in small),
        compiler_params=pltpu.CompilerParams(vmem_limit_bytes=LIMIT),
        name="finish",
    )(
        *routing, got_outs, got_grads, layer_in, cotangent, sums, sums, wa, wf, by_row, by_column,
        by_column, by_column, *small,
    )

def fast_body(
    layer_in,
    cotangent,
    target,
    keep_mask,
    capacity,
    attention_weights,
    feedforward_weights,
    vectors,
    row_moments,
    column_moments,
    vector_moments,
):
    inputs, upstream = layer_in.reshape(TOKENS, D), cotangent.reshape(TOKENS, D)
    routing = (target, keep_mask, capacity)
    vectors, row_moments, vector_moments = (
        value.transpose(1, 0, 2) for value in (vectors, row_moments, vector_moments)
    )
    results = layer(
        attention_weights[0],
        feedforward_weights[0],
        inputs,
        upstream,
        vectors,
        row_moments,
        vector_moments,
        column_moments,
        *routing,
    )
    layer_out, input_grad, ga, gf, ua, uf, vectors_grad, rows_new, columns_new, moments_new, vectors_new, scale = finish(
        routing, inputs, upstream, attention_weights[0], feedforward_weights[0], results
    )
    layer_out, input_grad = (value.reshape(layer_in.shape) for value in (layer_out, input_grad))
    return (
        layer_out,
        input_grad,
        ga[None],
        gf[None],
        vectors_grad.transpose(1, 0, 2),
        rows_new.transpose(1, 0, 2),
        columns_new,
        moments_new.transpose(1, 0, 2),
        ua[None],
        uf[None],
        vectors_new.transpose(1, 0, 2),
        scale,
    )


def solution(mesh):
    in_specs = (
        P(("group", "mp"), None, None),
        P(("group", "mp"), None, None),
        P(("group", "mp")),
        P(("group", "mp")),
        P(),
        P("group", None, "mp", None),
        P("group", None, "mp", None),
        P("group", None, "mp"),
        P("group", None, "mp"),
        P("group", None),
        P("group", None, "mp"),
    )
    out_specs = (
        P(("group", "mp"), None, None),
        P(("group", "mp"), None, None),
        P("group", None, "mp", None),
        P("group", None, "mp", None),
        P("group", None, "mp"),
        P("group", None, "mp"),
        P("group", None),
        P("group", None, "mp"),
        P("group", None, "mp", None),
        P("group", None, "mp", None),
        P("group", None, "mp"),
        P("group", None),
    )
    suited = mesh.shape["group"] == 4 and mesh.shape["mp"] == PEERS
    body = fast_body if suited else generic_body
    return jax.shard_map(body, mesh=mesh, in_specs=in_specs, out_specs=out_specs, check_vma=False)
```

```python
import functools
import types

import jax
import jax.numpy as jnp
from jax import lax
from jax.experimental import pallas as pl
from jax.experimental.pallas import tpu as pltpu
from jax.sharding import PartitionSpec as P

HEADS = 12
SLOTS = 2
STEP = 10


epsilon = 1e-05
tiny_square = 1e-30
clip_level = 1.0
matrix_rate = 0.01
vector_rate = 0.1


def normalize(stream, gains, shifts):
    center = stream - jnp.mean(stream, axis=-1, keepdims=True)
    inverse = lax.rsqrt(jnp.mean(center * center, axis=-1, keepdims=True) + epsilon)
    normed = center * inverse
    return (normed * gains + shifts, normed, inverse)


def normalize_back(upstream, gains, normed, inverse):
    scaled = upstream * gains
    return inverse * (
        scaled
        - jnp.mean(scaled, axis=-1, keepdims=True)
        - normed * jnp.mean(scaled * normed, axis=-1, keepdims=True)
    )


def gelu_exact(tensor):
    return jax.nn.gelu(tensor, approximate=False)


def generic_body(
    layer_in,
    cotangent,
    target,
    keep_mask,
    capacity,
    attention_weights,
    feedforward_weights,
    vectors,
    row_moments,
    column_moments,
    vector_moments,
):
    group_count = lax.axis_size("group")
    local_count = layer_in.shape[0]
    seq_len = layer_in.shape[1]
    model_width = layer_in.shape[2]
    head_dim = model_width // HEADS
    hidden = feedforward_weights.shape[3]
    slot_count = SLOTS
    buffered = group_count * slot_count
    row_total = buffered * seq_len
    score_scale = head_dim ** (-0.5)
    group_ids = jnp.arange(group_count, dtype=jnp.int32)
    aimed_at = (target[:, None] == group_ids[None, :]).astype(jnp.int32)
    wanted = aimed_at * keep_mask[:, None]
    earlier = jnp.cumsum(wanted, axis=0) - wanted
    position = jnp.sum(earlier * aimed_at, axis=1)
    allowed = jnp.sum(aimed_at * capacity[None, :], axis=1)
    admitted = (keep_mask == 1) & (position < allowed)
    placed = target * slot_count + position
    cell_ids = jnp.arange(buffered, dtype=jnp.int32)
    matched = admitted[:, None] & (placed[:, None] == cell_ids[None, :])
    local_ids = jnp.arange(local_count, dtype=jnp.int32)
    source = jnp.sum(jnp.where(matched, local_ids[:, None], 0), axis=0) + jnp.where(
        jnp.any(matched, axis=0), 0, local_count
    )
    blank_row = jnp.zeros((1, seq_len, model_width), jnp.float32)
    send_inputs = jnp.take(jnp.concatenate([layer_in, blank_row], axis=0), source, axis=0).reshape(
        group_count, slot_count, seq_len, model_width
    )
    send_grads = jnp.take(jnp.concatenate([cotangent, blank_row], axis=0), source, axis=0).reshape(
        group_count, slot_count, seq_len, model_width
    )
    got_inputs, got_grads = (
        lax.all_to_all(send_inputs, "group", split_axis=0, concat_axis=0, tiled=True),
        lax.all_to_all(send_grads, "group", split_axis=0, concat_axis=0, tiled=True),
    )
    attention_full, feedforward_full, vectors_full = (
        lax.all_gather(attention_weights[0].astype(jnp.bfloat16), "mp", axis=1, tiled=True),
        lax.all_gather(feedforward_weights[0].astype(jnp.bfloat16), "mp", axis=1, tiled=True),
        lax.all_gather(vectors[0].astype(jnp.bfloat16), "mp", axis=1, tiled=True),
    )
    vector_rows = vectors_full.astype(jnp.float32)
    bias_query = vector_rows[0]
    bias_value = vector_rows[1]
    bias_output = vector_rows[2]
    gain_first = vector_rows[3]
    shift_first = vector_rows[4]
    bias_down = vector_rows[5]
    gain_second = vector_rows[6]
    shift_second = vector_rows[7]
    bias_up = vector_rows[8:12].reshape(-1)
    inputs = got_inputs.reshape(row_total, model_width)
    inputs_low = inputs.astype(jnp.bfloat16)
    projected = jnp.einsum(
        "rd,cde->cre", inputs_low, attention_full[:3], preferred_element_type=jnp.float32
    )
    projection_bias = jnp.stack([bias_query, jnp.zeros_like(bias_query), bias_value])
    projected_low = (projected + projection_bias[:, None, :]).astype(jnp.bfloat16)
    queries = projected_low[0].reshape(buffered, seq_len, HEADS, head_dim)
    key_rows = projected_low[1].reshape(buffered, seq_len, HEADS, head_dim)
    values = projected_low[2].reshape(buffered, seq_len, HEADS, head_dim)
    scores = (
        jnp.einsum("nshe,nthe->nhst", queries, key_rows, preferred_element_type=jnp.float32)
        * score_scale
    )
    largest = jnp.max(scores, axis=-1, keepdims=True)
    shifted = jnp.exp(scores - largest)
    totals = jnp.sum(shifted, axis=-1, keepdims=True)
    log_totals = largest + jnp.log(totals)
    weights_low = (shifted / totals).astype(jnp.bfloat16)
    attended = jnp.einsum(
        "nhst,nthe->nshe", weights_low, values, preferred_element_type=jnp.float32
    )
    attended_low = attended.reshape(row_total, model_width).astype(jnp.bfloat16)
    branch = (
        jnp.dot(attended_low, attention_full[3], preferred_element_type=jnp.float32) + bias_output
    )
    first_norm, normed_first, inverse_first = normalize(inputs + branch, gain_first, shift_first)
    first_low = first_norm.astype(jnp.bfloat16)
    before_act = (
        jnp.dot(first_low, feedforward_full[0], preferred_element_type=jnp.float32) + bias_up
    )
    activated = gelu_exact(before_act).astype(jnp.bfloat16)
    down_branch = (
        jnp.einsum("rf,df->rd", activated, feedforward_full[1], preferred_element_type=jnp.float32)
        + bias_down
    )
    output_rows, normed_second, inverse_second = normalize(
        first_norm + down_branch, gain_second, shift_second
    )
    returned = lax.all_to_all(
        output_rows.reshape(group_count, slot_count, seq_len, model_width),
        "group",
        split_axis=0,
        concat_axis=0,
        tiled=True,
    )
    upstream = got_grads.reshape(row_total, model_width)
    grad_gain_second = jnp.sum(upstream * normed_second, axis=0)
    grad_shift_second = jnp.sum(upstream, axis=0)
    grad_second = normalize_back(upstream, gain_second, normed_second, inverse_second)
    grad_down = grad_second.astype(jnp.bfloat16)
    grad_bias_down = jnp.sum(grad_down.astype(jnp.float32), axis=0)
    grad_w_down = jnp.einsum("rd,rf->df", grad_down, activated, preferred_element_type=jnp.float32)
    grad_activated = jnp.dot(grad_down, feedforward_full[1], preferred_element_type=jnp.float32)
    gelu_pull = jax.vjp(gelu_exact, before_act)[1]
    grad_before = gelu_pull(grad_activated)[0].astype(jnp.bfloat16)
    grad_bias_up = jnp.sum(grad_before.astype(jnp.float32), axis=0)
    grad_w_up = jnp.einsum("rd,rf->df", first_low, grad_before, preferred_element_type=jnp.float32)
    grad_first = grad_second + jnp.einsum(
        "rf,df->rd", grad_before, feedforward_full[0], preferred_element_type=jnp.float32
    )
    feedforward_grads = jnp.stack([grad_w_up, grad_w_down])
    grad_gain_first = jnp.sum(grad_first * normed_first, axis=0)
    grad_shift_first = jnp.sum(grad_first, axis=0)
    grad_residual = normalize_back(grad_first, gain_first, normed_first, inverse_first)
    grad_branch = grad_residual.astype(jnp.bfloat16)
    grad_bias_output = jnp.sum(grad_branch.astype(jnp.float32), axis=0)
    grad_w_output = jnp.einsum(
        "rd,re->de", attended_low, grad_branch, preferred_element_type=jnp.float32
    )
    grad_attended = jnp.einsum(
        "re,de->rd", grad_branch, attention_full[3], preferred_element_type=jnp.float32
    )
    grad_heads = grad_attended.astype(jnp.bfloat16).reshape(buffered, seq_len, HEADS, head_dim)
    again = (
        jnp.einsum("nshe,nthe->nhst", queries, key_rows, preferred_element_type=jnp.float32)
        * score_scale
    )
    exact = jnp.exp(again - log_totals)
    grad_values = jnp.einsum(
        "nhst,nshe->nthe",
        exact.astype(jnp.bfloat16),
        grad_heads,
        preferred_element_type=jnp.float32,
    ).astype(jnp.bfloat16)
    grad_weights = jnp.einsum(
        "nshe,nthe->nhst", grad_heads, values, preferred_element_type=jnp.float32
    )
    grad_scores = (
        exact * (grad_weights - jnp.sum(grad_weights * exact, axis=-1, keepdims=True))
    ).astype(jnp.bfloat16)
    grad_queries = (
        jnp.einsum("nhst,nthe->nshe", grad_scores, key_rows, preferred_element_type=jnp.float32)
        * score_scale
    ).astype(jnp.bfloat16)
    grad_keys = (
        jnp.einsum("nhst,nshe->nthe", grad_scores, queries, preferred_element_type=jnp.float32)
        * score_scale
    ).astype(jnp.bfloat16)
    grad_projected = jnp.stack(
        [
            grad_queries.reshape(row_total, model_width),
            grad_keys.reshape(row_total, model_width),
            grad_values.reshape(row_total, model_width),
        ]
    )
    grad_w_projected = jnp.einsum(
        "rd,cre->cde", inputs_low, grad_projected, preferred_element_type=jnp.float32
    )
    grad_inputs = grad_residual + jnp.einsum(
        "cre,cde->rd", grad_projected, attention_full[:3], preferred_element_type=jnp.float32
    )
    grad_bias_projected = jnp.sum(grad_projected.astype(jnp.float32), axis=1)
    grads_back = lax.all_to_all(
        grad_inputs.reshape(group_count, slot_count, seq_len, model_width),
        "group",
        split_axis=0,
        concat_axis=0,
        tiled=True,
    )
    attention_grads = jnp.concatenate([grad_w_projected, grad_w_output[None]], axis=0)
    vector_grads = jnp.concatenate(
        [
            jnp.stack(
                [
                    grad_bias_projected[0],
                    grad_bias_projected[2],
                    grad_bias_output,
                    grad_gain_first,
                    grad_shift_first,
                    grad_bias_down,
                    grad_gain_second,
                    grad_shift_second,
                ]
            ),
            grad_bias_up.reshape(4, model_width),
        ],
        axis=0,
    )
    attention_part, feedforward_part, vectors_part = (
        lax.psum_scatter(attention_grads, "mp", scatter_dimension=1, tiled=True),
        lax.psum_scatter(feedforward_grads, "mp", scatter_dimension=1, tiled=True),
        lax.psum_scatter(vector_grads, "mp", scatter_dimension=1, tiled=True),
    )
    slot_index = jnp.where(admitted, placed, 0)
    layer_out = jnp.where(
        admitted[:, None, None],
        jnp.take(returned.reshape(buffered, seq_len, model_width), slot_index, axis=0),
        layer_in,
    )
    input_grad = jnp.where(
        admitted[:, None, None],
        jnp.take(grads_back.reshape(buffered, seq_len, model_width), slot_index, axis=0),
        cotangent,
    )
    decay_rate = 1.0 - STEP ** (-0.8)
    keep_rate = 1.0 - decay_rate
    square_attention = attention_part * attention_part + tiny_square
    square_feedforward = feedforward_part * feedforward_part + tiny_square
    square_vectors = vectors_part * vectors_part + tiny_square
    rows_attention = decay_rate * row_moments[0, :4] + keep_rate * jnp.mean(
        square_attention, axis=-1
    )
    rows_feedforward = decay_rate * row_moments[0, 4:] + keep_rate * jnp.mean(
        square_feedforward, axis=-1
    )
    renewed_vectors = decay_rate * vector_moments[0] + keep_rate * square_vectors
    step_vectors = vectors_part / jnp.sqrt(renewed_vectors)
    vector_squares = jnp.sum(step_vectors * step_vectors, axis=-1)
    attention_columns = jnp.sum(square_attention, axis=1)
    feedforward_columns = jnp.sum(square_feedforward, axis=1)
    row_sums = jnp.concatenate(
        [jnp.sum(rows_attention, axis=-1), jnp.sum(rows_feedforward, axis=-1)]
    )
    old_attention = column_moments[0, : 4 * model_width].reshape(4, model_width)
    old_feedforward = column_moments[0, 4 * model_width :].reshape(2, hidden)
    attention_sums, feedforward_sums, rows_summed, vector_total = lax.psum(
        (attention_columns, feedforward_columns, row_sums, vector_squares), "mp"
    )
    columns_attention = decay_rate * old_attention + keep_rate * attention_sums / model_width
    columns_feedforward = decay_rate * old_feedforward + keep_rate * feedforward_sums / model_width
    mean_rows = rows_summed / model_width
    step_attention = attention_part / jnp.sqrt(
        rows_attention[:, :, None] * columns_attention[:, None, :] / mean_rows[:4, None, None]
    )
    step_feedforward = feedforward_part / jnp.sqrt(
        rows_feedforward[:, :, None] * columns_feedforward[:, None, :] / mean_rows[4:, None, None]
    )
    attention_total, feedforward_total = lax.psum(
        (
            jnp.sum(step_attention * step_attention, axis=(1, 2)),
            jnp.sum(step_feedforward * step_feedforward, axis=(1, 2)),
        ),
        "mp",
    )
    scale_attention = jnp.sqrt(attention_total / (model_width * model_width))
    scale_feedforward = jnp.sqrt(feedforward_total / (model_width * hidden))
    scale_vectors = jnp.sqrt(vector_total / model_width)
    attention_updated = (
        attention_weights[0]
        - matrix_rate
        * step_attention
        / jnp.maximum(1.0, scale_attention / clip_level)[:, None, None]
    )
    feedforward_updated = (
        feedforward_weights[0]
        - matrix_rate
        * step_feedforward
        / jnp.maximum(1.0, scale_feedforward / clip_level)[:, None, None]
    )
    vectors_updated = (
        vectors[0]
        - vector_rate * step_vectors / jnp.maximum(1.0, scale_vectors / clip_level)[:, None]
    )
    renewed_rows = jnp.concatenate([rows_attention, rows_feedforward], axis=0)
    renewed_columns = jnp.concatenate(
        [columns_attention.reshape(-1), columns_feedforward.reshape(-1)]
    )
    update_scale = jnp.concatenate([scale_attention, scale_feedforward, scale_vectors])
    return (
        layer_out,
        input_grad,
        attention_part[None],
        feedforward_part[None],
        vectors_part[None],
        renewed_rows[None],
        renewed_columns[None],
        renewed_vectors[None],
        attention_updated[None],
        feedforward_updated[None],
        vectors_updated[None],
        update_scale[None],
    )


MESH = pl.DeviceIdType.MESH
ANY = pl.BlockSpec(memory_space=pl.ANY)
VMEM = pl.BlockSpec(memory_space=pltpu.VMEM)
SMEM = pl.BlockSpec(memory_space=pltpu.SMEM)
LANES = 128
PEERS = 8
LIMIT = 63 * 1024 * 1024
D = 768
FF = 3072
QKV = 3 * D
VEC = QKV + D
WIDE = VEC + LANES
SEQ = 64
TOKENS = 512
HEAD = D // HEADS
DECAY = 1.0 - STEP ** (-0.8)
KEEP = 1.0 - DECAY


class Spot:
    def __init__(self):
        g = lax.axis_index("group")
        m = lax.axis_index("mp")
        y, c = lax.div(g, 2), lax.rem(g, 2)
        z, x = lax.div(m, 2), lax.rem(m, 2)
        h, zl = lax.div(z, 2), lax.rem(z, 2)
        self.g, self.m, self.y, self.c, self.x, self.h, self.zl = g, m, y, c, x, h, zl
        self.home = c == h
        self.k = y * 2 + h
        self.r = c * 4 + zl * 2 + x
        self.across_x = (g, m + 1 - 2 * x)
        self.across_z = (g, m + 2 - 4 * zl)
        self.across_core = (g + 1 - 2 * c, m)
        self.partner = (y * 2 + 1 - c, ((1 - h) * 2 + zl) * 2 + x)

    def shard(self, dc=0, dz=0, dx=0):
        c = 1 - self.c if dc else self.c
        zl = 1 - self.zl if dz else self.zl
        x = 1 - self.x if dx else self.x
        return c * 4 + zl * 2 + x

    def router(self, n):
        y = 1 - self.y if n % 2 else self.y
        h = 1 - self.h if n // 2 else self.h
        return (y * 2 + self.c, (h * 2 + self.zl) * 2 + self.x), y * 2 + h

    def peer(self, step):
        m = lax.rem(self.m + step, PEERS)
        return (self.g, m), m


def rows(index, count):
    if isinstance(index, int):
        return pl.ds(index * count, count)
    return pl.ds(pl.multiple_of(index * count, count), count)


def remote(src, dst, send, recv, device):
    return pltpu.make_async_remote_copy(
        src_ref=src,
        dst_ref=dst,
        send_sem=send,
        recv_sem=recv,
        device_id=device,
        device_id_type=MESH,
    )


def greet(devices):
    barrier = pltpu.get_barrier_semaphore()
    for device in devices:
        pl.semaphore_signal(barrier, inc=1, device_id=device, device_id_type=MESH)
    pl.semaphore_wait(barrier, len(devices))


def dot(a, b):
    return jnp.dot(a, b, preferred_element_type=jnp.float32)


def dot_t(a, b):
    return lax.dot_general(a, b, (((1,), (1,)), ((), ())), preferred_element_type=jnp.float32)


def t_dot(a, b):
    return lax.dot_general(a, b, (((0,), (0,)), ((), ())), preferred_element_type=jnp.float32)


def loop(count, step, unroll=1):
    def turn(i, carry):
        for n in range(unroll):
            step(i * unroll + n)
        return carry

    if count == unroll:
        turn(0, 0)
    else:
        lax.fori_loop(0, count // unroll, turn, 0)


def mean_of(value):
    return jnp.sum(value, axis=-1, keepdims=True) * (1.0 / D)


def sum_rows(value):
    return jnp.sum(value, axis=0, keepdims=True)


def placing(target, keep_mask, capacity):
    count, groups = target.shape[0], capacity.shape[0]
    aims = [target[s] for s in range(count)]
    flags = [keep_mask[s] for s in range(count)]
    limits = [capacity[k] for k in range(groups)]
    placed = []
    for s in range(count):
        rank = jnp.int32(0)
        for before in range(s):
            rank = rank + flags[before] * (aims[before] == aims[s]).astype(jnp.int32)
        placed.append(
            [
                (
                    flags[s]
                    * (aims[s] == k).astype(jnp.int32)
                    * (rank == n).astype(jnp.int32)
                    * (rank < limits[k]).astype(jnp.int32)
                ).astype(jnp.float32)
                for k in range(groups)
                for n in range(SLOTS)
            ]
        )
    return placed


class Heads:
    def __init__(self):
        row = lax.broadcasted_iota(jnp.int32, (2 * LANES, LANES), 0)
        col = lax.broadcasted_iota(jnp.int32, (2 * LANES, LANES), 1)
        self.same = lax.rem(lax.div(row, SEQ), 2) == lax.div(col, SEQ)
        self.first = col[:LANES] < HEAD
        lane = lax.broadcasted_iota(jnp.int32, (1, LANES), 1)
        self.masks = [
            (lane < HEAD).astype(jnp.float32).astype(jnp.bfloat16),
            (lane >= HEAD).astype(jnp.float32).astype(jnp.bfloat16),
        ]

    def stack(self, pair):
        return jnp.concatenate([pair * mask for mask in self.masks], axis=0)

    def join(self, both):
        return jnp.where(self.first, both[:LANES], both[LANES:]).astype(jnp.bfloat16)

    def weigh(self, q, k):
        scores = jnp.where(self.same, dot_t(q, k) * HEAD ** (-0.5), -3.0e38)
        largest = jnp.max(scores, axis=-1, keepdims=True)
        shifted = jnp.exp(scores - largest)
        return shifted / jnp.sum(shifted, axis=-1, keepdims=True)


CHUNK = 512
CHUNKS = FF // CHUNK
PAIR = 2 * CHUNK
BASE = CHUNKS * PAIR
SPANS = ((CHUNK, CHUNK),) + tuple((i * PAIR, PAIR) for i in range(1, CHUNKS)) + (
    (BASE, D),
    (BASE + D, D),
    (BASE + 2 * D, D),
    (BASE + 3 * D, 512),
    (BASE + 3 * D + 512, 256 + LANES),
    (0, CHUNK),
)
OUT_PIECE, QUERY_PIECE, KEY_PIECE, VALUE_PIECE, LAST_PIECE, UP_PIECE = range(CHUNKS, CHUNKS + 6)
PIECES = CHUNKS + 6
Z_FIRST = (UP_PIECE,)
RING = 2
HALF = 384
SHARD_AT = 2 * LANES
STAT_F = 4 * FF + 2 * LANES
STAT_A = 6 * D + LANES
STAT_V = 2 * D + 2 * LANES
ATTENTION_AT = (BASE + D, BASE + 2 * D, BASE + 3 * D, BASE)


def forward_phase(spot, r):
    low, full = jnp.bfloat16, jnp.float32
    count = r.diag.shape[0]
    group_count = r.capacity.shape[0]
    target, keep_mask, capacity, vectors = r.target, r.keep_mask, r.capacity, r.vectors
    fa, f1, f2, xt, ot, ht, dft, qkv, g, gp = r.fa, r.f1, r.f2, r.xt, r.ot, r.ht, r.dft, r.qkv, r.g, r.gp
    n1, inv, dr, df, vt, vg, x, dy, o, h1, hb = r.n1, r.inv, r.dr, r.df, r.vt, r.vg, r.x, r.dy, r.o, r.h1, r.hb
    qb, bu, square, acc, total = r.qb, r.bu, r.square, r.acc, r.total
    swap_s, swap_r, x_s, x_r, z_s, z_r, d_s, d_r = r.swap_s, r.swap_r, r.x_s, r.x_r, r.z_s, r.z_r, r.d_s, r.d_r
    c_s, c_r, t_s, t_r, own_sem, keep_sem, load_sem = r.c_s, r.c_r, r.t_s, r.t_r, r.own_sem, r.keep_sem, r.load_sem

    def raw(block):
        return (n1, dr, h1)[block // 5].at[pl.ds(block % 5 * count, count)]

    def load_weights(block):
        src = r.wa.at[block] if block < 4 else r.wf.at[block // 4 - 1, :, pl.ds(block % 4 * D, D)]
        return pltpu.make_async_copy(src, raw(block), load_sem.at[block])

    def load_tokens(src, s):
        return pltpu.make_async_copy(
            src.at[pl.ds(s * SEQ, SEQ)], total.at[pl.ds(0, SEQ), pl.ds(s * D, D)], load_sem.at[12 + s]
        )

    for block in range(4):
        load_weights(block).start()
    for s in range(target.shape[0]):
        load_tokens(r.layer_in, s).start()
    for block in range(4, 12):
        load_weights(block).start()
    square[...] = jnp.zeros(square.shape, full)
    for row in range(12):
        square[row : row + 1, pl.ds(0, count)] = vectors[row]
    acc[pl.ds(SHARD_AT, count), pl.ds(VEC, LANES)] = square[...].T[:count].astype(low)
    placed = placing(target, keep_mask, capacity)
    r.greet()
    firsts, widths, fulls = (0, WIDE, WIDE + FF), (WIDE, FF, FF), (fa, f1, f2)
    shards = [acc.at[pl.ds(SHARD_AT, count), pl.ds(*span)] for span in zip(firsts, widths)]
    pieces = range(3)
    away = jnp.logical_not(spot.home)

    def swap(p):
        return remote(
            shards[p], fulls[p].at[rows(spot.m, count)], swap_s.at[p], swap_r.at[p], spot.partner
        )

    def keep(p):
        return pltpu.make_async_copy(shards[p], fulls[p].at[rows(spot.r, count)], own_sem.at[p])

    def hop(p, shard, send, recv, device):
        view = fulls[p].at[rows(shard, count)]
        return remote(view, view, send, recv, device)

    def over_x(p, shard):
        return hop(p, shard, x_s.at[p], x_r.at[p], spot.across_x)

    def over_z(p, shard):
        return hop(p, shard, z_s.at[p], z_r.at[p], spot.across_z)

    def diagonal(p, shard):
        return hop(p, shard, d_s.at[p], d_r.at[p], spot.across_x)

    def over_core(p, n, shard):
        return hop(p, shard, c_s.at[p, n], c_r.at[p, n], spot.across_core)

    routed = (x, dy)

    def token(a, n):
        device, k = spot.router(n)
        return remote(
            acc.at[pl.ds(a * LANES, LANES), rows(k, D)],
            routed[a].at[pl.ds(n * LANES, LANES)],
            t_s.at[a, n],
            t_r.at[a, n],
            device,
        )

    def token_keep(a):
        return pltpu.make_async_copy(
            acc.at[pl.ds(a * LANES, LANES), rows(spot.k, D)],
            routed[a].at[pl.ds(0, LANES)],
            keep_sem.at[a],
        )

    mine = spot.r
    by_x, by_z, by_both = spot.shard(dx=1), spot.shard(dz=1), spot.shard(dz=1, dx=1)

    def lead(p):
        over_x(p, mine).start()
        over_z(p, mine).start()
        over_core(p, 0, mine).start()

    def lead_home(p):
        keep(p).wait()
        lead(p)

    def lead_away(p):
        hop(p, mine, swap_s.at[p], swap_r.at[p], spot.partner).wait_recv()
        lead(p)

    def relay(p):
        over_z(p, by_z).wait_recv()
        diagonal(p, by_z).start()
        over_core(p, 2, by_z).start()
        over_x(p, by_x).wait_recv()
        over_core(p, 1, by_x).start()

    def finish(p):
        diagonal(p, by_both).wait_recv()
        over_core(p, 3, by_both).start()

    def collect_first(p):
        over_core(p, 0, spot.shard(dc=1)).wait_recv()

    def collect_rest(p):
        over_core(p, 1, spot.shard(dc=1, dx=1)).wait_recv()
        over_core(p, 2, spot.shard(dc=1, dz=1)).wait_recv()
        over_core(p, 3, spot.shard(dc=1, dz=1, dx=1)).wait_recv()

    def cast(p, block):
        load_weights(block).wait()
        at = firsts[p] + block % 4 * D
        acc[pl.ds(SHARD_AT, count), pl.ds(at, D)] = raw(block)[...].astype(low)

    for block in range(4):
        cast(0, block)

    @pl.when(away)
    def _():
        swap(0).start()

    @pl.when(spot.home)
    def _():
        keep(0).start()

    for p in (1, 2):
        for j in range(4):
            cast(p, p * 4 + j)

        @pl.when(spot.home)
        def _():
            lead_home(p - 1)
            keep(p).start()

    @pl.when(spot.home)
    def _():
        lead_home(2)

    def choose(a):
        def part(n):
            parts = [total[rows(n, 16), pl.ds(s * D, D)] for s in range(len(placed))]
            for slot in range(2 * group_count):
                value = sum(places[slot] * one for places, one in zip(placed, parts))
                at = pl.multiple_of(a * LANES + slot % 2 * SEQ + n * 16, 16)
                acc[pl.ds(at, 16), pl.ds(slot // 2 * D, D)] = value.astype(low)

        loop(SEQ // 16, part)

    for s in range(target.shape[0]):
        load_tokens(r.layer_in, s).wait()
    choose(0)
    for s in range(target.shape[0]):
        load_tokens(r.cotangent, s).start()
    token_keep(0).start()
    token(0, 1).start()

    @pl.when(away)
    def _():
        lead_away(0)
        swap(1).start()

    @pl.when(spot.home)
    def _():
        relay(0)
        finish(0)

    collect_first(0)
    token(0, 2).start()
    token(0, 3).start()
    for s in range(target.shape[0]):
        load_tokens(r.cotangent, s).wait()
    choose(1)
    square[...] = jnp.zeros(square.shape, full)
    for n, part in enumerate((vectors, r.vector_moments, r.row_moments)):
        for row in range(part.shape[0]):
            square[row : row + 1, pl.ds(0, count)] = part[row]
        r.small[n] = square[...].T[:count]

    @pl.when(away)
    def _():
        relay(0)
        finish(0)

    @pl.when(spot.home)
    def _():
        relay(1)
        finish(1)

    def turn(src, dst, i):
        block = rows(i, LANES)
        turned = src[block, :].T
        dst[rows(1 - spot.c, HALF), block] = turned[:HALF]
        dst[rows(spot.c, HALF), block] = turned[HALF:]

    token_keep(0).wait()
    token(0, 1).wait_recv()
    turn(x, xt, 0)
    turn(x, xt, 1)
    collect_rest(0)
    vt[...] = fa[:, pl.ds(VEC, LANES)].astype(full).T[:16]
    qb[:, pl.ds(0, D)] = vt[0:1]
    qb[:, pl.ds(D, D)] = jnp.zeros((1, D), full)
    qb[:, pl.ds(2 * D, D)] = vt[1:2]
    for i in range(4):
        bu[:, pl.ds(i * D, D)] = vt[8 + i : 9 + i]

    def project(first, j):
        cols = rows(j, 256)
        at = pl.ds(first, 256)
        qkv[at, cols] = (dot(x[at, :], fa[:, cols]) + qb[:, cols]).astype(low)

    heads = Heads()

    def attend(block, j):
        at = pl.ds(block * LANES, LANES)
        q = qkv[at, rows(j, LANES)]
        k = qkv[at, rows(j + 6, LANES)]
        v = qkv[at, rows(j + 12, LANES)]
        weights = heads.weigh(heads.stack(q), k).astype(low)
        o[at, rows(j, LANES)] = heads.join(dot(weights, v))

    def attend_block(block):
        def part(n):
            for j in range(3):
                attend(block, n * 3 + j)

        loop(2, part)

    loop(QKV // 256, functools.partial(project, 0), 3)

    @pl.when(spot.home)
    def _():
        relay(2)

    attend_block(0)
    attend_block(1)

    @pl.when(spot.home)
    def _():
        finish(2)

    token(0, 2).wait_recv()
    token(0, 3).wait_recv()
    loop(QKV // 256, functools.partial(project, 256), 3)

    @pl.when(away)
    def _():
        lead_away(1)
        swap(2).start()

    attend_block(2)
    attend_block(3)

    @pl.when(away)
    def _():
        relay(1)

    def attention_out(j):
        h1[:, rows(j, 256)] = dot(o[...], fa[:, pl.ds(QKV + j * 256, 256)])

    loop(D // 256, attention_out, 3)

    def first_norm(i):
        for n in range(2):
            at = pl.ds(pl.multiple_of(i * 64 + n * 32, 32), 32)
            stream = x[at, :].astype(full) + (h1[at, :] + vt[2:3])
            center = stream - mean_of(stream)
            inverse = lax.rsqrt(mean_of(center * center) + epsilon)
            normed = center * inverse
            n1[at, :] = normed
            inv[at, :] = jnp.broadcast_to(inverse, (32, LANES))
            value = normed * vt[3:4] + vt[4:5]
            h1[at, :] = value
            hb[at, :] = value.astype(low)

    loop(TOKENS // 64, first_norm)

    @pl.when(away)
    def _():
        lead_away(2)
        finish(1)

    collect_first(2)
    token_keep(1).start()
    token(1, 1).start()
    collect_first(1)
    collect_rest(1)

    def rise(j, dst):
        dr[:, pl.ds(dst * 256, 256)] = dot(hb[...], f1[:, rows(j, 256)])

    def bend(j, src):
        cols = rows(j, 256)
        for i in range(TOKENS // 32):
            at = pl.ds(i * 32, 32)
            u = dr[at, pl.ds(src * 256, 256)] + bu[:, cols]
            below = 0.5 + 0.5 * lax.erf(u * (0.5**0.5))
            slope = below + u * (jnp.exp(-0.5 * u * u) * 0.3989422804014327)
            g[at, cols] = (u * below).astype(low)
            gp[at, cols] = slope.astype(low)

    rise(0, 0)

    def up(t):
        rise(2 * t + 1, 1)
        bend(2 * t, 0)
        rise(lax.rem(2 * t + 2, FF // 256), 0)
        bend(2 * t + 1, 1)

    def up_some(first):
        loop(2, lambda t: up(t + first))

    up_some(0)

    @pl.when(away)
    def _():
        relay(2)

    token(1, 2).start()
    token(1, 3).start()
    up_some(2)

    @pl.when(away)
    def _():
        finish(2)

    up_some(4)
    for i in range(4):
        if i >= 2:
            turn(x, xt, i)
        turn(hb, ht, i)
        turn(o, ot, i)
    def down(half):
        at = rows(half, D // 2)
        dr[:, at] = dot_t(g[:, pl.ds(0, D)], f2[at, pl.ds(0, D)])

        def more(n):
            part = rows(n + 1, D)
            dr[:, at] += dot_t(g[:, part], f2[at, part])

        loop(FF // D - 1, more, 3)

    @pl.when(away)
    def _():
        collect_rest(2)

    down(spot.h)

    @pl.when(spot.home)
    def _():
        collect_rest(2)

    down(1 - spot.h)
    token_keep(1).wait()
    token(1, 1).wait_recv()
    vg[...] = jnp.zeros(vg.shape, full)

    def second_norm(i):
        sums = []
        for n in range(4):
            at = pl.ds(pl.multiple_of(i * LANES + n * 32, 32), 32)
            stream = h1[at, :] + (dr[at, :] + vt[5:6])
            center = stream - mean_of(stream)
            inverse = lax.rsqrt(mean_of(center * center) + epsilon)
            normed = center * inverse
            result = (normed * vt[6:7] + vt[7:8]).astype(low)
            upstream = dy[at, :].astype(full)
            dy[at, :] = result
            scaled = upstream * vt[6:7]
            back = inverse * (scaled - mean_of(scaled) - normed * mean_of(scaled * normed))
            dr[at, :] = back
            rounded = back.astype(low)
            df[at, :] = rounded
            sums.append((sum_rows(rounded.astype(full)), sum_rows(upstream * normed), sum_rows(upstream)))
        for row, parts in enumerate(zip(*sums)):
            vg[5 + row : 6 + row] += sum(parts)
        turn(df, dft, i)

    loop(2, second_norm)
    token(1, 2).wait_recv()
    token(1, 3).wait_recv()
    loop(2, lambda i: second_norm(i + 2))
    for a in (0, 1):
        for n in (1, 2, 3):
            token(a, n).wait_send()

    @pl.when(away)
    def _():
        for p in pieces:
            swap(p).wait_send()

    def settle():
        for p in pieces:
            over_x(p, mine).wait_send()
            over_z(p, mine).wait_send()
            diagonal(p, by_z).wait_send()
            for n, shard in enumerate((mine, by_x, by_z, by_both)):
                over_core(p, n, shard).wait_send()

    return settle


def backward_phase(spot, r, settle):
    low, full = jnp.bfloat16, jnp.float32
    count = r.diag.shape[0]
    away = jnp.logical_not(spot.home)
    columns, got_outs, got_grads, sums, by_row, by_column = r.columns, r.got_outs, r.got_grads, r.sums, r.by_row, r.by_column
    vectors_grad, rows_new, columns_new = r.vectors_grad, r.rows_new, r.columns_new
    moments_new, vectors_new, scale_new = r.moments_new, r.vectors_new, r.scale_new
    fa, f1, f2, xt, ot, ht, dft, qkv, g, gp = r.fa, r.f1, r.f2, r.xt, r.ot, r.ht, r.dft, r.qkv, r.g, r.gp
    n1, inv, dr, df, vt, vg, dbu, vt_low, square = r.n1, r.inv, r.dr, r.df, r.vt, r.vg, r.dbu, r.vt_low, r.square
    da, do, dx, du = r.x, r.dy, r.o, r.hb
    acc, other, stage_f, stage_v, total = r.acc, r.other, r.stage_f, r.stage_v, r.total
    diag, from_x, from_z, swapped = r.diag, r.from_x, r.from_z, r.swapped
    stf, sta, srf, sra, small, small_new, spread_row = r.stf, r.sta, r.srf, r.sra, r.small, r.small_new, r.square.at[pl.ds(0, count)]
    out_sem, core_s, core_r, x_s, x_r, z_s, z_r = r.out_sem, r.core_s, r.core_r, r.bx_s, r.bx_r, r.bz_s, r.bz_r
    d_s, d_r, swap_s, swap_r, st_s, st_r, st_keep = r.bd_s, r.bd_r, r.bswap_s, r.bswap_r, r.st_s, r.st_r, r.st_keep
    t_s, t_r, keep_sem = r.bt_s, r.bt_r, r.bkeep_sem
    routed = ((do, got_outs), (dx, got_grads))

    def token(a, n):
        device, k = spot.router(n)
        src, dst = routed[a]
        return remote(
            src.at[pl.ds(n * LANES, LANES)],
            dst.at[rows(spot.k, LANES)],
            t_s.at[a, n],
            t_r.at[a, n],
            device,
        )

    def token_from(a, n):
        device, k = spot.router(n)
        src, dst = routed[a]
        return remote(
            src.at[pl.ds(n * LANES, LANES)],
            dst.at[rows(k, LANES)],
            t_s.at[a, n],
            t_r.at[a, n],
            device,
        )

    def token_keep(a):
        src, dst = routed[a]
        return pltpu.make_async_copy(
            src.at[pl.ds(0, LANES)], dst.at[rows(spot.k, LANES)], keep_sem.at[a]
        )

    def send_tokens(a, which=(1, 2, 3)):
        for n in which:
            token(a, n).start()

    here = spot.zl * 2 + spot.x
    at_x = spot.zl * 2 + 1 - spot.x
    at_z = (1 - spot.zl) * 2 + spot.x
    at_both = (1 - spot.zl) * 2 + 1 - spot.x

    def cols(p):
        if isinstance(p, int):
            return pl.ds(*SPANS[p])
        return rows(p, PAIR)

    def trade(p):
        if isinstance(p, int) and p in (0, UP_PIECE):
            src, dst = stage_f.at[0, :, pl.ds(*SPANS[p])], other.at[:, cols(p)]
        elif isinstance(p, int) and p >= CHUNKS:
            first, width = SPANS[p]
            width = min(width, BASE + VEC - first)
            src = f1.at[pl.ds(0, HALF), pl.ds(first - BASE, width)]
            dst = other.at[:, pl.ds(first, width)]
        else:
            src, dst = stage_f.at[lax.rem(p, RING)], other.at[:, cols(p)]
        return remote(src, dst, core_s.at[p], core_r.at[p], spot.across_core)

    def trade_vectors():
        return remote(
            stage_v,
            other.at[:, pl.ds(BASE + VEC, LANES)],
            core_s.at[PIECES],
            core_r.at[PIECES],
            spot.across_core,
        )

    def over_x(p):
        return remote(
            acc.at[rows(at_x, count), cols(p)],
            from_x.at[:, cols(p)],
            x_s.at[p],
            x_r.at[p],
            spot.across_x,
        )

    def over_z(p):
        return remote(
            acc.at[rows(at_z, count), cols(p)],
            from_z.at[:, cols(p)],
            z_s.at[p],
            z_r.at[p],
            spot.across_z,
        )

    def diagonal(p, z_first):
        return remote(
            acc.at[rows(at_both, count), cols(p)],
            diag.at[:, cols(p)],
            d_s.at[p],
            d_r.at[p],
            spot.across_z if z_first else spot.across_x,
        )

    def swap(p):
        return remote(
            acc.at[rows(here, count), cols(p)],
            swapped.at[:, cols(p)],
            swap_s.at[p],
            swap_r.at[p],
            spot.partner,
        )

    stats, gathered = (stf, sta, r.stv), (srf, sra, r.srv)

    def share(n, step):
        device, _ = spot.peer(step)
        return remote(stats[n], gathered[n].at[spot.m], st_s.at[n, step], st_r.at[n, step], device)

    def share_from(n, step):
        device, m = spot.peer((PEERS - step) % PEERS)
        return remote(stats[n], gathered[n].at[m], st_s.at[n, step], st_r.at[n, step], device)

    def share_keep(n):
        return pltpu.make_async_copy(stats[n], gathered[n].at[spot.m], st_keep.at[n])

    def meet(p):
        trade(p).wait_recv()
        if isinstance(p, int) and p == LAST_PIECE:
            trade_vectors().wait_recv()

        def add(i):
            view = (rows(i, 32), cols(p))
            acc[view] = acc[view] + other[view]

        loop(HALF // 32, add, 3)

        def forward(z_first):
            diagonal(p, z_first).start()
            if z_first:
                over_z(p).start()
            else:
                over_x(p).start()

        forward(isinstance(p, int) and p in Z_FIRST)

    def relay(p):
        z_first = p in Z_FIRST
        diagonal(p, z_first).wait_recv()
        base = at_x if z_first else at_z

        def add(i):
            view = (pl.ds(pl.multiple_of(base * count + i * 32, 32), 32), cols(p))
            acc[view] = acc[view] + diag[rows(i, 32), cols(p)]

        loop(count // 32, add, 3)
        if z_first:
            over_x(p).start()
        else:
            over_z(p).start()

    def close(p):
        over_x(p).wait_recv()
        over_z(p).wait_recv()

        def add(i):
            view = (pl.ds(pl.multiple_of(here * count + i * 16, 16), 16), cols(p))
            part = (rows(i, 16), cols(p))
            done = acc[view].astype(full) + from_x[part].astype(full) + from_z[part].astype(full)
            total[part] = done
            acc[view] = done.astype(low)

        loop(count // 16, add, 3)

        @pl.when(away)
        def _():
            swap(p).start()

    token_keep(0).start()
    send_tokens(0)

    def chunk(c):
        third = lax.rem(c, RING)
        mine = rows(c, CHUNK)

        @pl.when(c == RING)
        def _():
            trade(0).wait_send()
            trade(UP_PIECE).wait_send()

        @pl.when(c > RING)
        def _():
            trade(c - RING).wait_send()

        first = pl.multiple_of(c * PAIR, PAIR)

        def give(left, right, shift, at):
            def part(n):
                n = n * 256
                whole = dot(left[...], right[:, pl.ds(pl.multiple_of(shift + n, 256), 256)]).astype(low)
                stage_f[third, :, pl.ds(pl.multiple_of(at + n, 256), 256)] = whole[:HALF]
                acc[:, pl.ds(pl.multiple_of(first + at + n, 256), 256)] = whole[HALF:]

            loop(CHUNK // 256, part, 2)

        def bend_back(i):
            at, here_c = rows(i, 256), rows(c * 2 + i, 256)
            value = dot(df[...], f2[:, here_c]) * gp[:, here_c].astype(full)
            rounded = value.astype(low)
            du[:, at] = rounded
            dbu[:, here_c] = sum_rows(rounded.astype(full))

        give(dft, g, c * CHUNK, CHUNK)

        @pl.when(c == 0)
        def _():
            trade(0).start()

        loop(CHUNK // 256, bend_back, 2)

        @pl.when(c == 0)
        def _():
            meet(0)

        @pl.when(c >= 2)
        def _():
            meet(c - 1)

        give(ht, du, 0, 0)

        @pl.when(c == 0)
        def _():
            trade(UP_PIECE).start()

        @pl.when(c > 0)
        def _():
            trade(c).start()
        def lift(i):
            at = rows(i, 256)
            dr[:, at] += dot_t(du[:, pl.ds(0, CHUNK)], f1[at, mine])

        loop(D // 256, lift, 3)

        @pl.when(c == 0)
        def _():
            meet(UP_PIECE)

        @pl.when(c == 2)
        def _():
            relay(0)

        @pl.when(c == 3)
        def _():
            relay(UP_PIECE)

        @pl.when(c == 5)
        def _():
            relay(1)
            close(0)
            close(UP_PIECE)

    loop(CHUNKS, chunk)
    meet(CHUNKS - 1)
    for row in range(4):
        vg[8 + row : 9 + row] = dbu[:, pl.ds(row * D, D)]
    settle()

    def first_norm_back(i):
        sums = []
        for n in range(2):
            at = pl.ds(pl.multiple_of(i * 64 + n * 32, 32), 32)
            normed = n1[at, :]
            upstream = dr[at, :]
            scaled = upstream * vt[3:4]
            back = inv[at, :1] * (scaled - mean_of(scaled) - normed * mean_of(scaled * normed))
            dr[at, :] = back
            rounded = back.astype(low)
            da[at, :] = rounded
            sums.append((sum_rows(rounded.astype(full)), sum_rows(upstream * normed), sum_rows(upstream)))
        for row, (one, two) in enumerate(zip(*sums)):
            vg[2 + row : 3 + row] += one + two

    loop(TOKENS // 64, first_norm_back)
    def outer(src, right, first, j, parts=(0, 1, 2)):
        def part(n):
            at = n * 256
            whole = dot(src[...], right[:, pl.ds(j * D + at, 256)]).astype(low)
            f1[pl.ds(0, HALF), pl.ds(first - BASE + at, 256)] = whole[:HALF]
            acc[:, pl.ds(first + at, 256)] = whole[HALF:]

        for n in parts:
            part(n)

    outer(ot, da, BASE, 0)
    trade(OUT_PIECE).start()

    token_keep(0).wait()
    for n in (1, 2, 3):
        token(0, n).wait_send()

    def out_back(j):
        do[:, rows(j, 256)] = dot_t(da[...], fa[rows(j, 256), pl.ds(QKV, D)]).astype(low)

    loop(D // 256, out_back, 3)
    relay(2)
    close(1)
    heads = Heads()

    def attend_back(block, j):
        at = rows(block, LANES)
        q_cols, k_cols, v_cols = rows(j, LANES), rows(j + 6, LANES), rows(j + 12, LANES)
        q, k, v = heads.stack(qkv[at, q_cols]), qkv[at, k_cols], qkv[at, v_cols]
        upstream = heads.stack(do[at, q_cols])
        weights = heads.weigh(q, k)
        grad_w = dot_t(upstream, v)
        centered = grad_w - jnp.sum(grad_w * weights, axis=-1, keepdims=True)
        grad_s = (weights * centered).astype(low)
        qkv[at, q_cols] = heads.join(dot(grad_s, k) * HEAD ** (-0.5))
        qkv[at, k_cols] = (t_dot(grad_s, q) * HEAD ** (-0.5)).astype(low)
        qkv[at, v_cols] = t_dot(weights.astype(low), upstream).astype(low)

    def attend_back_block(block):
        def part(n):
            for j in range(3):
                attend_back(block, n * 3 + j)

        loop(2, part)

    attend_back_block(0)
    meet(OUT_PIECE)
    relay(3)
    attend_back_block(1)
    close(2)
    attend_back_block(2)
    relay(4)
    close(3)
    attend_back_block(3)
    outer(xt, qkv, BASE + D, 0)
    trade(QUERY_PIECE).start()
    outer(xt, qkv, BASE + 2 * D, 1)
    trade(KEY_PIECE).start()

    def bias_sums(i):
        at = rows(i, LANES)
        vg[0:1] += sum_rows(qkv[at, pl.ds(0, D)].astype(full))
        vg[1:2] += sum_rows(qkv[at, pl.ds(2 * D, D)].astype(full))

    loop(4, bias_sums)
    vt_low[...] = vg[...].T.astype(low)
    stage_v[...] = vt_low[rows(1 - spot.c, HALF), :]
    trade_vectors().start()
    acc[:, pl.ds(BASE + VEC, LANES)] = vt_low[rows(spot.c, HALF), :]
    outer(xt, qkv, BASE + 3 * D, 2, (0, 1))
    trade(VALUE_PIECE).start()
    outer(xt, qkv, BASE + 3 * D, 2, (2,))
    trade(LAST_PIECE).start()
    meet(QUERY_PIECE)
    relay(5)
    close(4)
    meet(KEY_PIECE)

    def input_back(j):
        at = rows(j, 256)

        value = dr[:, at]
        for n in range(3):
            value = value + dot_t(qkv[:, rows(n, D)], fa[at, rows(n, D)])
        dx[:, at] = value.astype(low)

    loop(D // 256, input_back)
    token_keep(1).start()
    send_tokens(1)
    meet(VALUE_PIECE)
    meet(LAST_PIECE)
    lane = lax.broadcasted_iota(jnp.int32, (1, LANES), 1)
    row_new = {}

    def arrive(p):
        @pl.when(away)
        def _():
            swap(p).wait_recv()
            total[:, cols(p)] = swapped[:, cols(p)].astype(full)

        put(p).start()

    def put(p):
        return pltpu.make_async_copy(total.at[:, cols(p)], sums.at[:, cols(p)], out_sem.at[p])

    def tally_feedforward():
        arrive(UP_PIECE)
        for c in range(CHUNKS):
            arrive(c)
        for w in range(2):
            spread_row[...] = jnp.zeros(spread_row.shape, full)

            def add_squares(c):
                at = pl.ds(pl.multiple_of(c * PAIR + w * CHUNK, CHUNK), CHUNK)
                m = total[:, at]
                held = m * m + tiny_square
                spread_row[:, :1] += jnp.sum(held, axis=1, keepdims=True)
                stf[:, at] = sum_rows(held)

            loop(CHUNKS, add_squares)
            moments = DECAY * small[2, :, 4 + w : 5 + w] + KEEP * (spread_row[:, :1] / FF)
            row_new[4 + w] = moments
            inverse = 1.0 / moments

            def weigh_squares(c):
                first = pl.multiple_of(c * PAIR + w * CHUNK, CHUNK)
                m = total[:, pl.ds(first, CHUNK)]
                stf[:, pl.ds(pl.multiple_of(2 * FF + first, CHUNK), CHUNK)] = sum_rows(m * m * inverse)

            loop(CHUNKS, weigh_squares)
            stf[:, pl.ds(4 * FF + w * LANES, LANES)] = jnp.broadcast_to(sum_rows(moments), (1, LANES))
        spread(0)

    def spread(n):
        share_keep(n).start()
        for step in range(1, PEERS):
            share(n, step).start()

    row_sums = [jnp.zeros((1, LANES), full)]

    def tally_matrix(j, st, at, count_in):
        m = total[:, pl.ds(ATTENTION_AT[j], D)]
        squared = m * m
        held = squared + tiny_square
        mean = jnp.sum(held, axis=1, keepdims=True) / D
        moments = DECAY * small[2, :, j : j + 1] + KEEP * mean
        row_new[j] = moments
        st[:, pl.ds(at * D, D)] = sum_rows(held)
        st[:, pl.ds((count_in + at) * D, D)] = sum_rows(squared * (1.0 / moments))
        row_sums[0] = jnp.where(lane == at, sum_rows(moments), row_sums[0])
        if at == count_in - 1:
            st[:, pl.ds(2 * count_in * D, LANES)] = row_sums[0]

    def tally_vectors():
        m = total[:, pl.ds(BASE + VEC, LANES)]
        renewed = DECAY * small[1] + KEEP * (m * m + tiny_square)
        move = m * lax.rsqrt(renewed)
        small_new[0] = m
        small_new[1] = renewed
        small_new[2] = move
        r.stv[:, pl.ds(2 * D + LANES, LANES)] = sum_rows(move * move)

    scale = [jnp.zeros((1, LANES), full)]

    def gathered_sum(n, first, width):
        value = gathered[n][0, :, pl.ds(first, width)]
        for peer in range(1, PEERS):
            value = value + gathered[n][peer, :, pl.ds(first, width)]
        return value

    def take(n):
        share_keep(n).wait()
        for step in range(1, PEERS):
            share_from(n, step).wait_recv()

    def renew(n, index, mean, tiles, column_at, entries):
        weighted = jnp.zeros((1, 1), full)
        for at_stat, at_column, width in tiles:
            here_c = (slice(None), pl.ds(at_column, width))
            c = DECAY * columns[here_c] + KEEP * (gathered_sum(n, at_stat, width) / D)
            columns_new[here_c] = c
            sums = gathered_sum(n, column_at + at_stat, width)
            weighted = weighted + jnp.sum(sums * mean / c, axis=1, keepdims=True)
        size = jnp.sqrt(weighted / entries)
        scale[0] = jnp.where(lane == index, size, scale[0])
        factor = jnp.sqrt(mean) * (matrix_rate / jnp.maximum(1.0, size / clip_level))
        for _, at_column, width in tiles:
            here_c = (slice(None), pl.ds(at_column, width))
            by_column[here_c] = lax.rsqrt(columns_new[here_c]) * factor

    close(5)
    relay(OUT_PIECE)
    relay(QUERY_PIECE)
    close(OUT_PIECE)
    relay(KEY_PIECE)
    tally_feedforward()
    close(QUERY_PIECE)
    relay(VALUE_PIECE)
    arrive(OUT_PIECE)
    tally_matrix(3, sta, 0, 3)
    close(KEY_PIECE)
    relay(LAST_PIECE)
    arrive(QUERY_PIECE)
    tally_matrix(0, sta, 1, 3)
    close(VALUE_PIECE)
    arrive(KEY_PIECE)
    tally_matrix(1, sta, 2, 3)
    spread(1)
    close(LAST_PIECE)
    take(0)
    for w in range(2):
        mean = gathered_sum(0, 4 * FF + w * LANES, LANES)[:, :1] / D
        tiles = [
            (c * PAIR + w * CHUNK, 4 * D + w * FF + c * CHUNK, CHUNK) for c in range(CHUNKS)
        ]
        renew(0, 4 + w, mean, tiles, 2 * FF, D * FF)
    arrive(VALUE_PIECE)
    arrive(LAST_PIECE)
    tally_matrix(2, r.stv, 0, 1)
    tally_vectors()
    spread(2)
    take(1)
    extra = gathered_sum(1, 6 * D, LANES)
    for at, j in enumerate((3, 0, 1)):
        renew(1, j, extra[:, at : at + 1] / D, [(at * D, j * D, D)], 3 * D, D * D)
    take(2)
    extra = gathered_sum(2, 2 * D, LANES)
    renew(2, 2, extra[:, :1] / D, [(0, 2 * D, D)], D, D * D)
    size = jnp.sqrt(gathered_sum(2, 2 * D + LANES, LANES) / D)
    small_new[3] = small[0] - small_new[2] * (vector_rate / jnp.maximum(1.0, size / clip_level))
    scale_new[...] = jnp.where(lane < 6, scale[0], pltpu.roll(size, 6, 1))[:, : scale_new.shape[1]]
    row_all = jnp.zeros((count, LANES), full)
    lanes = lax.broadcasted_iota(jnp.int32, (count, LANES), 1)
    for j in range(6):
        row_all = jnp.where(lanes == j, row_new[j], row_all)
    small_new[2] = row_all
    by_row[...] = lax.rsqrt(jnp.where(lanes < 6, row_all, 1.0))
    for n, dst in enumerate((vectors_grad, moments_new, rows_new, vectors_new)):
        square[pl.ds(0, count), :] = small_new[n]
        turned = square[...].T
        for row in range(dst.shape[0]):
            dst[row] = turned[row : row + 1, :count]

    for p in range(PIECES):
        if CHUNKS - RING <= p < UP_PIECE:
            trade(p).wait_send()
        diagonal(p, p in Z_FIRST).wait_send()
        over_x(p).wait_send()
        over_z(p).wait_send()
    for n in range(3):
        for step in range(1, PEERS):
            share(n, step).wait_send()

    @pl.when(away)
    def _():
        for p in range(PIECES):
            swap(p).wait_send()

    trade_vectors().wait_send()
    token_keep(1).wait()
    for n in (1, 2, 3):
        token_from(0, n).wait_recv()
        token_from(1, n).wait_recv()
        token(1, n).wait_send()
    for p in range(PIECES):
        put(p).wait()


LAYER_IN = (
    "wa", "wf", "layer_in", "cotangent", "vectors", "row_moments", "vector_moments", "columns", "target", "keep_mask",
    "capacity",
)
LAYER_OUT = (
    "got_outs", "got_grads", "sums", "by_row", "by_column", "vectors_grad", "rows_new", "columns_new", "moments_new",
    "vectors_new", "scale_new",
)


def layer_scratch(count):
    low, full = jnp.bfloat16, jnp.float32
    wide = BASE + WIDE
    dma = pltpu.SemaphoreType.DMA
    buffers = dict(
        fa=((D, WIDE), low),
        f1=((D, FF), low),
        f2=((D, FF), low),
        xt=((D, TOKENS), low),
        ot=((D, TOKENS), low),
        ht=((D, TOKENS), low),
        dft=((D, TOKENS), low),
        qkv=((TOKENS, QKV), low),
        g=((TOKENS, FF), low),
        gp=((TOKENS, FF), low),
        n1=((TOKENS, D), full),
        inv=((TOKENS, LANES), full),
        dr=((TOKENS, D), full),
        df=((TOKENS, D), low),
        vt=((16, D), full),
        vg=((LANES, D), full),
        x=((TOKENS, D), low),
        dy=((TOKENS, D), low),
        o=((TOKENS, D), low),
        h1=((TOKENS, D), full),
        hb=((TOKENS, D), low),
        qb=((1, QKV), full),
        bu=((1, FF), full),
        square=((LANES, LANES), full),
        dbu=((1, FF), full),
        vt_low=((D, LANES), low),
        acc=((HALF, wide), low),
        other=((HALF, wide), low),
        stage_f=((RING, HALF, PAIR), low),
        stage_v=((HALF, LANES), low),
        diag=((count, wide), low),
        from_x=((count, wide), low),
        from_z=((count, wide), low),
        swapped=((count, wide), low),
        total=((count, wide), full),
        stf=((1, STAT_F), full),
        sta=((1, STAT_A), full),
        srf=((PEERS, 1, STAT_F), full),
        sra=((PEERS, 1, STAT_A), full),
        stv=((1, STAT_V), full),
        srv=((PEERS, 1, STAT_V), full),
        small=((3, count, LANES), full),
        small_new=((4, count, LANES), full),
    )
    scratch = {name: pltpu.VMEM(*one) for name, one in buffers.items()}
    for name in ("swap", "x", "z", "d"):
        for end in ("s", "r"):
            scratch[f"{name}_{end}"] = dma((3,))
            scratch[f"b{name}_{end}"] = dma((PIECES,))
    for end in ("s", "r"):
        scratch[f"c_{end}"] = dma((3, 4))
        scratch[f"t_{end}"] = dma((2, 4))
        scratch[f"bt_{end}"] = dma((2, 4))
        scratch[f"core_{end}"] = dma((PIECES + 1,))
        scratch[f"st_{end}"] = dma((3, PEERS))
    scratch.update(
        own_sem=dma((3,)), keep_sem=dma((2,)), bkeep_sem=dma((2,)), load_sem=dma((20,)),
        out_sem=dma((PIECES,)), st_keep=dma((3,)),
    )
    return scratch


def layer_kernel(names, *refs):
    r = types.SimpleNamespace(**dict(zip(names, refs)))
    spot = Spot()
    r.greet = lambda: greet(
        [spot.across_core, spot.partner]
        + [spot.router(n)[0] for n in (1, 2, 3)]
        + [spot.peer(step)[0] for step in range(1, PEERS)]
    )
    settle = forward_phase(spot, r)
    backward_phase(spot, r, settle)


def layer(wa, wf, layer_in, cotangent, vectors, row_moments, vector_moments, columns, *routing):
    low, full = jnp.bfloat16, jnp.float32
    count = wa.shape[1]
    sds = jax.ShapeDtypeStruct
    scratch = layer_scratch(count)
    return pl.pallas_call(
        functools.partial(layer_kernel, LAYER_IN + LAYER_OUT + tuple(scratch)),
        out_shape=(
            sds((TOKENS, D), low),
            sds((TOKENS, D), low),
            sds((count, BASE + WIDE), full),
            sds((count, LANES), full),
            sds(columns.shape, full),
            sds(vectors.shape, full),
            sds(row_moments.shape, full),
            sds(columns.shape, full),
            sds(vectors.shape, full),
            sds(vectors.shape, full),
            sds((1, 18), full),
        ),
        in_specs=[ANY] * 4 + [VMEM] * 4 + [SMEM] * 3,
        out_specs=(ANY,) * 3 + (VMEM,) * 8,
        scratch_shapes=list(scratch.values()),
        compiler_params=pltpu.CompilerParams(
            collective_id=0, has_side_effects=True, vmem_limit_bytes=LIMIT
        ),
        name="layer",
    )(wa, wf, layer_in, cotangent, vectors, row_moments, vector_moments, columns, *routing)


WIDTH = 1024


def finish_kernel(
    target, keep_mask, capacity, outs, grads, layer_in, cotangent, sums_f, sums_a, wa, wf, by_row, by_f1, by_f2, by_a,
    vectors_grad_i, rows_i, columns_i, moments_i, vectors_i, scale_i,
    layer_out, input_grad, ga, gf, ua, uf, vectors_grad, rows_new, columns_new, moments_new, vectors_new, scale,
):
    step = pl.program_id(0)
    for n in range(2):
        at = step * 2 + n
        aim = target[at]
        rank = jnp.int32(0)
        for s in range(target.shape[0]):
            same = (target[s] == aim) & (keep_mask[s] == 1) & (s < at)
            rank = rank + same.astype(jnp.int32)
        taken = (keep_mask[at] == 1) & (rank < capacity[aim])
        slot = jnp.where(taken, aim * SLOTS + rank, 0)
        here = pl.ds(n * SEQ, SEQ)
        for src, own, dst in ((outs, layer_in, layer_out), (grads, cotangent, input_grad)):
            back = src[rows(slot, SEQ), :].astype(jnp.float32)
            dst[here, :] = jnp.where(taken, back, own[here, :])

    @pl.when(step < FF // WIDTH)
    def _():
        for w, by_column in enumerate((by_f1, by_f2)):
            for n in range(WIDTH // CHUNK):
                at = pl.ds(n * CHUNK, CHUNK)
                m = sums_f[:, pl.ds((2 * n + w) * CHUNK, CHUNK)]
                gf[w, :, at] = m
                uf[w, :, at] = wf[w, :, at] - m * by_row[:, 4 + w : 5 + w] * by_column[:, at]

    for j in range(4):

        @pl.when(step == j)
        def _():
            m = sums_a[...]
            ga[0] = m
            ua[0] = wa[0] - m * by_row[:, j : j + 1] * by_a[...]

    @pl.when(step == 0)
    def _():
        for src, dst in (
            (vectors_grad_i, vectors_grad),
            (rows_i, rows_new),
            (columns_i, columns_new),
            (moments_i, moments_new),
            (vectors_i, vectors_new),
            (scale_i, scale),
        ):
            dst[...] = src[...]


def finish(routing, layer_in, cotangent, wa, wf, results):
    got_outs, got_grads, sums, by_row, by_column, *small = results
    count = wa.shape[1]
    full = jnp.float32

    def whole(value):
        return pl.BlockSpec(value.shape, lambda i: (0,) * len(value.shape))

    def tokens():
        return pl.BlockSpec((2 * SEQ, D), lambda i: (i, 0))

    def matrix():
        return pl.BlockSpec((1, count, D), lambda i: (jnp.minimum(i, 3), 0, 0))

    def chunk():
        return pl.BlockSpec((2, count, WIDTH), lambda i: (0, 0, third(i)))

    def third(i):
        return jnp.minimum(i, FF // WIDTH - 1)

    def column_block(shape, first):
        return pl.BlockSpec(shape, lambda i: (0, first // WIDTH + third(i)))

    return pl.pallas_call(
        finish_kernel,
        grid=(TOKENS // SEQ // 2,),
        out_shape=(
            jax.ShapeDtypeStruct((TOKENS, D), full),
            jax.ShapeDtypeStruct((TOKENS, D), full),
            jax.ShapeDtypeStruct(wa.shape, full),
            jax.ShapeDtypeStruct(wf.shape, full),
            jax.ShapeDtypeStruct(wa.shape, full),
            jax.ShapeDtypeStruct(wf.shape, full),
        )
        + tuple(jax.ShapeDtypeStruct(one.shape, full) for one in small),
        in_specs=[SMEM] * 3
        + [
            whole(got_outs),
            whole(got_grads),
            tokens(),
            tokens(),
            pl.BlockSpec((count, 2 * WIDTH), lambda i: (0, third(i))),
            pl.BlockSpec((count, D), lambda i: (0, BASE // D + lax.rem(jnp.minimum(i, 3) + 1, 4))),
            matrix(),
            chunk(),
            whole(by_row),
            column_block((1, WIDTH), 4 * D),
            column_block((1, WIDTH), 4 * D + FF),
            pl.BlockSpec((1, D), lambda i: (0, jnp.minimum(i, 3))),
        ]
        + [whole(one) for one in small],
        out_specs=(tokens(), tokens(), matrix(), chunk(), matrix(), chunk())
        + tuple(whole(one) for one in small),
        compiler_params=pltpu.CompilerParams(vmem_limit_bytes=LIMIT),
        name="finish",
    )(
        *routing, got_outs, got_grads, layer_in, cotangent, sums, sums, wa, wf, by_row, by_column,
        by_column, by_column, *small,
    )

def fast_body(
    layer_in,
    cotangent,
    target,
    keep_mask,
    capacity,
    attention_weights,
    feedforward_weights,
    vectors,
    row_moments,
    column_moments,
    vector_moments,
):
    inputs, upstream = layer_in.reshape(TOKENS, D), cotangent.reshape(TOKENS, D)
    routing = (target, keep_mask, capacity)
    vectors, row_moments, vector_moments = (
        value.transpose(1, 0, 2) for value in (vectors, row_moments, vector_moments)
    )
    results = layer(
        attention_weights[0],
        feedforward_weights[0],
        inputs,
        upstream,
        vectors,
        row_moments,
        vector_moments,
        column_moments,
        *routing,
    )
    layer_out, input_grad, ga, gf, ua, uf, vectors_grad, rows_new, columns_new, moments_new, vectors_new, scale = finish(
        routing, inputs, upstream, attention_weights[0], feedforward_weights[0], results
    )
    layer_out, input_grad = (value.reshape(layer_in.shape) for value in (layer_out, input_grad))
    return (
        layer_out,
        input_grad,
        ga[None],
        gf[None],
        vectors_grad.transpose(1, 0, 2),
        rows_new.transpose(1, 0, 2),
        columns_new,
        moments_new.transpose(1, 0, 2),
        ua[None],
        uf[None],
        vectors_new.transpose(1, 0, 2),
        scale,
    )


def solution(mesh):
    in_specs = (
        P(("group", "mp"), None, None),
        P(("group", "mp"), None, None),
        P(("group", "mp")),
        P(("group", "mp")),
        P(),
        P("group", None, "mp", None),
        P("group", None, "mp", None),
        P("group", None, "mp"),
        P("group", None, "mp"),
        P("group", None),
        P("group", None, "mp"),
    )
    out_specs = (
        P(("group", "mp"), None, None),
        P(("group", "mp"), None, None),
        P("group", None, "mp", None),
        P("group", None, "mp", None),
        P("group", None, "mp"),
        P("group", None, "mp"),
        P("group", None),
        P("group", None, "mp"),
        P("group", None, "mp", None),
        P("group", None, "mp", None),
        P("group", None, "mp"),
        P("group", None),
    )
    suited = mesh.shape["group"] == 4 and mesh.shape["mp"] == PEERS
    body = fast_body if suited else generic_body
    return jax.shard_map(body, mesh=mesh, in_specs=in_specs, out_specs=out_specs, check_vma=False)
```

```python
import functools
import types

import jax
import jax.numpy as jnp
from jax import lax
from jax.experimental import pallas as pl
from jax.experimental.pallas import tpu as pltpu
from jax.sharding import PartitionSpec as P

HEADS = 12
SLOTS = 2
STEP = 10


epsilon = 1e-05
tiny_square = 1e-30
clip_level = 1.0
matrix_rate = 0.01
vector_rate = 0.1


def normalize(stream, gains, shifts):
    center = stream - jnp.mean(stream, axis=-1, keepdims=True)
    inverse = lax.rsqrt(jnp.mean(center * center, axis=-1, keepdims=True) + epsilon)
    normed = center * inverse
    return (normed * gains + shifts, normed, inverse)


def normalize_back(upstream, gains, normed, inverse):
    scaled = upstream * gains
    return inverse * (
        scaled
        - jnp.mean(scaled, axis=-1, keepdims=True)
        - normed * jnp.mean(scaled * normed, axis=-1, keepdims=True)
    )


def gelu_exact(tensor):
    return jax.nn.gelu(tensor, approximate=False)


def generic_body(
    layer_in,
    cotangent,
    target,
    keep_mask,
    capacity,
    attention_weights,
    feedforward_weights,
    vectors,
    row_moments,
    column_moments,
    vector_moments,
):
    group_count = lax.axis_size("group")
    local_count = layer_in.shape[0]
    seq_len = layer_in.shape[1]
    model_width = layer_in.shape[2]
    head_dim = model_width // HEADS
    hidden = feedforward_weights.shape[3]
    slot_count = SLOTS
    buffered = group_count * slot_count
    row_total = buffered * seq_len
    score_scale = head_dim ** (-0.5)
    group_ids = jnp.arange(group_count, dtype=jnp.int32)
    aimed_at = (target[:, None] == group_ids[None, :]).astype(jnp.int32)
    wanted = aimed_at * keep_mask[:, None]
    earlier = jnp.cumsum(wanted, axis=0) - wanted
    position = jnp.sum(earlier * aimed_at, axis=1)
    allowed = jnp.sum(aimed_at * capacity[None, :], axis=1)
    admitted = (keep_mask == 1) & (position < allowed)
    placed = target * slot_count + position
    cell_ids = jnp.arange(buffered, dtype=jnp.int32)
    matched = admitted[:, None] & (placed[:, None] == cell_ids[None, :])
    local_ids = jnp.arange(local_count, dtype=jnp.int32)
    source = jnp.sum(jnp.where(matched, local_ids[:, None], 0), axis=0) + jnp.where(
        jnp.any(matched, axis=0), 0, local_count
    )
    blank_row = jnp.zeros((1, seq_len, model_width), jnp.float32)
    send_inputs = jnp.take(jnp.concatenate([layer_in, blank_row], axis=0), source, axis=0).reshape(
        group_count, slot_count, seq_len, model_width
    )
    send_grads = jnp.take(jnp.concatenate([cotangent, blank_row], axis=0), source, axis=0).reshape(
        group_count, slot_count, seq_len, model_width
    )
    got_inputs, got_grads = (
        lax.all_to_all(send_inputs, "group", split_axis=0, concat_axis=0, tiled=True),
        lax.all_to_all(send_grads, "group", split_axis=0, concat_axis=0, tiled=True),
    )
    attention_full, feedforward_full, vectors_full = (
        lax.all_gather(attention_weights[0].astype(jnp.bfloat16), "mp", axis=1, tiled=True),
        lax.all_gather(feedforward_weights[0].astype(jnp.bfloat16), "mp", axis=1, tiled=True),
        lax.all_gather(vectors[0].astype(jnp.bfloat16), "mp", axis=1, tiled=True),
    )
    vector_rows = vectors_full.astype(jnp.float32)
    bias_query = vector_rows[0]
    bias_value = vector_rows[1]
    bias_output = vector_rows[2]
    gain_first = vector_rows[3]
    shift_first = vector_rows[4]
    bias_down = vector_rows[5]
    gain_second = vector_rows[6]
    shift_second = vector_rows[7]
    bias_up = vector_rows[8:12].reshape(-1)
    inputs = got_inputs.reshape(row_total, model_width)
    inputs_low = inputs.astype(jnp.bfloat16)
    projected = jnp.einsum(
        "rd,cde->cre", inputs_low, attention_full[:3], preferred_element_type=jnp.float32
    )
    projection_bias = jnp.stack([bias_query, jnp.zeros_like(bias_query), bias_value])
    projected_low = (projected + projection_bias[:, None, :]).astype(jnp.bfloat16)
    queries = projected_low[0].reshape(buffered, seq_len, HEADS, head_dim)
    key_rows = projected_low[1].reshape(buffered, seq_len, HEADS, head_dim)
    values = projected_low[2].reshape(buffered, seq_len, HEADS, head_dim)
    scores = (
        jnp.einsum("nshe,nthe->nhst", queries, key_rows, preferred_element_type=jnp.float32)
        * score_scale
    )
    largest = jnp.max(scores, axis=-1, keepdims=True)
    shifted = jnp.exp(scores - largest)
    totals = jnp.sum(shifted, axis=-1, keepdims=True)
    log_totals = largest + jnp.log(totals)
    weights_low = (shifted / totals).astype(jnp.bfloat16)
    attended = jnp.einsum(
        "nhst,nthe->nshe", weights_low, values, preferred_element_type=jnp.float32
    )
    attended_low = attended.reshape(row_total, model_width).astype(jnp.bfloat16)
    branch = (
        jnp.dot(attended_low, attention_full[3], preferred_element_type=jnp.float32) + bias_output
    )
    first_norm, normed_first, inverse_first = normalize(inputs + branch, gain_first, shift_first)
    first_low = first_norm.astype(jnp.bfloat16)
    before_act = (
        jnp.dot(first_low, feedforward_full[0], preferred_element_type=jnp.float32) + bias_up
    )
    activated = gelu_exact(before_act).astype(jnp.bfloat16)
    down_branch = (
        jnp.einsum("rf,df->rd", activated, feedforward_full[1], preferred_element_type=jnp.float32)
        + bias_down
    )
    output_rows, normed_second, inverse_second = normalize(
        first_norm + down_branch, gain_second, shift_second
    )
    returned = lax.all_to_all(
        output_rows.reshape(group_count, slot_count, seq_len, model_width),
        "group",
        split_axis=0,
        concat_axis=0,
        tiled=True,
    )
    upstream = got_grads.reshape(row_total, model_width)
    grad_gain_second = jnp.sum(upstream * normed_second, axis=0)
    grad_shift_second = jnp.sum(upstream, axis=0)
    grad_second = normalize_back(upstream, gain_second, normed_second, inverse_second)
    grad_down = grad_second.astype(jnp.bfloat16)
    grad_bias_down = jnp.sum(grad_down.astype(jnp.float32), axis=0)
    grad_w_down = jnp.einsum("rd,rf->df", grad_down, activated, preferred_element_type=jnp.float32)
    grad_activated = jnp.dot(grad_down, feedforward_full[1], preferred_element_type=jnp.float32)
    gelu_pull = jax.vjp(gelu_exact, before_act)[1]
    grad_before = gelu_pull(grad_activated)[0].astype(jnp.bfloat16)
    grad_bias_up = jnp.sum(grad_before.astype(jnp.float32), axis=0)
    grad_w_up = jnp.einsum("rd,rf->df", first_low, grad_before, preferred_element_type=jnp.float32)
    grad_first = grad_second + jnp.einsum(
        "rf,df->rd", grad_before, feedforward_full[0], preferred_element_type=jnp.float32
    )
    feedforward_grads = jnp.stack([grad_w_up, grad_w_down])
    grad_gain_first = jnp.sum(grad_first * normed_first, axis=0)
    grad_shift_first = jnp.sum(grad_first, axis=0)
    grad_residual = normalize_back(grad_first, gain_first, normed_first, inverse_first)
    grad_branch = grad_residual.astype(jnp.bfloat16)
    grad_bias_output = jnp.sum(grad_branch.astype(jnp.float32), axis=0)
    grad_w_output = jnp.einsum(
        "rd,re->de", attended_low, grad_branch, preferred_element_type=jnp.float32
    )
    grad_attended = jnp.einsum(
        "re,de->rd", grad_branch, attention_full[3], preferred_element_type=jnp.float32
    )
    grad_heads = grad_attended.astype(jnp.bfloat16).reshape(buffered, seq_len, HEADS, head_dim)
    again = (
        jnp.einsum("nshe,nthe->nhst", queries, key_rows, preferred_element_type=jnp.float32)
        * score_scale
    )
    exact = jnp.exp(again - log_totals)
    grad_values = jnp.einsum(
        "nhst,nshe->nthe",
        exact.astype(jnp.bfloat16),
        grad_heads,
        preferred_element_type=jnp.float32,
    ).astype(jnp.bfloat16)
    grad_weights = jnp.einsum(
        "nshe,nthe->nhst", grad_heads, values, preferred_element_type=jnp.float32
    )
    grad_scores = (
        exact * (grad_weights - jnp.sum(grad_weights * exact, axis=-1, keepdims=True))
    ).astype(jnp.bfloat16)
    grad_queries = (
        jnp.einsum("nhst,nthe->nshe", grad_scores, key_rows, preferred_element_type=jnp.float32)
        * score_scale
    ).astype(jnp.bfloat16)
    grad_keys = (
        jnp.einsum("nhst,nshe->nthe", grad_scores, queries, preferred_element_type=jnp.float32)
        * score_scale
    ).astype(jnp.bfloat16)
    grad_projected = jnp.stack(
        [
            grad_queries.reshape(row_total, model_width),
            grad_keys.reshape(row_total, model_width),
            grad_values.reshape(row_total, model_width),
        ]
    )
    grad_w_projected = jnp.einsum(
        "rd,cre->cde", inputs_low, grad_projected, preferred_element_type=jnp.float32
    )
    grad_inputs = grad_residual + jnp.einsum(
        "cre,cde->rd", grad_projected, attention_full[:3], preferred_element_type=jnp.float32
    )
    grad_bias_projected = jnp.sum(grad_projected.astype(jnp.float32), axis=1)
    grads_back = lax.all_to_all(
        grad_inputs.reshape(group_count, slot_count, seq_len, model_width),
        "group",
        split_axis=0,
        concat_axis=0,
        tiled=True,
    )
    attention_grads = jnp.concatenate([grad_w_projected, grad_w_output[None]], axis=0)
    vector_grads = jnp.concatenate(
        [
            jnp.stack(
                [
                    grad_bias_projected[0],
                    grad_bias_projected[2],
                    grad_bias_output,
                    grad_gain_first,
                    grad_shift_first,
                    grad_bias_down,
                    grad_gain_second,
                    grad_shift_second,
                ]
            ),
            grad_bias_up.reshape(4, model_width),
        ],
        axis=0,
    )
    attention_part, feedforward_part, vectors_part = (
        lax.psum_scatter(attention_grads, "mp", scatter_dimension=1, tiled=True),
        lax.psum_scatter(feedforward_grads, "mp", scatter_dimension=1, tiled=True),
        lax.psum_scatter(vector_grads, "mp", scatter_dimension=1, tiled=True),
    )
    slot_index = jnp.where(admitted, placed, 0)
    layer_out = jnp.where(
        admitted[:, None, None],
        jnp.take(returned.reshape(buffered, seq_len, model_width), slot_index, axis=0),
        layer_in,
    )
    input_grad = jnp.where(
        admitted[:, None, None],
        jnp.take(grads_back.reshape(buffered, seq_len, model_width), slot_index, axis=0),
        cotangent,
    )
    decay_rate = 1.0 - STEP ** (-0.8)
    keep_rate = 1.0 - decay_rate
    square_attention = attention_part * attention_part + tiny_square
    square_feedforward = feedforward_part * feedforward_part + tiny_square
    square_vectors = vectors_part * vectors_part + tiny_square
    rows_attention = decay_rate * row_moments[0, :4] + keep_rate * jnp.mean(
        square_attention, axis=-1
    )
    rows_feedforward = decay_rate * row_moments[0, 4:] + keep_rate * jnp.mean(
        square_feedforward, axis=-1
    )
    renewed_vectors = decay_rate * vector_moments[0] + keep_rate * square_vectors
    step_vectors = vectors_part / jnp.sqrt(renewed_vectors)
    vector_squares = jnp.sum(step_vectors * step_vectors, axis=-1)
    attention_columns = jnp.sum(square_attention, axis=1)
    feedforward_columns = jnp.sum(square_feedforward, axis=1)
    row_sums = jnp.concatenate(
        [jnp.sum(rows_attention, axis=-1), jnp.sum(rows_feedforward, axis=-1)]
    )
    old_attention = column_moments[0, : 4 * model_width].reshape(4, model_width)
    old_feedforward = column_moments[0, 4 * model_width :].reshape(2, hidden)
    attention_sums, feedforward_sums, rows_summed, vector_total = lax.psum(
        (attention_columns, feedforward_columns, row_sums, vector_squares), "mp"
    )
    columns_attention = decay_rate * old_attention + keep_rate * attention_sums / model_width
    columns_feedforward = decay_rate * old_feedforward + keep_rate * feedforward_sums / model_width
    mean_rows = rows_summed / model_width
    step_attention = attention_part / jnp.sqrt(
        rows_attention[:, :, None] * columns_attention[:, None, :] / mean_rows[:4, None, None]
    )
    step_feedforward = feedforward_part / jnp.sqrt(
        rows_feedforward[:, :, None] * columns_feedforward[:, None, :] / mean_rows[4:, None, None]
    )
    attention_total, feedforward_total = lax.psum(
        (
            jnp.sum(step_attention * step_attention, axis=(1, 2)),
            jnp.sum(step_feedforward * step_feedforward, axis=(1, 2)),
        ),
        "mp",
    )
    scale_attention = jnp.sqrt(attention_total / (model_width * model_width))
    scale_feedforward = jnp.sqrt(feedforward_total / (model_width * hidden))
    scale_vectors = jnp.sqrt(vector_total / model_width)
    attention_updated = (
        attention_weights[0]
        - matrix_rate
        * step_attention
        / jnp.maximum(1.0, scale_attention / clip_level)[:, None, None]
    )
    feedforward_updated = (
        feedforward_weights[0]
        - matrix_rate
        * step_feedforward
        / jnp.maximum(1.0, scale_feedforward / clip_level)[:, None, None]
    )
    vectors_updated = (
        vectors[0]
        - vector_rate * step_vectors / jnp.maximum(1.0, scale_vectors / clip_level)[:, None]
    )
    renewed_rows = jnp.concatenate([rows_attention, rows_feedforward], axis=0)
    renewed_columns = jnp.concatenate(
        [columns_attention.reshape(-1), columns_feedforward.reshape(-1)]
    )
    update_scale = jnp.concatenate([scale_attention, scale_feedforward, scale_vectors])
    return (
        layer_out,
        input_grad,
        attention_part[None],
        feedforward_part[None],
        vectors_part[None],
        renewed_rows[None],
        renewed_columns[None],
        renewed_vectors[None],
        attention_updated[None],
        feedforward_updated[None],
        vectors_updated[None],
        update_scale[None],
    )


MESH = pl.DeviceIdType.MESH
ANY = pl.BlockSpec(memory_space=pl.ANY)
VMEM = pl.BlockSpec(memory_space=pltpu.VMEM)
SMEM = pl.BlockSpec(memory_space=pltpu.SMEM)
LANES = 128
PEERS = 8
LIMIT = 63 * 1024 * 1024
D = 768
FF = 3072
QKV = 3 * D
VEC = QKV + D
WIDE = VEC + LANES
SEQ = 64
TOKENS = 512
HEAD = D // HEADS
DECAY = 1.0 - STEP ** (-0.8)
KEEP = 1.0 - DECAY


class Spot:
    def __init__(self):
        g = lax.axis_index("group")
        m = lax.axis_index("mp")
        y, c = lax.div(g, 2), lax.rem(g, 2)
        z, x = lax.div(m, 2), lax.rem(m, 2)
        h, zl = lax.div(z, 2), lax.rem(z, 2)
        self.g, self.m, self.y, self.c, self.x, self.h, self.zl = g, m, y, c, x, h, zl
        self.home = c == h
        self.k = y * 2 + h
        self.r = c * 4 + zl * 2 + x
        self.across_x = (g, m + 1 - 2 * x)
        self.across_z = (g, m + 2 - 4 * zl)
        self.across_core = (g + 1 - 2 * c, m)
        self.partner = (y * 2 + 1 - c, ((1 - h) * 2 + zl) * 2 + x)

    def shard(self, dc=0, dz=0, dx=0):
        c = 1 - self.c if dc else self.c
        zl = 1 - self.zl if dz else self.zl
        x = 1 - self.x if dx else self.x
        return c * 4 + zl * 2 + x

    def router(self, n):
        y = 1 - self.y if n % 2 else self.y
        h = 1 - self.h if n // 2 else self.h
        return (y * 2 + self.c, (h * 2 + self.zl) * 2 + self.x), y * 2 + h

    def peer(self, step):
        m = lax.rem(self.m + step, PEERS)
        return (self.g, m), m


def rows(index, count):
    if isinstance(index, int):
        return pl.ds(index * count, count)
    return pl.ds(pl.multiple_of(index * count, count), count)


def remote(src, dst, send, recv, device):
    return pltpu.make_async_remote_copy(
        src_ref=src,
        dst_ref=dst,
        send_sem=send,
        recv_sem=recv,
        device_id=device,
        device_id_type=MESH,
    )


def greet(devices):
    barrier = pltpu.get_barrier_semaphore()
    for device in devices:
        pl.semaphore_signal(barrier, inc=1, device_id=device, device_id_type=MESH)
    pl.semaphore_wait(barrier, len(devices))


def dot(a, b):
    return jnp.dot(a, b, preferred_element_type=jnp.float32)


def dot_t(a, b):
    return lax.dot_general(a, b, (((1,), (1,)), ((), ())), preferred_element_type=jnp.float32)


def t_dot(a, b):
    return lax.dot_general(a, b, (((0,), (0,)), ((), ())), preferred_element_type=jnp.float32)


def loop(count, step, unroll=1):
    def turn(i, carry):
        for n in range(unroll):
            step(i * unroll + n)
        return carry

    if count == unroll:
        turn(0, 0)
    else:
        lax.fori_loop(0, count // unroll, turn, 0)


def mean_of(value):
    return jnp.sum(value, axis=-1, keepdims=True) * (1.0 / D)


def sum_rows(value):
    return jnp.sum(value, axis=0, keepdims=True)


def placing(target, keep_mask, capacity):
    count, groups = target.shape[0], capacity.shape[0]
    aims = [target[s] for s in range(count)]
    flags = [keep_mask[s] for s in range(count)]
    limits = [capacity[k] for k in range(groups)]
    placed = []
    for s in range(count):
        rank = jnp.int32(0)
        for before in range(s):
            rank = rank + flags[before] * (aims[before] == aims[s]).astype(jnp.int32)
        placed.append(
            [
                (
                    flags[s]
                    * (aims[s] == k).astype(jnp.int32)
                    * (rank == n).astype(jnp.int32)
                    * (rank < limits[k]).astype(jnp.int32)
                ).astype(jnp.float32)
                for k in range(groups)
                for n in range(SLOTS)
            ]
        )
    return placed


class Heads:
    def __init__(self):
        row = lax.broadcasted_iota(jnp.int32, (2 * LANES, LANES), 0)
        col = lax.broadcasted_iota(jnp.int32, (2 * LANES, LANES), 1)
        self.same = lax.rem(lax.div(row, SEQ), 2) == lax.div(col, SEQ)
        self.first = col[:LANES] < HEAD
        lane = lax.broadcasted_iota(jnp.int32, (1, LANES), 1)
        self.masks = [
            (lane < HEAD).astype(jnp.float32).astype(jnp.bfloat16),
            (lane >= HEAD).astype(jnp.float32).astype(jnp.bfloat16),
        ]

    def stack(self, pair):
        return jnp.concatenate([pair * mask for mask in self.masks], axis=0)

    def join(self, both):
        return jnp.where(self.first, both[:LANES], both[LANES:]).astype(jnp.bfloat16)

    def weigh(self, q, k):
        scores = jnp.where(self.same, dot_t(q, k) * HEAD ** (-0.5), -3.0e38)
        largest = jnp.max(scores, axis=-1, keepdims=True)
        shifted = jnp.exp(scores - largest)
        return shifted / jnp.sum(shifted, axis=-1, keepdims=True)


CHUNK = 512
CHUNKS = FF // CHUNK
PAIR = 2 * CHUNK
BASE = CHUNKS * PAIR
SPANS = ((CHUNK, CHUNK),) + tuple((i * PAIR, PAIR) for i in range(1, CHUNKS)) + (
    (BASE, D),
    (BASE + D, D),
    (BASE + 2 * D, D),
    (BASE + 3 * D, D + LANES),
    (0, CHUNK),
)
OUT_PIECE, QUERY_PIECE, KEY_PIECE, VALUE_PIECE = range(CHUNKS, CHUNKS + 4)
UP_PIECE = CHUNKS + 4
PIECES = CHUNKS + 5
Z_FIRST = ()
RING = 2
HALF = 384
SHARD_AT = 2 * LANES
STAT_F = 4 * FF + 2 * LANES
STAT_A = 8 * D + 2 * LANES
ATTENTION_AT = (BASE + D, BASE + 2 * D, BASE + 3 * D, BASE)


def forward_phase(spot, r):
    low, full = jnp.bfloat16, jnp.float32
    count = r.diag.shape[0]
    group_count = r.capacity.shape[0]
    target, keep_mask, capacity, vectors = r.target, r.keep_mask, r.capacity, r.vectors
    fa, f1, f2, xt, ot, ht, dft, qkv, g, gp = r.fa, r.f1, r.f2, r.xt, r.ot, r.ht, r.dft, r.qkv, r.g, r.gp
    n1, inv, dr, df, vt, vg, x, dy, o, h1, hb = r.n1, r.inv, r.dr, r.df, r.vt, r.vg, r.x, r.dy, r.o, r.h1, r.hb
    qb, bu, square, acc, total = r.qb, r.bu, r.square, r.acc, r.total
    swap_s, swap_r, x_s, x_r, z_s, z_r, d_s, d_r = r.swap_s, r.swap_r, r.x_s, r.x_r, r.z_s, r.z_r, r.d_s, r.d_r
    c_s, c_r, t_s, t_r, own_sem, keep_sem, load_sem = r.c_s, r.c_r, r.t_s, r.t_r, r.own_sem, r.keep_sem, r.load_sem

    def raw(block):
        return (n1, dr, h1)[block // 5].at[pl.ds(block % 5 * count, count)]

    def load_weights(block):
        src = r.wa.at[block] if block < 4 else r.wf.at[block // 4 - 1, :, pl.ds(block % 4 * D, D)]
        return pltpu.make_async_copy(src, raw(block), load_sem.at[block])

    def load_tokens(src, s):
        return pltpu.make_async_copy(
            src.at[pl.ds(s * SEQ, SEQ)], total.at[pl.ds(0, SEQ), pl.ds(s * D, D)], load_sem.at[12 + s]
        )

    for block in range(4):
        load_weights(block).start()
    for s in range(target.shape[0]):
        load_tokens(r.layer_in, s).start()
    for block in range(4, 12):
        load_weights(block).start()
    square[...] = jnp.zeros(square.shape, full)
    for row in range(12):
        square[row : row + 1, pl.ds(0, count)] = vectors[row]
    acc[pl.ds(SHARD_AT, count), pl.ds(VEC, LANES)] = square[...].T[:count].astype(low)
    placed = placing(target, keep_mask, capacity)
    r.greet()
    firsts, widths, fulls = (0, WIDE, WIDE + FF), (WIDE, FF, FF), (fa, f1, f2)
    shards = [acc.at[pl.ds(SHARD_AT, count), pl.ds(*span)] for span in zip(firsts, widths)]
    pieces = range(3)
    away = jnp.logical_not(spot.home)

    def swap(p):
        return remote(
            shards[p], fulls[p].at[rows(spot.m, count)], swap_s.at[p], swap_r.at[p], spot.partner
        )

    def keep(p):
        return pltpu.make_async_copy(shards[p], fulls[p].at[rows(spot.r, count)], own_sem.at[p])

    def hop(p, shard, send, recv, device):
        view = fulls[p].at[rows(shard, count)]
        return remote(view, view, send, recv, device)

    def over_x(p, shard):
        return hop(p, shard, x_s.at[p], x_r.at[p], spot.across_x)

    def over_z(p, shard):
        return hop(p, shard, z_s.at[p], z_r.at[p], spot.across_z)

    def diagonal(p, shard):
        return hop(p, shard, d_s.at[p], d_r.at[p], spot.across_x)

    def over_core(p, n, shard):
        return hop(p, shard, c_s.at[p, n], c_r.at[p, n], spot.across_core)

    routed = (x, dy)

    def token(a, n):
        device, k = spot.router(n)
        return remote(
            acc.at[pl.ds(a * LANES, LANES), rows(k, D)],
            routed[a].at[pl.ds(n * LANES, LANES)],
            t_s.at[a, n],
            t_r.at[a, n],
            device,
        )

    def token_keep(a):
        return pltpu.make_async_copy(
            acc.at[pl.ds(a * LANES, LANES), rows(spot.k, D)],
            routed[a].at[pl.ds(0, LANES)],
            keep_sem.at[a],
        )

    mine = spot.r
    by_x, by_z, by_both = spot.shard(dx=1), spot.shard(dz=1), spot.shard(dz=1, dx=1)

    def lead(p):
        over_x(p, mine).start()
        over_z(p, mine).start()
        over_core(p, 0, mine).start()

    def lead_home(p):
        keep(p).wait()
        lead(p)

    def lead_away(p):
        hop(p, mine, swap_s.at[p], swap_r.at[p], spot.partner).wait_recv()
        lead(p)

    def relay(p):
        over_z(p, by_z).wait_recv()
        diagonal(p, by_z).start()
        over_core(p, 2, by_z).start()
        over_x(p, by_x).wait_recv()
        over_core(p, 1, by_x).start()

    def finish(p):
        diagonal(p, by_both).wait_recv()
        over_core(p, 3, by_both).start()

    def collect_first(p):
        over_core(p, 0, spot.shard(dc=1)).wait_recv()

    def collect_rest(p):
        over_core(p, 1, spot.shard(dc=1, dx=1)).wait_recv()
        over_core(p, 2, spot.shard(dc=1, dz=1)).wait_recv()
        over_core(p, 3, spot.shard(dc=1, dz=1, dx=1)).wait_recv()

    def cast(p, block):
        load_weights(block).wait()
        at = firsts[p] + block % 4 * D
        acc[pl.ds(SHARD_AT, count), pl.ds(at, D)] = raw(block)[...].astype(low)

    for block in range(4):
        cast(0, block)

    @pl.when(away)
    def _():
        swap(0).start()

    @pl.when(spot.home)
    def _():
        keep(0).start()

    for p in (1, 2):
        for j in range(4):
            cast(p, p * 4 + j)

        @pl.when(spot.home)
        def _():
            lead_home(p - 1)
            keep(p).start()

    @pl.when(spot.home)
    def _():
        lead_home(2)

    def choose(a):
        def part(n):
            parts = [total[rows(n, 16), pl.ds(s * D, D)] for s in range(len(placed))]
            for slot in range(2 * group_count):
                value = sum(places[slot] * one for places, one in zip(placed, parts))
                at = pl.multiple_of(a * LANES + slot % 2 * SEQ + n * 16, 16)
                acc[pl.ds(at, 16), pl.ds(slot // 2 * D, D)] = value.astype(low)

        loop(SEQ // 16, part)

    for s in range(target.shape[0]):
        load_tokens(r.layer_in, s).wait()
    choose(0)
    for s in range(target.shape[0]):
        load_tokens(r.cotangent, s).start()
    token_keep(0).start()
    token(0, 1).start()

    @pl.when(away)
    def _():
        lead_away(0)
        swap(1).start()

    @pl.when(spot.home)
    def _():
        relay(0)
        finish(0)

    collect_first(0)
    token(0, 2).start()
    token(0, 3).start()
    for s in range(target.shape[0]):
        load_tokens(r.cotangent, s).wait()
    choose(1)
    square[...] = jnp.zeros(square.shape, full)
    for n, part in enumerate((vectors, r.vector_moments, r.row_moments)):
        for row in range(part.shape[0]):
            square[row : row + 1, pl.ds(0, count)] = part[row]
        r.small[n] = square[...].T[:count]

    @pl.when(away)
    def _():
        relay(0)
        finish(0)

    @pl.when(spot.home)
    def _():
        relay(1)
        finish(1)

    def turn(src, dst, i):
        block = rows(i, LANES)
        turned = src[block, :].T
        dst[rows(1 - spot.c, HALF), block] = turned[:HALF]
        dst[rows(spot.c, HALF), block] = turned[HALF:]

    token_keep(0).wait()
    token(0, 1).wait_recv()
    turn(x, xt, 0)
    turn(x, xt, 1)
    collect_rest(0)
    vt[...] = fa[:, pl.ds(VEC, LANES)].astype(full).T[:16]
    qb[:, pl.ds(0, D)] = vt[0:1]
    qb[:, pl.ds(D, D)] = jnp.zeros((1, D), full)
    qb[:, pl.ds(2 * D, D)] = vt[1:2]
    for i in range(4):
        bu[:, pl.ds(i * D, D)] = vt[8 + i : 9 + i]

    def project(first, j):
        cols = rows(j, 256)
        at = pl.ds(first, 256)
        qkv[at, cols] = (dot(x[at, :], fa[:, cols]) + qb[:, cols]).astype(low)

    heads = Heads()

    def attend(block, j):
        at = pl.ds(block * LANES, LANES)
        q = qkv[at, rows(j, LANES)]
        k = qkv[at, rows(j + 6, LANES)]
        v = qkv[at, rows(j + 12, LANES)]
        weights = heads.weigh(heads.stack(q), k).astype(low)
        o[at, rows(j, LANES)] = heads.join(dot(weights, v))

    def attend_block(block):
        def part(n):
            for j in range(3):
                attend(block, n * 3 + j)

        loop(2, part)

    loop(QKV // 256, functools.partial(project, 0), 3)

    @pl.when(spot.home)
    def _():
        relay(2)

    attend_block(0)
    attend_block(1)

    @pl.when(spot.home)
    def _():
        finish(2)

    token(0, 2).wait_recv()
    token(0, 3).wait_recv()
    loop(QKV // 256, functools.partial(project, 256), 3)

    @pl.when(away)
    def _():
        lead_away(1)
        swap(2).start()

    attend_block(2)
    attend_block(3)

    @pl.when(away)
    def _():
        relay(1)

    def attention_out(j):
        h1[:, rows(j, 256)] = dot(o[...], fa[:, pl.ds(QKV + j * 256, 256)])

    loop(D // 256, attention_out, 3)

    def first_norm(i):
        for n in range(2):
            at = pl.ds(pl.multiple_of(i * 64 + n * 32, 32), 32)
            stream = x[at, :].astype(full) + (h1[at, :] + vt[2:3])
            center = stream - mean_of(stream)
            inverse = lax.rsqrt(mean_of(center * center) + epsilon)
            normed = center * inverse
            n1[at, :] = normed
            inv[at, :] = jnp.broadcast_to(inverse, (32, LANES))
            value = normed * vt[3:4] + vt[4:5]
            h1[at, :] = value
            hb[at, :] = value.astype(low)

    loop(TOKENS // 64, first_norm)

    @pl.when(away)
    def _():
        lead_away(2)
        finish(1)

    collect_first(2)
    token_keep(1).start()
    token(1, 1).start()
    collect_first(1)
    collect_rest(1)

    def rise(j, dst):
        dr[:, pl.ds(dst * 256, 256)] = dot(hb[...], f1[:, rows(j, 256)])

    def bend(j, src):
        cols = rows(j, 256)
        for i in range(TOKENS // 32):
            at = pl.ds(i * 32, 32)
            u = dr[at, pl.ds(src * 256, 256)] + bu[:, cols]
            below = 0.5 + 0.5 * lax.erf(u * (0.5**0.5))
            slope = below + u * (jnp.exp(-0.5 * u * u) * 0.3989422804014327)
            g[at, cols] = (u * below).astype(low)
            gp[at, cols] = slope.astype(low)

    rise(0, 0)

    def up(t):
        rise(2 * t + 1, 1)
        bend(2 * t, 0)
        rise(lax.rem(2 * t + 2, FF // 256), 0)
        bend(2 * t + 1, 1)

    def up_some(first):
        loop(2, lambda t: up(t + first))

    up_some(0)

    @pl.when(away)
    def _():
        relay(2)

    token(1, 2).start()
    token(1, 3).start()
    up_some(2)

    @pl.when(away)
    def _():
        finish(2)

    up_some(4)
    for i in range(4):
        if i >= 2:
            turn(x, xt, i)
        turn(hb, ht, i)
        turn(o, ot, i)
    def down(half):
        at = rows(half, D // 2)
        dr[:, at] = dot_t(g[:, pl.ds(0, D)], f2[at, pl.ds(0, D)])

        def more(n):
            part = rows(n + 1, D)
            dr[:, at] += dot_t(g[:, part], f2[at, part])

        loop(FF // D - 1, more, 3)

    @pl.when(away)
    def _():
        collect_rest(2)

    down(spot.h)

    @pl.when(spot.home)
    def _():
        collect_rest(2)

    down(1 - spot.h)
    token_keep(1).wait()
    token(1, 1).wait_recv()
    vg[...] = jnp.zeros(vg.shape, full)

    def second_norm(i):
        sums = []
        for n in range(4):
            at = pl.ds(pl.multiple_of(i * LANES + n * 32, 32), 32)
            stream = h1[at, :] + (dr[at, :] + vt[5:6])
            center = stream - mean_of(stream)
            inverse = lax.rsqrt(mean_of(center * center) + epsilon)
            normed = center * inverse
            result = (normed * vt[6:7] + vt[7:8]).astype(low)
            upstream = dy[at, :].astype(full)
            dy[at, :] = result
            scaled = upstream * vt[6:7]
            back = inverse * (scaled - mean_of(scaled) - normed * mean_of(scaled * normed))
            dr[at, :] = back
            rounded = back.astype(low)
            df[at, :] = rounded
            sums.append((sum_rows(rounded.astype(full)), sum_rows(upstream * normed), sum_rows(upstream)))
        for row, parts in enumerate(zip(*sums)):
            vg[5 + row : 6 + row] += sum(parts)
        turn(df, dft, i)

    loop(2, second_norm)
    token(1, 2).wait_recv()
    token(1, 3).wait_recv()
    loop(2, lambda i: second_norm(i + 2))
    for a in (0, 1):
        for n in (1, 2, 3):
            token(a, n).wait_send()

    @pl.when(away)
    def _():
        for p in pieces:
            swap(p).wait_send()

    def settle():
        for p in pieces:
            over_x(p, mine).wait_send()
            over_z(p, mine).wait_send()
            diagonal(p, by_z).wait_send()
            for n, shard in enumerate((mine, by_x, by_z, by_both)):
                over_core(p, n, shard).wait_send()

    return settle


def backward_phase(spot, r, settle):
    low, full = jnp.bfloat16, jnp.float32
    count = r.diag.shape[0]
    away = jnp.logical_not(spot.home)
    columns, got_outs, got_grads, sums, by_row, by_column = r.columns, r.got_outs, r.got_grads, r.sums, r.by_row, r.by_column
    vectors_grad, rows_new, columns_new = r.vectors_grad, r.rows_new, r.columns_new
    moments_new, vectors_new, scale_new = r.moments_new, r.vectors_new, r.scale_new
    fa, f1, f2, xt, ot, ht, dft, qkv, g, gp = r.fa, r.f1, r.f2, r.xt, r.ot, r.ht, r.dft, r.qkv, r.g, r.gp
    n1, inv, dr, df, vt, vg, dbu, vt_low, square = r.n1, r.inv, r.dr, r.df, r.vt, r.vg, r.dbu, r.vt_low, r.square
    da, do, dx, du = r.x, r.dy, r.o, r.hb
    acc, other, stage_f, stage_v, total = r.acc, r.other, r.stage_f, r.stage_v, r.total
    diag, from_x, from_z, swapped = r.diag, r.from_x, r.from_z, r.swapped
    stf, sta, srf, sra, small, small_new, spread_row = r.stf, r.sta, r.srf, r.sra, r.small, r.small_new, r.square.at[pl.ds(0, count)]
    out_sem, core_s, core_r, x_s, x_r, z_s, z_r = r.out_sem, r.core_s, r.core_r, r.bx_s, r.bx_r, r.bz_s, r.bz_r
    d_s, d_r, swap_s, swap_r, st_s, st_r, st_keep = r.bd_s, r.bd_r, r.bswap_s, r.bswap_r, r.st_s, r.st_r, r.st_keep
    t_s, t_r, keep_sem = r.bt_s, r.bt_r, r.bkeep_sem
    routed = ((do, got_outs), (dx, got_grads))

    def token(a, n):
        device, k = spot.router(n)
        src, dst = routed[a]
        return remote(
            src.at[pl.ds(n * LANES, LANES)],
            dst.at[rows(spot.k, LANES)],
            t_s.at[a, n],
            t_r.at[a, n],
            device,
        )

    def token_from(a, n):
        device, k = spot.router(n)
        src, dst = routed[a]
        return remote(
            src.at[pl.ds(n * LANES, LANES)],
            dst.at[rows(k, LANES)],
            t_s.at[a, n],
            t_r.at[a, n],
            device,
        )

    def token_keep(a):
        src, dst = routed[a]
        return pltpu.make_async_copy(
            src.at[pl.ds(0, LANES)], dst.at[rows(spot.k, LANES)], keep_sem.at[a]
        )

    def send_tokens(a, which=(1, 2, 3)):
        for n in which:
            token(a, n).start()

    here = spot.zl * 2 + spot.x
    at_x = spot.zl * 2 + 1 - spot.x
    at_z = (1 - spot.zl) * 2 + spot.x
    at_both = (1 - spot.zl) * 2 + 1 - spot.x

    def cols(p):
        if isinstance(p, int):
            return pl.ds(*SPANS[p])
        return rows(p, PAIR)

    def trade(p):
        if isinstance(p, int) and p in (0, UP_PIECE):
            src, dst = stage_f.at[0, :, pl.ds(*SPANS[p])], other.at[:, cols(p)]
        elif isinstance(p, int) and p >= CHUNKS:
            first, width = SPANS[p][0], D
            src = f1.at[pl.ds(0, HALF), pl.ds(first - BASE, width)]
            dst = other.at[:, pl.ds(first, width)]
        else:
            src, dst = stage_f.at[lax.rem(p, RING)], other.at[:, cols(p)]
        return remote(src, dst, core_s.at[p], core_r.at[p], spot.across_core)

    def trade_vectors():
        return remote(
            stage_v,
            other.at[:, pl.ds(BASE + VEC, LANES)],
            core_s.at[PIECES],
            core_r.at[PIECES],
            spot.across_core,
        )

    def over_x(p):
        return remote(
            acc.at[rows(at_x, count), cols(p)],
            from_x.at[:, cols(p)],
            x_s.at[p],
            x_r.at[p],
            spot.across_x,
        )

    def over_z(p):
        return remote(
            acc.at[rows(at_z, count), cols(p)],
            from_z.at[:, cols(p)],
            z_s.at[p],
            z_r.at[p],
            spot.across_z,
        )

    def diagonal(p, z_first):
        return remote(
            acc.at[rows(at_both, count), cols(p)],
            diag.at[:, cols(p)],
            d_s.at[p],
            d_r.at[p],
            spot.across_z if z_first else spot.across_x,
        )

    def swap(p):
        return remote(
            acc.at[rows(here, count), cols(p)],
            swapped.at[:, cols(p)],
            swap_s.at[p],
            swap_r.at[p],
            spot.partner,
        )

    stats, gathered = (stf, sta), (srf, sra)

    def share(n, step):
        device, _ = spot.peer(step)
        return remote(stats[n], gathered[n].at[spot.m], st_s.at[n, step], st_r.at[n, step], device)

    def share_from(n, step):
        device, m = spot.peer((PEERS - step) % PEERS)
        return remote(stats[n], gathered[n].at[m], st_s.at[n, step], st_r.at[n, step], device)

    def share_keep(n):
        return pltpu.make_async_copy(stats[n], gathered[n].at[spot.m], st_keep.at[n])

    def meet(p):
        trade(p).wait_recv()
        if isinstance(p, int) and p == VALUE_PIECE:
            trade_vectors().wait_recv()

        def add(i):
            view = (rows(i, 32), cols(p))
            acc[view] = acc[view] + other[view]

        loop(HALF // 32, add, 3)

        def forward(z_first):
            diagonal(p, z_first).start()
            if z_first:
                over_z(p).start()
            else:
                over_x(p).start()

        forward(isinstance(p, int) and p in Z_FIRST)

    def relay(p):
        z_first = p in Z_FIRST
        diagonal(p, z_first).wait_recv()
        base = at_x if z_first else at_z

        def add(i):
            view = (pl.ds(pl.multiple_of(base * count + i * 32, 32), 32), cols(p))
            acc[view] = acc[view] + diag[rows(i, 32), cols(p)]

        loop(count // 32, add, 3)
        if z_first:
            over_x(p).start()
        else:
            over_z(p).start()

    def close(p):
        over_x(p).wait_recv()
        over_z(p).wait_recv()

        def add(i):
            view = (pl.ds(pl.multiple_of(here * count + i * 16, 16), 16), cols(p))
            part = (rows(i, 16), cols(p))
            done = acc[view].astype(full) + from_x[part].astype(full) + from_z[part].astype(full)
            total[part] = done
            acc[view] = done.astype(low)

        loop(count // 16, add, 3)

        @pl.when(away)
        def _():
            swap(p).start()

    token_keep(0).start()
    send_tokens(0)

    def chunk(c):
        third = lax.rem(c, RING)
        mine = rows(c, CHUNK)

        @pl.when(c == RING)
        def _():
            trade(0).wait_send()
            trade(UP_PIECE).wait_send()

        @pl.when(c > RING)
        def _():
            trade(c - RING).wait_send()

        first = pl.multiple_of(c * PAIR, PAIR)

        def give(left, right, shift, at):
            def part(n):
                n = n * 256
                whole = dot(left[...], right[:, pl.ds(pl.multiple_of(shift + n, 256), 256)]).astype(low)
                stage_f[third, :, pl.ds(pl.multiple_of(at + n, 256), 256)] = whole[:HALF]
                acc[:, pl.ds(pl.multiple_of(first + at + n, 256), 256)] = whole[HALF:]

            loop(CHUNK // 256, part, 2)

        def bend_back(i):
            at, here_c = rows(i, 256), rows(c * 2 + i, 256)
            value = dot(df[...], f2[:, here_c]) * gp[:, here_c].astype(full)
            rounded = value.astype(low)
            du[:, at] = rounded
            dbu[:, here_c] = sum_rows(rounded.astype(full))

        give(dft, g, c * CHUNK, CHUNK)

        @pl.when(c == 0)
        def _():
            trade(0).start()

        loop(CHUNK // 256, bend_back, 2)

        @pl.when(c == 0)
        def _():
            meet(0)

        @pl.when(c >= 2)
        def _():
            meet(c - 1)

        give(ht, du, 0, 0)

        @pl.when(c == 0)
        def _():
            trade(UP_PIECE).start()

        @pl.when(c > 0)
        def _():
            trade(c).start()
        def lift(i):
            at = rows(i, 256)
            dr[:, at] += dot_t(du[:, pl.ds(0, CHUNK)], f1[at, mine])

        loop(D // 256, lift, 3)

        @pl.when(c == 0)
        def _():
            meet(UP_PIECE)

        @pl.when(c == 2)
        def _():
            relay(0)

        @pl.when(c == 3)
        def _():
            relay(UP_PIECE)

        @pl.when(c == 5)
        def _():
            relay(1)
            close(0)
            close(UP_PIECE)

    loop(CHUNKS, chunk)
    meet(CHUNKS - 1)
    for row in range(4):
        vg[8 + row : 9 + row] = dbu[:, pl.ds(row * D, D)]
    settle()

    def first_norm_back(i):
        sums = []
        for n in range(2):
            at = pl.ds(pl.multiple_of(i * 64 + n * 32, 32), 32)
            normed = n1[at, :]
            upstream = dr[at, :]
            scaled = upstream * vt[3:4]
            back = inv[at, :1] * (scaled - mean_of(scaled) - normed * mean_of(scaled * normed))
            dr[at, :] = back
            rounded = back.astype(low)
            da[at, :] = rounded
            sums.append((sum_rows(rounded.astype(full)), sum_rows(upstream * normed), sum_rows(upstream)))
        for row, (one, two) in enumerate(zip(*sums)):
            vg[2 + row : 3 + row] += one + two

    loop(TOKENS // 64, first_norm_back)
    def outer(src, right, first, j):
        def part(n):
            at = n * 256
            whole = dot(src[...], right[:, pl.ds(j * D + at, 256)]).astype(low)
            f1[pl.ds(0, HALF), pl.ds(first - BASE + at, 256)] = whole[:HALF]
            acc[:, pl.ds(first + at, 256)] = whole[HALF:]

        loop(D // 256, part, 3)

    outer(ot, da, BASE, 0)
    trade(OUT_PIECE).start()

    token_keep(0).wait()
    for n in (1, 2, 3):
        token(0, n).wait_send()

    def out_back(j):
        do[:, rows(j, 256)] = dot_t(da[...], fa[rows(j, 256), pl.ds(QKV, D)]).astype(low)

    loop(D // 256, out_back, 3)
    relay(2)
    close(1)
    heads = Heads()

    def attend_back(block, j):
        at = rows(block, LANES)
        q_cols, k_cols, v_cols = rows(j, LANES), rows(j + 6, LANES), rows(j + 12, LANES)
        q, k, v = heads.stack(qkv[at, q_cols]), qkv[at, k_cols], qkv[at, v_cols]
        upstream = heads.stack(do[at, q_cols])
        weights = heads.weigh(q, k)
        grad_w = dot_t(upstream, v)
        centered = grad_w - jnp.sum(grad_w * weights, axis=-1, keepdims=True)
        grad_s = (weights * centered).astype(low)
        qkv[at, q_cols] = heads.join(dot(grad_s, k) * HEAD ** (-0.5))
        qkv[at, k_cols] = (t_dot(grad_s, q) * HEAD ** (-0.5)).astype(low)
        qkv[at, v_cols] = t_dot(weights.astype(low), upstream).astype(low)

    def attend_back_block(block):
        def part(n):
            for j in range(3):
                attend_back(block, n * 3 + j)

        loop(2, part)

    attend_back_block(0)
    meet(OUT_PIECE)
    relay(3)
    attend_back_block(1)
    close(2)
    attend_back_block(2)
    relay(4)
    close(3)
    attend_back_block(3)
    outer(xt, qkv, BASE + D, 0)
    trade(QUERY_PIECE).start()
    outer(xt, qkv, BASE + 2 * D, 1)
    trade(KEY_PIECE).start()

    def bias_sums(i):
        at = rows(i, LANES)
        vg[0:1] += sum_rows(qkv[at, pl.ds(0, D)].astype(full))
        vg[1:2] += sum_rows(qkv[at, pl.ds(2 * D, D)].astype(full))

    loop(4, bias_sums)
    vt_low[...] = vg[...].T.astype(low)
    stage_v[...] = vt_low[rows(1 - spot.c, HALF), :]
    trade_vectors().start()
    acc[:, pl.ds(BASE + VEC, LANES)] = vt_low[rows(spot.c, HALF), :]
    outer(xt, qkv, BASE + 3 * D, 2)
    trade(VALUE_PIECE).start()
    meet(QUERY_PIECE)
    relay(5)
    close(4)
    meet(KEY_PIECE)

    def input_back(j):
        at = rows(j, 256)

        value = dr[:, at]
        for n in range(3):
            value = value + dot_t(qkv[:, rows(n, D)], fa[at, rows(n, D)])
        dx[:, at] = value.astype(low)

    loop(D // 256, input_back)
    token_keep(1).start()
    send_tokens(1)
    meet(VALUE_PIECE)
    lane = lax.broadcasted_iota(jnp.int32, (1, LANES), 1)
    row_new = {}

    def arrive(p):
        @pl.when(away)
        def _():
            swap(p).wait_recv()
            total[:, cols(p)] = swapped[:, cols(p)].astype(full)

        put(p).start()

    def put(p):
        return pltpu.make_async_copy(total.at[:, cols(p)], sums.at[:, cols(p)], out_sem.at[p])

    def tally_feedforward():
        arrive(UP_PIECE)
        for c in range(CHUNKS):
            arrive(c)
        for w in range(2):
            spread_row[...] = jnp.zeros(spread_row.shape, full)

            def add_squares(c):
                at = pl.ds(pl.multiple_of(c * PAIR + w * CHUNK, CHUNK), CHUNK)
                m = total[:, at]
                held = m * m + tiny_square
                spread_row[:, :1] += jnp.sum(held, axis=1, keepdims=True)
                stf[:, at] = sum_rows(held)

            loop(CHUNKS, add_squares)
            r = DECAY * small[2, :, 4 + w : 5 + w] + KEEP * (spread_row[:, :1] / FF)
            row_new[4 + w] = r
            inverse = 1.0 / r

            def weigh_squares(c):
                first = pl.multiple_of(c * PAIR + w * CHUNK, CHUNK)
                m = total[:, pl.ds(first, CHUNK)]
                stf[:, pl.ds(pl.multiple_of(2 * FF + first, CHUNK), CHUNK)] = sum_rows(m * m * inverse)

            loop(CHUNKS, weigh_squares)
            stf[:, pl.ds(4 * FF + w * LANES, LANES)] = jnp.broadcast_to(sum_rows(r), (1, LANES))
        spread(0)

    def spread(n):
        share_keep(n).start()
        for step in range(1, PEERS):
            share(n, step).start()

    row_sums = [jnp.zeros((1, LANES), full)]

    def tally_matrix(j):
        m = total[:, pl.ds(ATTENTION_AT[j], D)]
        squared = m * m
        held = squared + tiny_square
        mean = jnp.sum(held, axis=1, keepdims=True) / D
        r = DECAY * small[2, :, j : j + 1] + KEEP * mean
        row_new[j] = r
        sta[:, pl.ds(j * D, D)] = sum_rows(held)
        sta[:, pl.ds((4 + j) * D, D)] = sum_rows(squared * (1.0 / r))
        row_sums[0] = jnp.where(lane == j, sum_rows(r), row_sums[0])

    def tally_vectors():
        sta[:, pl.ds(8 * D, LANES)] = row_sums[0]
        m = total[:, pl.ds(BASE + VEC, LANES)]
        renewed = DECAY * small[1] + KEEP * (m * m + tiny_square)
        move = m * lax.rsqrt(renewed)
        small_new[0] = m
        small_new[1] = renewed
        small_new[2] = move
        sta[:, pl.ds(8 * D + LANES, LANES)] = sum_rows(move * move)
        spread(1)

    scale = [jnp.zeros((1, LANES), full)]

    def gathered_sum(n, first, width):
        value = gathered[n][0, :, pl.ds(first, width)]
        for peer in range(1, PEERS):
            value = value + gathered[n][peer, :, pl.ds(first, width)]
        return value

    def take(n):
        share_keep(n).wait()
        for step in range(1, PEERS):
            share_from(n, step).wait_recv()

    def renew(n, index, mean, tiles, column_at, entries):
        weighted = jnp.zeros((1, 1), full)
        for at_stat, at_column, width in tiles:
            here_c = (slice(None), pl.ds(at_column, width))
            c = DECAY * columns[here_c] + KEEP * (gathered_sum(n, at_stat, width) / D)
            columns_new[here_c] = c
            sums = gathered_sum(n, column_at + at_stat, width)
            weighted = weighted + jnp.sum(sums * mean / c, axis=1, keepdims=True)
        size = jnp.sqrt(weighted / entries)
        scale[0] = jnp.where(lane == index, size, scale[0])
        factor = jnp.sqrt(mean) * (matrix_rate / jnp.maximum(1.0, size / clip_level))
        for _, at_column, width in tiles:
            here_c = (slice(None), pl.ds(at_column, width))
            by_column[here_c] = lax.rsqrt(columns_new[here_c]) * factor

    close(5)
    relay(OUT_PIECE)
    relay(QUERY_PIECE)
    close(OUT_PIECE)
    relay(KEY_PIECE)
    tally_feedforward()
    close(QUERY_PIECE)
    relay(VALUE_PIECE)
    arrive(OUT_PIECE)
    tally_matrix(3)
    close(KEY_PIECE)
    arrive(QUERY_PIECE)
    tally_matrix(0)
    close(VALUE_PIECE)
    arrive(KEY_PIECE)
    tally_matrix(1)
    take(0)
    for w in range(2):
        mean = gathered_sum(0, 4 * FF + w * LANES, LANES)[:, :1] / D
        tiles = [
            (c * PAIR + w * CHUNK, 4 * D + w * FF + c * CHUNK, CHUNK) for c in range(CHUNKS)
        ]
        renew(0, 4 + w, mean, tiles, 2 * FF, D * FF)
    arrive(VALUE_PIECE)
    tally_matrix(2)
    tally_vectors()
    take(1)
    extra = gathered_sum(1, 8 * D, LANES)
    for j in range(4):
        renew(1, j, extra[:, j : j + 1] / D, [(j * D, j * D, D)], 4 * D, D * D)
    size = jnp.sqrt(gathered_sum(1, 8 * D + LANES, LANES) / D)
    small_new[3] = small[0] - small_new[2] * (vector_rate / jnp.maximum(1.0, size / clip_level))
    scale_new[...] = jnp.where(lane < 6, scale[0], pltpu.roll(size, 6, 1))[:, : scale_new.shape[1]]
    row_all = jnp.zeros((count, LANES), full)
    lanes = lax.broadcasted_iota(jnp.int32, (count, LANES), 1)
    for j in range(6):
        row_all = jnp.where(lanes == j, row_new[j], row_all)
    small_new[2] = row_all
    by_row[...] = lax.rsqrt(jnp.where(lanes < 6, row_all, 1.0))
    for n, dst in enumerate((vectors_grad, moments_new, rows_new, vectors_new)):
        square[pl.ds(0, count), :] = small_new[n]
        turned = square[...].T
        for row in range(dst.shape[0]):
            dst[row] = turned[row : row + 1, :count]

    for p in range(PIECES):
        if CHUNKS - RING <= p < UP_PIECE:
            trade(p).wait_send()
        diagonal(p, p in Z_FIRST).wait_send()
        over_x(p).wait_send()
        over_z(p).wait_send()
    for n in range(2):
        for step in range(1, PEERS):
            share(n, step).wait_send()

    @pl.when(away)
    def _():
        for p in range(PIECES):
            swap(p).wait_send()

    trade_vectors().wait_send()
    token_keep(1).wait()
    for n in (1, 2, 3):
        token_from(0, n).wait_recv()
        token_from(1, n).wait_recv()
        token(1, n).wait_send()
    for p in range(PIECES):
        put(p).wait()


LAYER_IN = (
    "wa", "wf", "layer_in", "cotangent", "vectors", "row_moments", "vector_moments", "columns", "target", "keep_mask",
    "capacity",
)
LAYER_OUT = (
    "got_outs", "got_grads", "sums", "by_row", "by_column", "vectors_grad", "rows_new", "columns_new", "moments_new",
    "vectors_new", "scale_new",
)


def layer_scratch(count):
    low, full = jnp.bfloat16, jnp.float32
    wide = BASE + WIDE
    dma = pltpu.SemaphoreType.DMA
    buffers = dict(
        fa=((D, WIDE), low),
        f1=((D, FF), low),
        f2=((D, FF), low),
        xt=((D, TOKENS), low),
        ot=((D, TOKENS), low),
        ht=((D, TOKENS), low),
        dft=((D, TOKENS), low),
        qkv=((TOKENS, QKV), low),
        g=((TOKENS, FF), low),
        gp=((TOKENS, FF), low),
        n1=((TOKENS, D), full),
        inv=((TOKENS, LANES), full),
        dr=((TOKENS, D), full),
        df=((TOKENS, D), low),
        vt=((16, D), full),
        vg=((LANES, D), full),
        x=((TOKENS, D), low),
        dy=((TOKENS, D), low),
        o=((TOKENS, D), low),
        h1=((TOKENS, D), full),
        hb=((TOKENS, D), low),
        qb=((1, QKV), full),
        bu=((1, FF), full),
        square=((LANES, LANES), full),
        dbu=((1, FF), full),
        vt_low=((D, LANES), low),
        acc=((HALF, wide), low),
        other=((HALF, wide), low),
        stage_f=((RING, HALF, PAIR), low),
        stage_v=((HALF, LANES), low),
        diag=((count, wide), low),
        from_x=((count, wide), low),
        from_z=((count, wide), low),
        swapped=((count, wide), low),
        total=((count, wide), full),
        stf=((1, STAT_F), full),
        sta=((1, STAT_A), full),
        srf=((PEERS, 1, STAT_F), full),
        sra=((PEERS, 1, STAT_A), full),
        small=((3, count, LANES), full),
        small_new=((4, count, LANES), full),
    )
    scratch = {name: pltpu.VMEM(*one) for name, one in buffers.items()}
    for name in ("swap", "x", "z", "d"):
        for end in ("s", "r"):
            scratch[f"{name}_{end}"] = dma((3,))
            scratch[f"b{name}_{end}"] = dma((PIECES,))
    for end in ("s", "r"):
        scratch[f"c_{end}"] = dma((3, 4))
        scratch[f"t_{end}"] = dma((2, 4))
        scratch[f"bt_{end}"] = dma((2, 4))
        scratch[f"core_{end}"] = dma((PIECES + 1,))
        scratch[f"st_{end}"] = dma((2, PEERS))
    scratch.update(
        own_sem=dma((3,)), keep_sem=dma((2,)), bkeep_sem=dma((2,)), load_sem=dma((20,)),
        out_sem=dma((PIECES,)), st_keep=dma((2,)),
    )
    return scratch


def layer_kernel(names, *refs):
    r = types.SimpleNamespace(**dict(zip(names, refs)))
    spot = Spot()
    r.greet = lambda: greet(
        [spot.across_core, spot.partner]
        + [spot.router(n)[0] for n in (1, 2, 3)]
        + [spot.peer(step)[0] for step in range(1, PEERS)]
    )
    settle = forward_phase(spot, r)
    backward_phase(spot, r, settle)


def layer(wa, wf, layer_in, cotangent, vectors, row_moments, vector_moments, columns, *routing):
    low, full = jnp.bfloat16, jnp.float32
    count = wa.shape[1]
    sds = jax.ShapeDtypeStruct
    scratch = layer_scratch(count)
    return pl.pallas_call(
        functools.partial(layer_kernel, LAYER_IN + LAYER_OUT + tuple(scratch)),
        out_shape=(
            sds((TOKENS, D), low),
            sds((TOKENS, D), low),
            sds((count, BASE + WIDE), full),
            sds((count, LANES), full),
            sds(columns.shape, full),
            sds(vectors.shape, full),
            sds(row_moments.shape, full),
            sds(columns.shape, full),
            sds(vectors.shape, full),
            sds(vectors.shape, full),
            sds((1, 18), full),
        ),
        in_specs=[ANY] * 4 + [VMEM] * 4 + [SMEM] * 3,
        out_specs=(ANY,) * 3 + (VMEM,) * 8,
        scratch_shapes=list(scratch.values()),
        compiler_params=pltpu.CompilerParams(
            collective_id=0, has_side_effects=True, vmem_limit_bytes=LIMIT
        ),
        name="layer",
    )(wa, wf, layer_in, cotangent, vectors, row_moments, vector_moments, columns, *routing)


WIDTH = 1024


def finish_kernel(
    target, keep_mask, capacity, outs, grads, layer_in, cotangent, sums_f, sums_a, wa, wf, by_row, by_f1, by_f2, by_a,
    vectors_grad_i, rows_i, columns_i, moments_i, vectors_i, scale_i,
    layer_out, input_grad, ga, gf, ua, uf, vectors_grad, rows_new, columns_new, moments_new, vectors_new, scale,
):
    step = pl.program_id(0)
    for n in range(2):
        at = step * 2 + n
        aim = target[at]
        rank = jnp.int32(0)
        for s in range(target.shape[0]):
            same = (target[s] == aim) & (keep_mask[s] == 1) & (s < at)
            rank = rank + same.astype(jnp.int32)
        taken = (keep_mask[at] == 1) & (rank < capacity[aim])
        slot = jnp.where(taken, aim * SLOTS + rank, 0)
        here = pl.ds(n * SEQ, SEQ)
        for src, own, dst in ((outs, layer_in, layer_out), (grads, cotangent, input_grad)):
            back = src[rows(slot, SEQ), :].astype(jnp.float32)
            dst[here, :] = jnp.where(taken, back, own[here, :])

    @pl.when(step < FF // WIDTH)
    def _():
        for w, by_column in enumerate((by_f1, by_f2)):
            for n in range(WIDTH // CHUNK):
                at = pl.ds(n * CHUNK, CHUNK)
                m = sums_f[:, pl.ds((2 * n + w) * CHUNK, CHUNK)]
                gf[w, :, at] = m
                uf[w, :, at] = wf[w, :, at] - m * by_row[:, 4 + w : 5 + w] * by_column[:, at]

    for j in range(4):

        @pl.when(step == j)
        def _():
            m = sums_a[...]
            ga[0] = m
            ua[0] = wa[0] - m * by_row[:, j : j + 1] * by_a[...]

    @pl.when(step == 0)
    def _():
        for src, dst in (
            (vectors_grad_i, vectors_grad),
            (rows_i, rows_new),
            (columns_i, columns_new),
            (moments_i, moments_new),
            (vectors_i, vectors_new),
            (scale_i, scale),
        ):
            dst[...] = src[...]


def finish(routing, layer_in, cotangent, wa, wf, results):
    got_outs, got_grads, sums, by_row, by_column, *small = results
    count = wa.shape[1]
    full = jnp.float32

    def whole(value):
        return pl.BlockSpec(value.shape, lambda i: (0,) * len(value.shape))

    def tokens():
        return pl.BlockSpec((2 * SEQ, D), lambda i: (i, 0))

    def matrix():
        return pl.BlockSpec((1, count, D), lambda i: (jnp.minimum(i, 3), 0, 0))

    def chunk():
        return pl.BlockSpec((2, count, WIDTH), lambda i: (0, 0, third(i)))

    def third(i):
        return jnp.minimum(i, FF // WIDTH - 1)

    def column_block(shape, first):
        return pl.BlockSpec(shape, lambda i: (0, first // WIDTH + third(i)))

    return pl.pallas_call(
        finish_kernel,
        grid=(TOKENS // SEQ // 2,),
        out_shape=(
            jax.ShapeDtypeStruct((TOKENS, D), full),
            jax.ShapeDtypeStruct((TOKENS, D), full),
            jax.ShapeDtypeStruct(wa.shape, full),
            jax.ShapeDtypeStruct(wf.shape, full),
            jax.ShapeDtypeStruct(wa.shape, full),
            jax.ShapeDtypeStruct(wf.shape, full),
        )
        + tuple(jax.ShapeDtypeStruct(one.shape, full) for one in small),
        in_specs=[SMEM] * 3
        + [
            whole(got_outs),
            whole(got_grads),
            tokens(),
            tokens(),
            pl.BlockSpec((count, 2 * WIDTH), lambda i: (0, third(i))),
            pl.BlockSpec((count, D), lambda i: (0, BASE // D + lax.rem(jnp.minimum(i, 3) + 1, 4))),
            matrix(),
            chunk(),
            whole(by_row),
            column_block((1, WIDTH), 4 * D),
            column_block((1, WIDTH), 4 * D + FF),
            pl.BlockSpec((1, D), lambda i: (0, jnp.minimum(i, 3))),
        ]
        + [whole(one) for one in small],
        out_specs=(tokens(), tokens(), matrix(), chunk(), matrix(), chunk())
        + tuple(whole(one) for one in small),
        compiler_params=pltpu.CompilerParams(vmem_limit_bytes=LIMIT),
        name="finish",
    )(
        *routing, got_outs, got_grads, layer_in, cotangent, sums, sums, wa, wf, by_row, by_column,
        by_column, by_column, *small,
    )

def fast_body(
    layer_in,
    cotangent,
    target,
    keep_mask,
    capacity,
    attention_weights,
    feedforward_weights,
    vectors,
    row_moments,
    column_moments,
    vector_moments,
):
    inputs, upstream = layer_in.reshape(TOKENS, D), cotangent.reshape(TOKENS, D)
    routing = (target, keep_mask, capacity)
    vectors, row_moments, vector_moments = (
        value.transpose(1, 0, 2) for value in (vectors, row_moments, vector_moments)
    )
    results = layer(
        attention_weights[0],
        feedforward_weights[0],
        inputs,
        upstream,
        vectors,
        row_moments,
        vector_moments,
        column_moments,
        *routing,
    )
    layer_out, input_grad, ga, gf, ua, uf, vectors_grad, rows_new, columns_new, moments_new, vectors_new, scale = finish(
        routing, inputs, upstream, attention_weights[0], feedforward_weights[0], results
    )
    layer_out, input_grad = (value.reshape(layer_in.shape) for value in (layer_out, input_grad))
    return (
        layer_out,
        input_grad,
        ga[None],
        gf[None],
        vectors_grad.transpose(1, 0, 2),
        rows_new.transpose(1, 0, 2),
        columns_new,
        moments_new.transpose(1, 0, 2),
        ua[None],
        uf[None],
        vectors_new.transpose(1, 0, 2),
        scale,
    )


def solution(mesh):
    in_specs = (
        P(("group", "mp"), None, None),
        P(("group", "mp"), None, None),
        P(("group", "mp")),
        P(("group", "mp")),
        P(),
        P("group", None, "mp", None),
        P("group", None, "mp", None),
        P("group", None, "mp"),
        P("group", None, "mp"),
        P("group", None),
        P("group", None, "mp"),
    )
    out_specs = (
        P(("group", "mp"), None, None),
        P(("group", "mp"), None, None),
        P("group", None, "mp", None),
        P("group", None, "mp", None),
        P("group", None, "mp"),
        P("group", None, "mp"),
        P("group", None),
        P("group", None, "mp"),
        P("group", None, "mp", None),
        P("group", None, "mp", None),
        P("group", None, "mp"),
        P("group", None),
    )
    suited = mesh.shape["group"] == 4 and mesh.shape["mp"] == PEERS
    body = fast_body if suited else generic_body
    return jax.shard_map(body, mesh=mesh, in_specs=in_specs, out_specs=out_specs, check_vma=False)
```
